128 devices in a mesh: depth: 8 (over y, core), image: 16 (over z, x).
Axes of the slice: x: 4, y: 4, z: 4, core: 2. Of those that a mesh axis runs over, the one named last changes fastest.
Arguments:
- populations: float32 [19, 256, 256, 128], P(None, 'depth', 'image'), may hold values from 0 to 0.4, as said below
- transfer: float32 [16, 5, 8], P('image'), may hold values from 0.1 to 1
- direction: int32 [16], P('image'), may hold values from 0 to 1
Outputs:
- final_populations: float32 [19, 256, 256, 128], P(None, 'depth', 'image')
- vorticity: bfloat16 [256, 256, 128], P('depth', 'image')
- images: float32 [16, 4, 256, 128], P('image', None, 'depth')
The draws below stay inside these ranges and needn't reach their ends.
Inputs may be any that keep to these rules, and one draw needn't show every extreme that they name: `populations`: each population is positive, its lattice weight times a density near one with a perturbation by a rough flow of small speed. `direction`: 0 views from the side of small x, 1 from the side of large x.
All inputs are finite; a program needn't handle non-finite values.
Results may differ from the reference program's by a relative error of at most 0.001.
Values may be sent and summed in bfloat16 or wider, within the bound.
No kernel may reach another device: no remote copies, remote signals or barrier semaphores. Data moves between devices by JAX's collectives and lax.ppermute only.
A program may use at most 128 MiB of HBM per device.

```python
import jax
import jax.numpy as jnp
from jax import lax

NZ = 128
STEPS = 4
TF_BUMPS = 8
NX = 256
NY = 256
TFS = 16


lattice_velocities = ((0, 0, 0), (1, 0, 0), (-1, 0, 0), (0, 1, 0), (0, -1, 0), (0, 0, 1), (0, 0, -1), (1, 1, 0), (-1, -1, 0), (1, -1, 0), (-1, 1, 0), (1, 0, 1), (-1, 0, -1), (1, 0, -1), (-1, 0, 1), (0, 1, 1), (0, -1, -1), (0, 1, -1), (0, -1, 1))


lattice_weights = (1.0 / 3.0,) + (1.0 / 18.0,) * 6 + (1.0 / 36.0,) * 12


def draw_populations(key, part):
    flow_key = jax.random.fold_in(key, 11)
    noise_key = jax.random.fold_in(key, 23)
    flow = jnp.clip(0.05 * jax.random.normal(flow_key, (3, NX, NY, NZ), jnp.float32), -0.12, 0.12)
    noise = jax.random.uniform(noise_key, (19, NX, NY, NZ), jnp.float32, -0.1, 0.1)
    pieces = []
    for number in range(19):
        project = jnp.zeros((NX, NY, NZ), jnp.float32)
        for axis_index in range(3):
            factor = lattice_velocities[number][axis_index]
            if factor != 0:
                project = project + factor * flow[axis_index]
        pieces.append(lattice_weights[number] * (1.0 + 3.0 * project + noise[number]))
    return jnp.stack(pieces).astype(jnp.float32)


def place_ends(drawn, rng, least, top_value):
    longest = drawn.shape.index(max(drawn.shape))
    spots = []
    for shift in (0, 1):
        where = [jax.random.randint(jax.random.fold_in(rng, axis), (), 0, length) for axis, length in enumerate(drawn.shape)]
        where[longest] = (where[longest] + shift) % drawn.shape[longest]
        spots.append(tuple(where))
    return drawn.at[spots[0]].set(least).at[spots[1]].set(top_value)


def level_of(rng, shape, split, least, top_value):
    loudness, own = 1.0, jax.random.fold_in(rng, 6)
    for dim, parts in split:
        heights = jnp.exp(jax.random.uniform(jax.random.fold_in(own, dim), (parts,), jnp.float32, least / len(split), top_value / len(split)))
        loudness = loudness * jnp.repeat(heights, shape[dim] // parts).reshape([-1 if axis == dim else 1 for axis in range(len(shape))])
    return loudness


def setup_inputs(seed: int = 0) -> dict:
    splits = jax.random.split(jax.random.key(seed), 4)
    return {
        "populations": draw_populations(jax.random.fold_in(splits[3], 71), 0),
        "transfer": jnp.clip(0.1 + 0.9 * jax.random.uniform(splits[1], (TFS, 5, TF_BUMPS), jnp.float32) ** level_of(splits[1], (TFS, 5, TF_BUMPS), ((0, 16),), -0.2, 0.2), 0.1, 1.0),
        "direction": place_ends(jax.random.randint(splits[2], (TFS,), 0, 2), jax.random.fold_in(splits[2], 1), 0, 1).astype(jnp.int32),
    }


lattice_velocities = ((0, 0, 0), (1, 0, 0), (-1, 0, 0), (0, 1, 0), (0, -1, 0), (0, 0, 1), (0, 0, -1), (1, 1, 0), (-1, -1, 0), (1, -1, 0), (-1, 1, 0), (1, 0, 1), (-1, 0, -1), (1, 0, -1), (-1, 0, 1), (0, 1, 1), (0, -1, -1), (0, 1, -1), (0, -1, 1))
lattice_weights = (1.0 / 3.0,) + (1.0 / 18.0,) * 6 + (1.0 / 36.0,) * 12
relaxation = 1.25
bump_width = 0.15
level_offset = 0.05

def moments(field):
    density = field[0]
    for number in range(1, 19):
        density = density + field[number]
    components = []
    for axis_index in range(3):
        total = jnp.zeros_like(density)
        for number in range(19):
            factor = lattice_velocities[number][axis_index]
            if factor != 0:
                total = total + factor * field[number]
        components.append(total / density)
    return (density, components)

def collide(field):
    density, flow = moments(field)
    squared = flow[0] * flow[0] + flow[1] * flow[1] + flow[2] * flow[2]
    result = []
    for number in range(19):
        project = jnp.zeros_like(density)
        for axis_index in range(3):
            factor = lattice_velocities[number][axis_index]
            if factor != 0:
                project = project + factor * flow[axis_index]
        equilibrium = lattice_weights[number] * density * (1.0 + 3.0 * project + 4.5 * project * project - 1.5 * squared)
        result.append(field[number] - relaxation * (field[number] - equilibrium))
    return result

def slope(values, axis_index):
    return (jnp.roll(values, -1, axis_index) - jnp.roll(values, 1, axis_index)) * 0.5

def reference(populations, transfer, direction):
    field = populations
    for turn_index in range(STEPS):
        collided = collide(field)
        field = jnp.stack([jnp.roll(collided[number], lattice_velocities[number], axis=(0, 1, 2)) for number in range(19)])
    density, flow = moments(field)
    spin_x = slope(flow[2], 1) - slope(flow[1], 2)
    spin_y = slope(flow[0], 2) - slope(flow[2], 0)
    spin_z = slope(flow[1], 0) - slope(flow[0], 1)
    vorticity = jnp.sqrt(spin_x * spin_x + spin_y * spin_y + spin_z * spin_z).astype(jnp.bfloat16)
    level = vorticity.astype(jnp.float32)
    level = level / (level + level_offset)

    def render_one(pair):
        params, flip = pair
        extinction = jnp.zeros_like(level)
        emission = [jnp.zeros_like(level) for channel in range(3)]
        for bump_index in range(TF_BUMPS):
            bump = jnp.exp(-jnp.square((level - params[0, bump_index]) / bump_width))
            extinction = extinction + params[1, bump_index] * bump
            for channel in range(3):
                emission[channel] = emission[channel] + params[2 + channel, bump_index] * bump
        optical = extinction / NX
        inclusive = jnp.cumsum(optical, axis=0)
        total = inclusive[-1]
        front = jnp.where(flip == 1, total[None] - inclusive, inclusive - optical)
        weight = jnp.exp(-front) * (1.0 - jnp.exp(-optical))
        colors = [lax.optimization_barrier(jnp.sum(weight * emission[channel], axis=0)) for channel in range(3)]
        return jnp.stack(colors + [1.0 - jnp.exp(-total)])
    images = lax.map(render_one, (transfer, direction))
    return (field, vorticity, images)
```

```python
import functools

import jax
import jax.numpy as jnp
import numpy as np
from jax import lax
from jax.experimental import pallas as pl
from jax.experimental.pallas import tpu as pltpu
from jax.sharding import PartitionSpec as P

VEL = (
    (0, 0, 0),
    (1, 0, 0), (-1, 0, 0), (0, 1, 0), (0, -1, 0), (0, 0, 1), (0, 0, -1),
    (1, 1, 0), (-1, -1, 0), (1, -1, 0), (-1, 1, 0),
    (1, 0, 1), (-1, 0, -1), (1, 0, -1), (-1, 0, 1),
    (0, 1, 1), (0, -1, -1), (0, 1, -1), (0, -1, 1),
)
WEIGHT = (1.0 / 3.0,) + (1.0 / 18.0,) * 6 + (1.0 / 36.0,) * 12
OMEGA = 1.25
Q = len(VEL)
STEPS = 4
HALO = STEPS + 1
AXIS_PAIRS = ((1, 2), (3, 4), (5, 6))
DIAG_PAIRS = ((7, 8), (9, 10), (11, 12), (13, 14), (15, 16), (17, 18))
SCALE = 8192.0

X_PAIRS = tuple(
    (a, b, 5) for a, b in zip((1, 7, 9, 11, 13), (2, 8, 10, 12, 14))
) + ((0, 3, 4), (4, 5, 4), (6, 15, 4), (16, 17, 4), (18, None, 4))


def low_rows(p):
    return 4 + VEL[p][0]


def face_list(nearest, step):
    sent = []
    for layer in range(1, HALO + 1):
        y = nearest + step * (layer - 1)
        for p in range(Q):
            inward = VEL[p][1] * (-step)
            if layer <= 4 + inward:
                sent.append((y, p))
    return sent


def momentum(f):
    s = {}
    d = {}
    for a, b in AXIS_PAIRS + DIAG_PAIRS:
        s[a] = f[a] + f[b]
        d[a] = f[a] - f[b]
    density = ((s[1] + s[3]) + (s[5] + s[7])) + ((s[9] + s[11]) + (s[13] + s[15])) + (s[17] + f[0])
    jx = (d[1] + d[7]) + (d[9] + d[11]) + d[13]
    jy = (d[3] + d[7]) - (d[9] - d[15]) + d[17]
    jz = (d[5] + d[11]) - (d[13] - d[15]) - d[17]
    return density, (jx, jy, jz), s, d


def collide(f):
    density, j, s, d = momentum(f)
    inverse = 1.0 / density
    u = [c * inverse for c in j]
    speed = j[0] * u[0] + j[1] * u[1] + j[2] * u[2]
    common = density - 1.5 * speed
    out = [None] * Q
    out[0] = (OMEGA * WEIGHT[0]) * common - (OMEGA - 1.0) * f[0]
    rest = 0.5 * (OMEGA - 1.0)
    for pairs, w in ((AXIS_PAIRS, WEIGHT[1]), (DIAG_PAIRS, WEIGHT[7])):
        base = (OMEGA * w) * common
        jw = [(3.0 * OMEGA * w) * c for c in j]
        uw = [1.5 * c for c in u]
        for a, b in pairs:
            project_j = None
            project_u = None
            for axis in range(3):
                c = VEL[a][axis]
                if c == 0:
                    continue
                if project_j is None:
                    assert c == 1
                    project_j, project_u = jw[axis], uw[axis]
                elif c > 0:
                    project_j, project_u = project_j + jw[axis], project_u + uw[axis]
                else:
                    project_j, project_u = project_j - jw[axis], project_u - uw[axis]
            even = (base + project_j * project_u) - rest * s[a]
            odd = project_j - rest * d[a]
            out[a] = even + odd
            out[b] = even - odd
    return out


def code(value, p):
    return jnp.round(value * (SCALE / WEIGHT[p]) - SCALE)


def decode(value, p):
    return value * (WEIGHT[p] / SCALE) + WEIGHT[p]


def row_index():
    return lax.broadcasted_iota(jnp.int32, (8, 128), 0)


def pack16(first, second):
    return jnp.concatenate([first, second], axis=0).astype(jnp.int32).astype(jnp.int16)


def wide(value):
    return value.astype(jnp.int32).astype(jnp.float32)


def first_kernel(depth_cells, width_cells, parity_ref, f_ref, r_ref, da_ref, db_ref, ia_ref, ib_ref):
    tiles = depth_cells // 8
    rows = row_index()

    def at_y(y, carry):
        for j in range(tiles):
            f = [
                f_ref[p, pl.ds(j * 8 * width_cells + y, 8, stride=width_cells), :]
                for p in range(Q)
            ]
            out = collide(f)
            for p in range(Q):
                r_ref[p, y, 8 * j : 8 * j + 8, :] = pltpu.roll(out[p], low_rows(p), 0)
        return carry

    lax.fori_loop(0, width_cells, at_y, 0)

    odd_depth = jnp.full((8, 128), parity_ref[0], jnp.int32) == 1
    odd_image = jnp.full((8, 128), parity_ref[1], jnp.int32) == 1

    def face_x(t, carry):
        for number, (a, b, n) in enumerate(X_PAIRS):
            low, high = [], []
            for k in range(2):
                y = 2 * t + k
                for sent, first_row in ((low, 0), (high, depth_cells - 8)):
                    piece = code(r_ref[a, y, first_row : first_row + 8, :], a)
                    if b is not None:
                        other = code(r_ref[b, y, first_row : first_row + 8, :], b)
                        other = pltpu.roll(other, n, 0)
                        keep = rows < n if sent is high else rows >= n
                        piece = jnp.where(keep, piece, other)
                    sent.append(piece)
            da = [jnp.where(odd_depth, l, h) for l, h in zip(low, high)]
            db = [jnp.where(odd_depth, h, l) for l, h in zip(low, high)]
            da_ref[number, t] = pack16(*da)
            db_ref[number, t] = pack16(*db)
        return carry

    lax.fori_loop(0, width_cells // 2, face_x, 0)

    low_face = face_list(0, 1)
    high_face = face_list(width_cells - 1, -1)
    for index, ((yl, pl_), (yh, ph)) in enumerate(zip(low_face, high_face)):
        for c in range(depth_cells // 16):
            a, b = [], []
            for k in range(2):
                first_row = 16 * c + 8 * k
                low = code(r_ref[pl_, yl, first_row : first_row + 8, :], pl_)
                high = code(r_ref[ph, yh, first_row : first_row + 8, :], ph)
                a.append(jnp.where(odd_image, low, high))
                b.append(jnp.where(odd_image, high, low))
            ia_ref[index, 16 * c : 16 * c + 16, :] = pack16(*a)
            ib_ref[index, 16 * c : 16 * c + 16, :] = pack16(*b)


def x_halo(low, high, n, second, rows):
    if second:
        low = pltpu.roll(low, 8 - n, 0)
        high = pltpu.roll(high, 8 - n, 0)
        n = 8 - n
    return jnp.where(rows < n, low, high)


X_PLACE = {}
for number_, (a_, b_, n_) in enumerate(X_PAIRS):
    X_PLACE[a_] = (number_, n_, False)
    if b_ is not None:
        X_PLACE[b_] = (number_, n_, True)


def corner_kernel(width_cells, parity_ref, xa_ref, xb_ref, h_ref, ca_ref, cb_ref):
    rows = row_index()
    odd_depth = jnp.full((8, 128), parity_ref[0], jnp.int32) == 1
    odd_image = jnp.full((8, 128), parity_ref[1], jnp.int32) == 1

    def halo(t, carry):
        for number, (a, b, n) in enumerate(X_PAIRS):
            va = wide(xa_ref[number, t])
            vb = wide(xb_ref[number, t])
            for k in range(2):
                pa, pb = va[8 * k : 8 * k + 8], vb[8 * k : 8 * k + 8]
                low = jnp.where(odd_depth, pa, pb)
                high = jnp.where(odd_depth, pb, pa)
                h_ref[a, 2 * t + k] = x_halo(low, high, n, False, rows)
                if b is not None:
                    h_ref[b, 2 * t + k] = x_halo(low, high, n, True, rows)
        return carry

    lax.fori_loop(0, width_cells // 2, halo, 0)
    low_face = face_list(0, 1)
    high_face = face_list(width_cells - 1, -1)
    for index in range(0, len(low_face), 2):
        a, b = [], []
        for (yl, pl_), (yh, ph) in zip(low_face[index : index + 2], high_face[index : index + 2]):
            low, high = h_ref[pl_, yl], h_ref[ph, yh]
            a.append(jnp.where(odd_image, low, high))
            b.append(jnp.where(odd_image, high, low))
        ca_ref[index // 2] = pack16(*a)
        cb_ref[index // 2] = pack16(*b)


PAD = 8


def steps_kernel(
    depth_cells, width_cells, parity_ref, r_ref, h_ref, ya_ref, yb_ref, ca_ref, cb_ref,
    out_ref, vort_ref, sa_ref, sb_ref, flow_ref, plain_ref,
):
    tiles = depth_cells // 8
    wide_tiles = tiles + 1
    rows = row_index()
    odd_image = jnp.full((8, 128), parity_ref[1], jnp.int32) == 1

    def streamed(p, y, pieces, halo):
        n = low_rows(p)
        before = halo
        for t in range(wide_tiles):
            here = pieces[t] if t < tiles else halo
            sa_ref[p, y, PAD + 8 * t : PAD + 8 * t + 8, :] = jnp.where(rows < n, before, here)
            before = here

    def own(y, carry):
        for p in range(Q):
            pieces = [r_ref[p, y, 8 * t : 8 * t + 8, :] for t in range(tiles)]
            streamed(p, y + HALO, pieces, decode(h_ref[p, y], p))
        return carry

    lax.fori_loop(0, width_cells, own, 0)

    low_face = face_list(0, 1)
    high_face = face_list(width_cells - 1, -1)
    for index in range(0, len(low_face), 2):
        corner_a, corner_b = wide(ca_ref[index // 2]), wide(cb_ref[index // 2])
        for k in range(2):
            (yl, pl_), (yh, ph) = low_face[index + k], high_face[index + k]
            ca, cb = corner_a[8 * k : 8 * k + 8], corner_b[8 * k : 8 * k + 8]
            low = [jnp.where(odd_image, ca, cb)]
            high = [jnp.where(odd_image, cb, ca)]
            for c in range(depth_cells // 16):
                ya = wide(ya_ref[index + k, 16 * c : 16 * c + 16, :])
                yb = wide(yb_ref[index + k, 16 * c : 16 * c + 16, :])
                for half in range(2):
                    a, b = ya[8 * half : 8 * half + 8], yb[8 * half : 8 * half + 8]
                    low.append(jnp.where(odd_image, a, b))
                    high.append(jnp.where(odd_image, b, a))
            low = [decode(v, ph) for v in low]
            high = [decode(v, pl_) for v in high]
            streamed(ph, yh - width_cells + HALO, low[1:], low[0])
            streamed(pl_, yl + width_cells + HALO, high[1:], high[0])

    def step(source, target, reach, shift):
        def at_y(y, carry):
            for t in range(wide_tiles):
                first = PAD + 8 * t
                f = [source[p, y - VEL[p][1], first : first + 8, :] for p in range(Q)]
                out = collide(f)
                for p in range(Q):
                    cx, _, cz = VEL[p]
                    value = out[p] if cz == 0 else pltpu.roll(out[p], cz % 128, 1)
                    row = first + shift + cx
                    target[p, y, row : row + 8, :] = value
            return carry

        lax.fori_loop(HALO - reach, HALO + width_cells + reach, at_y, 0)

    def first_step(source, target, reach):
        def at_y(y, carry):
            for t in range(wide_tiles):
                first = PAD + 8 * t
                f = []
                for p in range(Q):
                    cz = VEL[p][2]
                    value = source[p, y - VEL[p][1], first : first + 8, :]
                    f.append(value if cz == 0 else pltpu.roll(value, cz % 128, 1))
                out = collide(f)
                for p in range(Q):
                    cx, _, cz = VEL[p]
                    value = out[p] if cz == 0 else pltpu.roll(out[p], cz % 128, 1)
                    target[p, y, first + cx : first + cx + 8, :] = value
            return carry

        lax.fori_loop(HALO - reach, HALO + width_cells + reach, at_y, 0)

    first_step(sa_ref, sb_ref, 4)
    step(sb_ref, sa_ref, 3, 0)
    step(sa_ref, sb_ref, 2, 4)
    base = PAD + 8

    def flow_at(y, carry):
        for t in range(-1, tiles + 1):
            first = base + 8 * t
            f = [sb_ref[p, y - VEL[p][1], first : first + 8, :] for p in range(Q)]
            density, j, _, _ = momentum(f)
            inverse = 1.0 / density
            for axis in range(3):
                flow_ref[axis, y, first : first + 8, :] = j[axis] * inverse
        return carry

    lax.fori_loop(HALO - 1, HALO + width_cells + 1, flow_at, 0)

    def final_at(y, carry):
        for t in range(tiles):
            first = base + 8 * t
            for p in range(Q):
                out_ref[p, pl.ds(8 * t * width_cells + y - HALO, 8, stride=width_cells), :] = sb_ref[
                    p, y - VEL[p][1], first : first + 8, :
                ]
        return carry

    lax.fori_loop(HALO, HALO + width_cells, final_at, 0)

    def spin_at(y, carry):
        for t in range(tiles):
            first = base + 8 * t

            def dx(axis):
                return (flow_ref[axis, y, first + 1 : first + 9, :] - flow_ref[axis, y, first - 1 : first + 7, :]) * 0.5

            def dy(axis):
                return (flow_ref[axis, y + 1, first : first + 8, :] - flow_ref[axis, y - 1, first : first + 8, :]) * 0.5

            def dz(axis):
                value = flow_ref[axis, y, first : first + 8, :]
                return (pltpu.roll(value, 127, 1) - pltpu.roll(value, 1, 1)) * 0.5

            sx = dy(2) - dz(1)
            sy = dz(0) - dx(2)
            sz = dx(1) - dy(0)
            plain_ref[pl.ds(8 * t * width_cells + y - HALO, 8, stride=width_cells), :] = jnp.sqrt(
                sx * sx + sy * sy + sz * sz
            )
        return carry

    lax.fori_loop(HALO, HALO + width_cells, spin_at, 0)

    def rounded(x, carry):
        at = pl.ds(pl.multiple_of(x * 16, 16), 16)
        vort_ref[at, :] = plain_ref[at, :].astype(jnp.bfloat16)
        return carry

    lax.fori_loop(0, depth_cells * width_cells // 16, rounded, 0)


BUMP_WIDTH = 0.15
LEVEL_OFFSET = 0.05
STRETCH = float(np.sqrt(np.log2(np.e)) / BUMP_WIDTH)
CENTRE = 4.0
LOG2E = float(np.log2(np.e))


def bump_tables(transfer, ray_cells):
    b = STRETCH * transfer[:, 0] - CENTRE
    fade = jnp.exp2(-b * b)
    strength = transfer[:, 1:] * fade[:, None]
    strength = strength.at[:, 0].multiply(LOG2E / ray_cells)
    return jnp.concatenate([(2.0 * b)[:, None], strength], axis=1)


def render_kernel(depth_cells, width_cells, groups, pick_ref, table_ref, backward_ref, vort_ref, image_ref, place_ref, fade_ref):
    bumps = table_ref.shape[1] // 5

    def prepare(x, carry):
        at = pl.ds(pl.multiple_of(x * width_cells, width_cells), width_cells)
        value = vort_ref[at, :].astype(jnp.float32)
        level = value / (value + LEVEL_OFFSET)
        place = STRETCH * level - CENTRE
        place_ref[x] = place
        fade_ref[x] = jnp.exp2(-place * place)
        return carry

    lax.fori_loop(0, depth_cells, prepare, 0)

    def one(group, carry):
        m = 2 * group + pick_ref[0]
        backward = backward_ref[m]
        centre = [table_ref[m, k] for k in range(bumps)]
        strength = [[table_ref[m, (1 + c) * bumps + k] for k in range(bumps)] for c in range(4)]

        def cell(step, state):
            clear, red, green, blue = state
            x = jnp.where(backward == 1, depth_cells - 1 - step, step)
            place, fade = place_ref[x], fade_ref[x]
            total = [None] * 4
            for k in range(bumps):
                bump = jnp.exp2(place * centre[k])
                for c in range(4):
                    term = bump * strength[c][k]
                    total[c] = term if total[c] is None else total[c] + term
            behind = clear * jnp.exp2(-(total[0] * fade))
            weight = (clear - behind) * fade
            return (behind, red + weight * total[1], green + weight * total[2], blue + weight * total[3])

        zero = jnp.zeros((width_cells, 128), jnp.float32)
        clear, red, green, blue = lax.fori_loop(0, depth_cells, cell, (zero + 1.0, zero, zero, zero))
        image_ref[group, 0] = red
        image_ref[group, 1] = green
        image_ref[group, 2] = blue
        image_ref[group, 3] = clear
        return carry

    lax.fori_loop(0, groups, one, 0)


def composite_kernel(slabs, pick_ref, backward_ref, piece_ref, image_ref):
    backward = backward_ref[pick_ref[0]]
    shape = piece_ref.shape[2:]
    clear = jnp.ones(shape, jnp.float32)
    color = [jnp.zeros(shape, jnp.float32) for c in range(3)]
    for step in range(slabs):
        s = jnp.where(backward == 1, slabs - 1 - step, step)
        color = [color[c] + clear * piece_ref[s, c] for c in range(3)]
        clear = clear * piece_ref[s, 3]
    for c in range(3):
        image_ref[c] = color[c]
    image_ref[3] = 1.0 - clear


VMEM = pl.BlockSpec(memory_space=pltpu.VMEM)
SMEM = pl.BlockSpec(memory_space=pltpu.SMEM)
GRANT = pltpu.CompilerParams(vmem_limit_bytes=58 * 1024 * 1024)


def partner(index, count, phase):
    return index ^ 1 if phase == 0 else (((index + 1) ^ 1) - 1) % count


def swap(value, axis, count, phase):
    return lax.ppermute(value, axis, [(i, partner(i, count, phase)) for i in range(count)])


def on_device(populations, transfer, direction):
    _, depth_cells, width_cells, lanes = populations.shape
    depth_count, image_count = lax.axis_size("depth"), lax.axis_size("image")
    ray_cells = depth_cells * depth_count
    cells = depth_cells * width_cells
    f32, i16 = jnp.float32, jnp.int16
    d, i = lax.axis_index("depth"), lax.axis_index("image")
    parity = jnp.stack([d % 2, i % 2]).astype(jnp.int32)
    faces = len(face_list(0, 1))

    tables = lax.all_gather(
        jnp.concatenate([transfer.reshape(1, -1), direction.astype(f32)[:, None]], axis=1),
        "image", axis=0, tiled=True,
    )
    backward = tables[:, -1].astype(jnp.int32)
    bumps = transfer.shape[2]
    tables = bump_tables(tables[:, :-1].reshape(-1, 5, bumps), ray_cells).reshape(-1, 5 * bumps)

    x_shape = jax.ShapeDtypeStruct((len(X_PAIRS), width_cells // 2, 16, lanes), i16)
    y_shape = jax.ShapeDtypeStruct((faces, depth_cells, lanes), i16)
    c_shape = jax.ShapeDtypeStruct((faces // 2, 16, lanes), i16)
    turned, da, db, ia, ib = pl.pallas_call(
        functools.partial(first_kernel, depth_cells, width_cells),
        out_shape=(
            jax.ShapeDtypeStruct((Q, width_cells, depth_cells, lanes), f32),
            x_shape, x_shape, y_shape, y_shape,
        ),
        in_specs=[SMEM, VMEM],
        out_specs=(VMEM,) * 5,
        compiler_params=GRANT,
        name="first",
    )(parity, populations.reshape(Q, cells, lanes))

    xa = swap(da, "depth", depth_count, 0)
    xb = swap(db, "depth", depth_count, 1)
    ya = swap(ia, "image", image_count, 0)
    yb = swap(ib, "image", image_count, 1)
    halo, ca, cb = pl.pallas_call(
        functools.partial(corner_kernel, width_cells),
        out_shape=(jax.ShapeDtypeStruct((Q, width_cells, 8, lanes), f32), c_shape, c_shape),
        in_specs=[SMEM, VMEM, VMEM],
        out_specs=(VMEM,) * 3,
        compiler_params=GRANT,
        name="corner",
    )(parity, xa, xb)
    ca = swap(ca, "image", image_count, 0)
    cb = swap(cb, "image", image_count, 1)

    depth_rows = depth_cells + 8 + 2 * PAD
    width_rows = width_cells + 2 * HALO
    final, vorticity = pl.pallas_call(
        functools.partial(steps_kernel, depth_cells, width_cells),
        out_shape=(
            jax.ShapeDtypeStruct((Q, cells, lanes), f32),
            jax.ShapeDtypeStruct((cells, lanes), jnp.bfloat16),
        ),
        in_specs=[SMEM] + [VMEM] * 6,
        out_specs=(VMEM, VMEM),
        scratch_shapes=[
            pltpu.VMEM((Q, width_rows, depth_rows, lanes), f32),
            pltpu.VMEM((Q, width_rows, depth_rows, lanes), f32),
            pltpu.VMEM((3, width_rows, depth_rows, lanes), f32),
            pltpu.VMEM((cells, lanes), f32),
        ],
        compiler_params=GRANT,
        name="steps",
    )(parity, turned, halo, ya, yb, ca, cb)

    groups = depth_count
    pieces = []
    for k in range(2):
        pick = ((i + k) % 2).astype(jnp.int32)[None]
        partial = pl.pallas_call(
            functools.partial(render_kernel, depth_cells, width_cells, groups),
            out_shape=jax.ShapeDtypeStruct((groups, 4, width_cells, lanes), f32),
            in_specs=[SMEM, SMEM, SMEM, VMEM],
            out_specs=VMEM,
            scratch_shapes=[
                pltpu.VMEM((depth_cells, width_cells, lanes), f32),
                pltpu.VMEM((depth_cells, width_cells, lanes), f32),
            ],
            compiler_params=GRANT,
            name="render",
        )(pick, tables, backward, vorticity)
        slabs = lax.all_to_all(partial, "depth", 0, 0, tiled=True)
        image = pl.pallas_call(
            functools.partial(composite_kernel, depth_count),
            out_shape=jax.ShapeDtypeStruct((4, width_cells, lanes), f32),
            in_specs=[SMEM, SMEM, VMEM],
            out_specs=VMEM,
            name="composite",
        )(2 * d.astype(jnp.int32)[None] + pick, backward, slabs)
        route = []
        for sd in range(depth_count):
            for si in range(image_count):
                route.append((sd * image_count + si, (si // 2) * image_count + 2 * sd + (si + k) % 2))
        pieces.append(lax.ppermute(image, ("depth", "image"), route))
    flip = (i % 2) == 1
    top = jnp.where(flip, pieces[1], pieces[0])
    bottom = jnp.where(flip, pieces[0], pieces[1])
    images = jnp.concatenate([top, bottom], axis=1)[None]
    return (
        final.reshape(populations.shape),
        vorticity.reshape(depth_cells, width_cells, lanes),
        images,
    )


def solution(mesh):
    in_specs = (P(None, "depth", "image", None), P("image", None, None), P("image"))
    out_specs = (
        P(None, "depth", "image", None),
        P("depth", "image", None),
        P("image", None, "depth", None),
    )
    return jax.shard_map(
        on_device, mesh=mesh, in_specs=in_specs, out_specs=out_specs, check_vma=False
    )
```

```python
import functools

import jax
import jax.numpy as jnp
import numpy as np
from jax import lax
from jax.experimental import pallas as pl
from jax.experimental.pallas import tpu as pltpu
from jax.sharding import PartitionSpec as P

VEL = (
    (0, 0, 0),
    (1, 0, 0), (-1, 0, 0), (0, 1, 0), (0, -1, 0), (0, 0, 1), (0, 0, -1),
    (1, 1, 0), (-1, -1, 0), (1, -1, 0), (-1, 1, 0),
    (1, 0, 1), (-1, 0, -1), (1, 0, -1), (-1, 0, 1),
    (0, 1, 1), (0, -1, -1), (0, 1, -1), (0, -1, 1),
)
WEIGHT = (1.0 / 3.0,) + (1.0 / 18.0,) * 6 + (1.0 / 36.0,) * 12
OMEGA = 1.25
Q = len(VEL)
STEPS = 4
HALO = STEPS + 1
AXIS_PAIRS = ((1, 2), (3, 4), (5, 6))
DIAG_PAIRS = ((7, 8), (9, 10), (11, 12), (13, 14), (15, 16), (17, 18))
SCALE = 8192.0

X_PAIRS = tuple(
    (a, b, 5) for a, b in zip((1, 7, 9, 11, 13), (2, 8, 10, 12, 14))
) + ((0, 3, 4), (4, 5, 4), (6, 15, 4), (16, 17, 4), (18, None, 4))


def low_rows(p):
    return 4 + VEL[p][0]


def face_list(nearest, step):
    sent = []
    for layer in range(1, HALO + 1):
        y = nearest + step * (layer - 1)
        for p in range(Q):
            inward = VEL[p][1] * (-step)
            if layer <= 4 + inward:
                sent.append((y, p))
    return sent


def momentum(f):
    s = {}
    d = {}
    for a, b in AXIS_PAIRS + DIAG_PAIRS:
        s[a] = f[a] + f[b]
        d[a] = f[a] - f[b]
    density = ((s[1] + s[3]) + (s[5] + s[7])) + ((s[9] + s[11]) + (s[13] + s[15])) + (s[17] + f[0])
    jx = (d[1] + d[7]) + (d[9] + d[11]) + d[13]
    jy = (d[3] + d[7]) - (d[9] - d[15]) + d[17]
    jz = (d[5] + d[11]) - (d[13] - d[15]) - d[17]
    return density, (jx, jy, jz), s, d


def collide(f):
    density, j, s, d = momentum(f)
    inverse = 1.0 / density
    u = [c * inverse for c in j]
    speed = j[0] * u[0] + j[1] * u[1] + j[2] * u[2]
    common = density - 1.5 * speed
    out = [None] * Q
    out[0] = (OMEGA * WEIGHT[0]) * common - (OMEGA - 1.0) * f[0]
    rest = 0.5 * (OMEGA - 1.0)
    for pairs, w in ((AXIS_PAIRS, WEIGHT[1]), (DIAG_PAIRS, WEIGHT[7])):
        base = (OMEGA * w) * common
        jw = [(3.0 * OMEGA * w) * c for c in j]
        uw = [1.5 * c for c in u]
        for a, b in pairs:
            project_j = None
            project_u = None
            for axis in range(3):
                c = VEL[a][axis]
                if c == 0:
                    continue
                if project_j is None:
                    assert c == 1
                    project_j, project_u = jw[axis], uw[axis]
                elif c > 0:
                    project_j, project_u = project_j + jw[axis], project_u + uw[axis]
                else:
                    project_j, project_u = project_j - jw[axis], project_u - uw[axis]
            even = (base + project_j * project_u) - rest * s[a]
            odd = project_j - rest * d[a]
            out[a] = even + odd
            out[b] = even - odd
    return out


def code(value, p):
    return jnp.round(value * (SCALE / WEIGHT[p]) - SCALE)


def decode(value, p):
    return value * (WEIGHT[p] / SCALE) + WEIGHT[p]


def row_index():
    return lax.broadcasted_iota(jnp.int32, (8, 128), 0)


def pack16(first, second):
    return jnp.concatenate([first, second], axis=0).astype(jnp.int32).astype(jnp.int16)


def wide(value):
    return value.astype(jnp.int32).astype(jnp.float32)


def first_kernel(depth_cells, width_cells, parity_ref, f_ref, r_ref, da_ref, db_ref, ia_ref, ib_ref):
    tiles = depth_cells // 8
    rows = row_index()

    def at_y(y, carry):
        for j in range(tiles):
            f = [
                f_ref[p, pl.ds(j * 8 * width_cells + y, 8, stride=width_cells), :]
                for p in range(Q)
            ]
            out = collide(f)
            for p in range(Q):
                value = pltpu.roll(out[p], low_rows(p), 0)
                cz = VEL[p][2]
                r_ref[p, y, 8 * j : 8 * j + 8, :] = value if cz == 0 else pltpu.roll(value, cz % 128, 1)
        return carry

    lax.fori_loop(0, width_cells, at_y, 0)

    odd_depth = jnp.full((8, 128), parity_ref[0], jnp.int32) == 1
    odd_image = jnp.full((8, 128), parity_ref[1], jnp.int32) == 1

    def face_x(t, carry):
        for number, (a, b, n) in enumerate(X_PAIRS):
            low, high = [], []
            for k in range(2):
                y = 2 * t + k
                for sent, first_row in ((low, 0), (high, depth_cells - 8)):
                    piece = code(r_ref[a, y, first_row : first_row + 8, :], a)
                    if b is not None:
                        other = code(r_ref[b, y, first_row : first_row + 8, :], b)
                        other = pltpu.roll(other, n, 0)
                        keep = rows < n if sent is high else rows >= n
                        piece = jnp.where(keep, piece, other)
                    sent.append(piece)
            da = [jnp.where(odd_depth, l, h) for l, h in zip(low, high)]
            db = [jnp.where(odd_depth, h, l) for l, h in zip(low, high)]
            da_ref[number, t] = pack16(*da)
            db_ref[number, t] = pack16(*db)
        return carry

    lax.fori_loop(0, width_cells // 2, face_x, 0)

    low_face = face_list(0, 1)
    high_face = face_list(width_cells - 1, -1)
    for index, ((yl, pl_), (yh, ph)) in enumerate(zip(low_face, high_face)):
        for c in range(depth_cells // 16):
            a, b = [], []
            for k in range(2):
                first_row = 16 * c + 8 * k
                low = code(r_ref[pl_, yl, first_row : first_row + 8, :], pl_)
                high = code(r_ref[ph, yh, first_row : first_row + 8, :], ph)
                a.append(jnp.where(odd_image, low, high))
                b.append(jnp.where(odd_image, high, low))
            ia_ref[index, 16 * c : 16 * c + 16, :] = pack16(*a)
            ib_ref[index, 16 * c : 16 * c + 16, :] = pack16(*b)


def x_halo(low, high, n, second, rows):
    if second:
        low = pltpu.roll(low, 8 - n, 0)
        high = pltpu.roll(high, 8 - n, 0)
        n = 8 - n
    return jnp.where(rows < n, low, high)


X_PLACE = {}
for number_, (a_, b_, n_) in enumerate(X_PAIRS):
    X_PLACE[a_] = (number_, n_, False)
    if b_ is not None:
        X_PLACE[b_] = (number_, n_, True)


def corner_kernel(width_cells, parity_ref, xa_ref, xb_ref, h_ref, ca_ref, cb_ref):
    rows = row_index()
    odd_depth = jnp.full((8, 128), parity_ref[0], jnp.int32) == 1
    odd_image = jnp.full((8, 128), parity_ref[1], jnp.int32) == 1

    def halo(t, carry):
        for number, (a, b, n) in enumerate(X_PAIRS):
            va = wide(xa_ref[number, t])
            vb = wide(xb_ref[number, t])
            for k in range(2):
                pa, pb = va[8 * k : 8 * k + 8], vb[8 * k : 8 * k + 8]
                low = jnp.where(odd_depth, pa, pb)
                high = jnp.where(odd_depth, pb, pa)
                h_ref[a, 2 * t + k] = x_halo(low, high, n, False, rows)
                if b is not None:
                    h_ref[b, 2 * t + k] = x_halo(low, high, n, True, rows)
        return carry

    lax.fori_loop(0, width_cells // 2, halo, 0)
    low_face = face_list(0, 1)
    high_face = face_list(width_cells - 1, -1)
    for index in range(0, len(low_face), 2):
        a, b = [], []
        for (yl, pl_), (yh, ph) in zip(low_face[index : index + 2], high_face[index : index + 2]):
            low, high = h_ref[pl_, yl], h_ref[ph, yh]
            a.append(jnp.where(odd_image, low, high))
            b.append(jnp.where(odd_image, high, low))
        ca_ref[index // 2] = pack16(*a)
        cb_ref[index // 2] = pack16(*b)


PAD = 8


def steps_kernel(
    depth_cells, width_cells, parity_ref, r_ref, h_ref, ya_ref, yb_ref, ca_ref, cb_ref,
    out_ref, vort_ref, sa_ref, sb_ref, flow_ref, plain_ref,
):
    tiles = depth_cells // 8
    wide_tiles = tiles + 1
    rows = row_index()
    odd_image = jnp.full((8, 128), parity_ref[1], jnp.int32) == 1

    def streamed(p, y, pieces, halo):
        n = low_rows(p)
        before = halo
        for t in range(wide_tiles):
            here = pieces[t] if t < tiles else halo
            sa_ref[p, y, PAD + 8 * t : PAD + 8 * t + 8, :] = jnp.where(rows < n, before, here)
            before = here

    def own(y, carry):
        for p in range(Q):
            pieces = [r_ref[p, y, 8 * t : 8 * t + 8, :] for t in range(tiles)]
            streamed(p, y + HALO, pieces, decode(h_ref[p, y], p))
        return carry

    lax.fori_loop(0, width_cells, own, 0)

    low_face = face_list(0, 1)
    high_face = face_list(width_cells - 1, -1)
    for index in range(0, len(low_face), 2):
        corner_a, corner_b = wide(ca_ref[index // 2]), wide(cb_ref[index // 2])
        for k in range(2):
            (yl, pl_), (yh, ph) = low_face[index + k], high_face[index + k]
            ca, cb = corner_a[8 * k : 8 * k + 8], corner_b[8 * k : 8 * k + 8]
            low = [jnp.where(odd_image, ca, cb)]
            high = [jnp.where(odd_image, cb, ca)]
            for c in range(depth_cells // 16):
                ya = wide(ya_ref[index + k, 16 * c : 16 * c + 16, :])
                yb = wide(yb_ref[index + k, 16 * c : 16 * c + 16, :])
                for half in range(2):
                    a, b = ya[8 * half : 8 * half + 8], yb[8 * half : 8 * half + 8]
                    low.append(jnp.where(odd_image, a, b))
                    high.append(jnp.where(odd_image, b, a))
            low = [decode(v, ph) for v in low]
            high = [decode(v, pl_) for v in high]
            streamed(ph, yh - width_cells + HALO, low[1:], low[0])
            streamed(pl_, yl + width_cells + HALO, high[1:], high[0])

    def step(source, target, reach, shift):
        def at_y(y, carry):
            for t in range(wide_tiles):
                first = PAD + 8 * t
                f = [source[p, y - VEL[p][1], first : first + 8, :] for p in range(Q)]
                out = collide(f)
                for p in range(Q):
                    cx, _, cz = VEL[p]
                    value = out[p] if cz == 0 else pltpu.roll(out[p], cz % 128, 1)
                    row = first + shift + cx
                    target[p, y, row : row + 8, :] = value
            return carry

        lax.fori_loop(HALO - reach, HALO + width_cells + reach, at_y, 0)

    step(sa_ref, sb_ref, 4, 0)
    step(sb_ref, sa_ref, 3, 0)
    step(sa_ref, sb_ref, 2, 4)
    base = PAD + 8

    def flow_at(y, carry):
        for t in range(-1, tiles + 1):
            first = base + 8 * t
            f = [sb_ref[p, y - VEL[p][1], first : first + 8, :] for p in range(Q)]
            density, j, _, _ = momentum(f)
            inverse = 1.0 / density
            for axis in range(3):
                flow_ref[axis, y, first : first + 8, :] = j[axis] * inverse
        return carry

    lax.fori_loop(HALO - 1, HALO + width_cells + 1, flow_at, 0)

    def final_at(y, carry):
        for t in range(tiles):
            first = base + 8 * t
            for p in range(Q):
                out_ref[p, pl.ds(8 * t * width_cells + y - HALO, 8, stride=width_cells), :] = sb_ref[
                    p, y - VEL[p][1], first : first + 8, :
                ]
        return carry

    lax.fori_loop(HALO, HALO + width_cells, final_at, 0)

    def spin_at(y, carry):
        for t in range(tiles):
            first = base + 8 * t

            def dx(axis):
                return (flow_ref[axis, y, first + 1 : first + 9, :] - flow_ref[axis, y, first - 1 : first + 7, :]) * 0.5

            def dy(axis):
                return (flow_ref[axis, y + 1, first : first + 8, :] - flow_ref[axis, y - 1, first : first + 8, :]) * 0.5

            def dz(axis):
                value = flow_ref[axis, y, first : first + 8, :]
                return (pltpu.roll(value, 127, 1) - pltpu.roll(value, 1, 1)) * 0.5

            sx = dy(2) - dz(1)
            sy = dz(0) - dx(2)
            sz = dx(1) - dy(0)
            plain_ref[pl.ds(8 * t * width_cells + y - HALO, 8, stride=width_cells), :] = jnp.sqrt(
                sx * sx + sy * sy + sz * sz
            )
        return carry

    lax.fori_loop(HALO, HALO + width_cells, spin_at, 0)

    def rounded(x, carry):
        at = pl.ds(pl.multiple_of(x * 16, 16), 16)
        vort_ref[at, :] = plain_ref[at, :].astype(jnp.bfloat16)
        return carry

    lax.fori_loop(0, depth_cells * width_cells // 16, rounded, 0)


BUMP_WIDTH = 0.15
LEVEL_OFFSET = 0.05
STRETCH = float(np.sqrt(np.log2(np.e)) / BUMP_WIDTH)
CENTRE = 4.0
LOG2E = float(np.log2(np.e))


def bump_tables(transfer, ray_cells):
    b = STRETCH * transfer[:, 0] - CENTRE
    fade = jnp.exp2(-b * b)
    strength = transfer[:, 1:] * fade[:, None]
    strength = strength.at[:, 0].multiply(LOG2E / ray_cells)
    return jnp.concatenate([(2.0 * b)[:, None], strength], axis=1)


BLOCK = 4


def render_kernel(depth_cells, width_cells, groups, pick_ref, table_ref, backward_ref, vort_ref, image_ref, place_ref, fade_ref):
    bumps = table_ref.shape[1] // 5

    def prepare(x, carry):
        at = pl.ds(pl.multiple_of(x * width_cells, width_cells), width_cells)
        value = vort_ref[at, :].astype(jnp.float32)
        level = value / (value + LEVEL_OFFSET)
        place = STRETCH * level - CENTRE
        fade = jnp.exp2(-place * place)
        for order, to in ((0, x), (1, depth_cells - 1 - x)):
            place_ref[order, to] = place
            fade_ref[order, to] = fade
        return carry

    lax.fori_loop(0, depth_cells, prepare, 0)

    def one(group, carry):
        m = 2 * group + pick_ref[0]
        order = backward_ref[m]

        def cells(block, state):
            clear, red, green, blue = state
            at = pl.ds(block * BLOCK, BLOCK)
            place = place_ref[order, at]
            total = [None] * 4
            for k in range(bumps):
                bump = jnp.exp2(place * table_ref[m, k])
                for c in range(4):
                    term = bump * table_ref[m, (1 + c) * bumps + k]
                    total[c] = term if total[c] is None else total[c] + term
            fade = fade_ref[order, at]
            passing = jnp.exp2(-(total[0] * fade))
            for b in range(BLOCK):
                behind = clear * passing[b]
                weight = (clear - behind) * fade[b]
                clear = behind
                red = red + weight * total[1][b]
                green = green + weight * total[2][b]
                blue = blue + weight * total[3][b]
            return clear, red, green, blue

        zero = jnp.zeros((width_cells, 128), jnp.float32)
        clear, red, green, blue = lax.fori_loop(0, depth_cells // BLOCK, cells, (zero + 1.0, zero, zero, zero))
        image_ref[group, 0] = red
        image_ref[group, 1] = green
        image_ref[group, 2] = blue
        image_ref[group, 3] = clear
        return carry

    lax.fori_loop(0, groups, one, 0)


def composite_kernel(slabs, pick_ref, backward_ref, piece_ref, image_ref):
    backward = backward_ref[pick_ref[0]]
    shape = piece_ref.shape[2:]
    clear = jnp.ones(shape, jnp.float32)
    color = [jnp.zeros(shape, jnp.float32) for c in range(3)]
    for step in range(slabs):
        s = jnp.where(backward == 1, slabs - 1 - step, step)
        color = [color[c] + clear * piece_ref[s, c] for c in range(3)]
        clear = clear * piece_ref[s, 3]
    for c in range(3):
        image_ref[c] = color[c]
    image_ref[3] = 1.0 - clear


VMEM = pl.BlockSpec(memory_space=pltpu.VMEM)
SMEM = pl.BlockSpec(memory_space=pltpu.SMEM)
GRANT = pltpu.CompilerParams(vmem_limit_bytes=58 * 1024 * 1024)


def cost(microseconds):
    return pl.CostEstimate(flops=0, bytes_accessed=int(microseconds * 3.69e6), transcendentals=0)


def partner(index, count, phase):
    return index ^ 1 if phase == 0 else (((index + 1) ^ 1) - 1) % count


def swap(value, axis, count, phase):
    return lax.ppermute(value, axis, [(i, partner(i, count, phase)) for i in range(count)])


def on_device(populations, transfer, direction):
    _, depth_cells, width_cells, lanes = populations.shape
    depth_count, image_count = lax.axis_size("depth"), lax.axis_size("image")
    ray_cells = depth_cells * depth_count
    cells = depth_cells * width_cells
    f32, i16 = jnp.float32, jnp.int16
    d, i = lax.axis_index("depth"), lax.axis_index("image")
    parity = jnp.stack([d % 2, i % 2]).astype(jnp.int32)
    faces = len(face_list(0, 1))

    x_shape = jax.ShapeDtypeStruct((len(X_PAIRS), width_cells // 2, 16, lanes), i16)
    y_shape = jax.ShapeDtypeStruct((faces, depth_cells, lanes), i16)
    c_shape = jax.ShapeDtypeStruct((faces // 2, 16, lanes), i16)
    turned, da, db, ia, ib = pl.pallas_call(
        functools.partial(first_kernel, depth_cells, width_cells),
        out_shape=(
            jax.ShapeDtypeStruct((Q, width_cells, depth_cells, lanes), f32),
            x_shape, x_shape, y_shape, y_shape,
        ),
        in_specs=[SMEM, VMEM],
        out_specs=(VMEM,) * 5,
        compiler_params=GRANT,
        cost_estimate=cost(12),
        name="first",
    )(parity, populations.reshape(Q, cells, lanes))

    xa = swap(da, "depth", depth_count, 0)
    xb = swap(db, "depth", depth_count, 1)
    ya = swap(ia, "image", image_count, 0)
    yb = swap(ib, "image", image_count, 1)
    halo, ca, cb = pl.pallas_call(
        functools.partial(corner_kernel, width_cells),
        out_shape=(jax.ShapeDtypeStruct((Q, width_cells, 8, lanes), f32), c_shape, c_shape),
        in_specs=[SMEM, VMEM, VMEM],
        out_specs=(VMEM,) * 3,
        compiler_params=GRANT,
        cost_estimate=cost(2),
        name="corner",
    )(parity, xa, xb)
    sent_a, sent_b = ca, cb
    ca = swap(sent_a, "image", image_count, 0)
    cb = swap(sent_b, "image", image_count, 1)

    bumps = transfer.shape[2]
    row = jnp.concatenate([transfer.reshape(-1), direction.astype(f32)])
    row = jnp.pad(row, (0, lanes - row.shape[0]))
    row, _ = lax.optimization_barrier((row, ia))
    tables = lax.all_to_all(
        jnp.broadcast_to(row, (image_count, 8, lanes)), "image", 0, 0, tiled=True
    )[:, 0]
    backward = tables[:, 5 * bumps].astype(jnp.int32)
    tables = bump_tables(tables[:, : 5 * bumps].reshape(-1, 5, bumps), ray_cells).reshape(-1, 5 * bumps)

    depth_rows = depth_cells + 8 + 2 * PAD
    width_rows = width_cells + 2 * HALO
    final, vorticity = pl.pallas_call(
        functools.partial(steps_kernel, depth_cells, width_cells),
        out_shape=(
            jax.ShapeDtypeStruct((Q, cells, lanes), f32),
            jax.ShapeDtypeStruct((cells, lanes), jnp.bfloat16),
        ),
        in_specs=[SMEM] + [VMEM] * 6,
        out_specs=(VMEM, VMEM),
        scratch_shapes=[
            pltpu.VMEM((Q, width_rows, depth_rows, lanes), f32),
            pltpu.VMEM((Q, width_rows, depth_rows, lanes), f32),
            pltpu.VMEM((3, width_rows, depth_rows, lanes), f32),
            pltpu.VMEM((cells, lanes), f32),
        ],
        compiler_params=GRANT,
        cost_estimate=cost(25),
        name="steps",
    )(parity, turned, halo, ya, yb, ca, cb)

    groups = depth_count
    pieces = []
    for k in range(2):
        pick = ((i + k) % 2).astype(jnp.int32)[None]
        partial = pl.pallas_call(
            functools.partial(render_kernel, depth_cells, width_cells, groups),
            out_shape=jax.ShapeDtypeStruct((groups, 4, width_cells, lanes), f32),
            in_specs=[SMEM, SMEM, SMEM, VMEM],
            out_specs=VMEM,
            scratch_shapes=[
                pltpu.VMEM((2, depth_cells, width_cells, lanes), f32),
                pltpu.VMEM((2, depth_cells, width_cells, lanes), f32),
            ],
            compiler_params=GRANT,
            cost_estimate=cost(10),
            name="render",
        )(pick, tables, backward, vorticity)
        slabs = lax.all_to_all(partial, "depth", 0, 0, tiled=True)
        image = pl.pallas_call(
            functools.partial(composite_kernel, depth_count),
            out_shape=jax.ShapeDtypeStruct((4, width_cells, lanes), f32),
            in_specs=[SMEM, SMEM, VMEM],
            out_specs=VMEM,
            cost_estimate=cost(1),
            name="composite",
        )(2 * d.astype(jnp.int32)[None] + pick, backward, slabs)
        route = []
        for sd in range(depth_count):
            for si in range(image_count):
                route.append((sd * image_count + si, (si // 2) * image_count + 2 * sd + (si + k) % 2))
        pieces.append(lax.ppermute(image, ("depth", "image"), route))
    flip = (i % 2) == 1
    top = jnp.where(flip, pieces[1], pieces[0])
    bottom = jnp.where(flip, pieces[0], pieces[1])
    images = jnp.concatenate([top, bottom], axis=1)[None]
    return (
        final.reshape(populations.shape),
        vorticity.reshape(depth_cells, width_cells, lanes),
        images,
    )


def solution(mesh):
    in_specs = (P(None, "depth", "image", None), P("image", None, None), P("image"))
    out_specs = (
        P(None, "depth", "image", None),
        P("depth", "image", None),
        P("image", None, "depth", None),
    )
    return jax.shard_map(
        on_device, mesh=mesh, in_specs=in_specs, out_specs=out_specs, check_vma=False
    )
```

```python
import functools

import jax
import jax.numpy as jnp
import numpy as np
from jax import lax
from jax.experimental import pallas as pl
from jax.experimental.pallas import tpu as pltpu
from jax.sharding import PartitionSpec as P

VEL = (
    (0, 0, 0),
    (1, 0, 0), (-1, 0, 0), (0, 1, 0), (0, -1, 0), (0, 0, 1), (0, 0, -1),
    (1, 1, 0), (-1, -1, 0), (1, -1, 0), (-1, 1, 0),
    (1, 0, 1), (-1, 0, -1), (1, 0, -1), (-1, 0, 1),
    (0, 1, 1), (0, -1, -1), (0, 1, -1), (0, -1, 1),
)
WEIGHT = (1.0 / 3.0,) + (1.0 / 18.0,) * 6 + (1.0 / 36.0,) * 12
OMEGA = 1.25
Q = len(VEL)
STEPS = 4
HALO = STEPS + 1
AXIS_PAIRS = ((1, 2), (3, 4), (5, 6))
DIAG_PAIRS = ((7, 8), (9, 10), (11, 12), (13, 14), (15, 16), (17, 18))
SCALE = 8192.0

X_PAIRS = tuple(
    (a, b, 5) for a, b in zip((1, 7, 9, 11, 13), (2, 8, 10, 12, 14))
) + ((0, 3, 4), (4, 5, 4), (6, 15, 4), (16, 17, 4), (18, None, 4))


def low_rows(p):
    return 4 + VEL[p][0]


def face_list(nearest, step):
    sent = []
    for layer in range(1, HALO + 1):
        y = nearest + step * (layer - 1)
        for p in range(Q):
            inward = VEL[p][1] * (-step)
            if layer <= 4 + inward:
                sent.append((y, p))
    return sent


def momentum(f):
    s = {}
    d = {}
    for a, b in AXIS_PAIRS + DIAG_PAIRS:
        s[a] = f[a] + f[b]
        d[a] = f[a] - f[b]
    density = ((s[1] + s[3]) + (s[5] + s[7])) + ((s[9] + s[11]) + (s[13] + s[15])) + (s[17] + f[0])
    jx = (d[1] + d[7]) + (d[9] + d[11]) + d[13]
    jy = (d[3] + d[7]) - (d[9] - d[15]) + d[17]
    jz = (d[5] + d[11]) - (d[13] - d[15]) - d[17]
    return density, (jx, jy, jz), s, d


def collide(f):
    density, j, s, d = momentum(f)
    inverse = 1.0 / density
    u = [c * inverse for c in j]
    speed = j[0] * u[0] + j[1] * u[1] + j[2] * u[2]
    common = density - 1.5 * speed
    out = [None] * Q
    out[0] = (OMEGA * WEIGHT[0]) * common - (OMEGA - 1.0) * f[0]
    rest = 0.5 * (OMEGA - 1.0)
    for pairs, w in ((AXIS_PAIRS, WEIGHT[1]), (DIAG_PAIRS, WEIGHT[7])):
        base = (OMEGA * w) * common
        jw = [(3.0 * OMEGA * w) * c for c in j]
        uw = [1.5 * c for c in u]
        for a, b in pairs:
            project_j = None
            project_u = None
            for axis in range(3):
                c = VEL[a][axis]
                if c == 0:
                    continue
                if project_j is None:
                    assert c == 1
                    project_j, project_u = jw[axis], uw[axis]
                elif c > 0:
                    project_j, project_u = project_j + jw[axis], project_u + uw[axis]
                else:
                    project_j, project_u = project_j - jw[axis], project_u - uw[axis]
            even = (base + project_j * project_u) - rest * s[a]
            odd = project_j - rest * d[a]
            out[a] = even + odd
            out[b] = even - odd
    return out


def code(value, p):
    return jnp.round(value * (SCALE / WEIGHT[p]) - SCALE)


def decode(value, p):
    return value * (WEIGHT[p] / SCALE) + WEIGHT[p]


def row_index():
    return lax.broadcasted_iota(jnp.int32, (8, 128), 0)


def pack16(first, second):
    return jnp.concatenate([first, second], axis=0).astype(jnp.int32).astype(jnp.int16)


def wide(value):
    return value.astype(jnp.int32).astype(jnp.float32)


def first_kernel(
    depth_cells, width_cells, parity_ref, f_hbm, r_hbm, da_ref, db_ref, ia_ref, ib_ref, f_ref, r_ref, in_sems, out_sem
):
    tiles = depth_cells // 8
    rows = row_index()
    chunk = 8 * width_cells
    loads = [
        pltpu.make_async_copy(
            f_hbm.at[:, pl.ds(j * chunk, chunk)], f_ref.at[:, pl.ds(j * chunk, chunk)], in_sems.at[j]
        )
        for j in range(tiles)
    ]
    for load in loads:
        load.start()

    for j in range(tiles):
        loads[j].wait()

        def at_y(y, carry):
            f = [f_ref[p, pl.ds(j * chunk + y, 8, stride=width_cells), :] for p in range(Q)]
            out = collide(f)
            for p in range(Q):
                value = pltpu.roll(out[p], low_rows(p), 0)
                cz = VEL[p][2]
                r_ref[p, y, 8 * j : 8 * j + 8, :] = value if cz == 0 else pltpu.roll(value, cz % 128, 1)
            return carry

        lax.fori_loop(0, width_cells, at_y, 0, unroll=2)

    keep_r = pltpu.make_async_copy(r_ref, r_hbm, out_sem)
    keep_r.start()

    odd_depth = jnp.full((8, 128), parity_ref[0], jnp.int32) == 1
    odd_image = jnp.full((8, 128), parity_ref[1], jnp.int32) == 1

    def face_x(t, carry):
        for number, (a, b, n) in enumerate(X_PAIRS):
            low, high = [], []
            for k in range(2):
                y = 2 * t + k
                for sent, first_row in ((low, 0), (high, depth_cells - 8)):
                    piece = code(r_ref[a, y, first_row : first_row + 8, :], a)
                    if b is not None:
                        other = code(r_ref[b, y, first_row : first_row + 8, :], b)
                        other = pltpu.roll(other, n, 0)
                        keep = rows < n if sent is high else rows >= n
                        piece = jnp.where(keep, piece, other)
                    sent.append(piece)
            da = [jnp.where(odd_depth, l, h) for l, h in zip(low, high)]
            db = [jnp.where(odd_depth, h, l) for l, h in zip(low, high)]
            da_ref[number, t] = pack16(*da)
            db_ref[number, t] = pack16(*db)
        return carry

    lax.fori_loop(0, width_cells // 2, face_x, 0)

    low_face = face_list(0, 1)
    high_face = face_list(width_cells - 1, -1)
    for index, ((yl, pl_), (yh, ph)) in enumerate(zip(low_face, high_face)):
        for c in range(depth_cells // 16):
            a, b = [], []
            for k in range(2):
                first_row = 16 * c + 8 * k
                low = code(r_ref[pl_, yl, first_row : first_row + 8, :], pl_)
                high = code(r_ref[ph, yh, first_row : first_row + 8, :], ph)
                a.append(jnp.where(odd_image, low, high))
                b.append(jnp.where(odd_image, high, low))
            ia_ref[index, 16 * c : 16 * c + 16, :] = pack16(*a)
            ib_ref[index, 16 * c : 16 * c + 16, :] = pack16(*b)
    keep_r.wait()


def x_halo(low, high, n, second, rows):
    if second:
        low = pltpu.roll(low, 8 - n, 0)
        high = pltpu.roll(high, 8 - n, 0)
        n = 8 - n
    return jnp.where(rows < n, low, high)


X_PLACE = {}
for number_, (a_, b_, n_) in enumerate(X_PAIRS):
    X_PLACE[a_] = (number_, n_, False)
    if b_ is not None:
        X_PLACE[b_] = (number_, n_, True)


def corner_kernel(width_cells, parity_ref, xa_ref, xb_ref, h_ref, ca_ref, cb_ref):
    rows = row_index()
    odd_depth = jnp.full((8, 128), parity_ref[0], jnp.int32) == 1
    odd_image = jnp.full((8, 128), parity_ref[1], jnp.int32) == 1

    def halo(t, carry):
        for number, (a, b, n) in enumerate(X_PAIRS):
            va = wide(xa_ref[number, t])
            vb = wide(xb_ref[number, t])
            for k in range(2):
                pa, pb = va[8 * k : 8 * k + 8], vb[8 * k : 8 * k + 8]
                low = jnp.where(odd_depth, pa, pb)
                high = jnp.where(odd_depth, pb, pa)
                h_ref[a, 2 * t + k] = x_halo(low, high, n, False, rows)
                if b is not None:
                    h_ref[b, 2 * t + k] = x_halo(low, high, n, True, rows)
        return carry

    lax.fori_loop(0, width_cells // 2, halo, 0)
    low_face = face_list(0, 1)
    high_face = face_list(width_cells - 1, -1)
    for index in range(0, len(low_face), 2):
        a, b = [], []
        for (yl, pl_), (yh, ph) in zip(low_face[index : index + 2], high_face[index : index + 2]):
            low, high = h_ref[pl_, yl], h_ref[ph, yh]
            a.append(jnp.where(odd_image, low, high))
            b.append(jnp.where(odd_image, high, low))
        ca_ref[index // 2] = pack16(*a)
        cb_ref[index // 2] = pack16(*b)


PAD = 8


def put_streamed(target, p, y, pieces, halo, rows):
    n = low_rows(p)
    before = halo
    for t in range(len(pieces) + 1):
        here = pieces[t] if t < len(pieces) else halo
        target[p, y, PAD + 8 * t : PAD + 8 * t + 8, :] = jnp.where(rows < n, before, here)
        before = here


def step_row(source, target, y, wide_tiles, shift):
    for t in range(wide_tiles):
        first = PAD + 8 * t
        out = collide([source[p, y - VEL[p][1], first : first + 8, :] for p in range(Q)])
        for p in range(Q):
            cx, _, cz = VEL[p]
            value = out[p] if cz == 0 else pltpu.roll(out[p], cz % 128, 1)
            row = first + shift + cx
            target[p, y, row : row + 8, :] = value


BASE = PAD + 8


def flow_row(source, flow_ref, y, tiles):
    for t in range(-1, tiles + 1):
        first = BASE + 8 * t
        density, j, _, _ = momentum([source[p, y - VEL[p][1], first : first + 8, :] for p in range(Q)])
        inverse = 1.0 / density
        for axis in range(3):
            flow_ref[axis, y, first : first + 8, :] = j[axis] * inverse


def final_row(source, out_ref, y, origin, tiles, width_cells):
    for t in range(tiles):
        first = BASE + 8 * t
        for p in range(Q):
            out_ref[p, pl.ds(8 * t * width_cells + y - origin, 8, stride=width_cells), :] = source[
                p, y - VEL[p][1], first : first + 8, :
            ]


def inner_kernel(
    depth_cells, width_cells, r_ref, h_ref, final_ref, flow_ref, s2_hbm, s3_hbm, s4_hbm, sa_ref, sb_ref, sems
):
    tiles = depth_cells // 8
    rows = row_index()

    def own(y, carry):
        for p in range(Q):
            pieces = [r_ref[p, y, 8 * t : 8 * t + 8, :] for t in range(tiles)]
            put_streamed(sa_ref, p, y, pieces, decode(h_ref[p, y], p), rows)
        return carry

    lax.fori_loop(0, width_cells, own, 0)

    def hand_on(source, target, step):
        low, high = (step, width_cells - 2 - step)
        copies = [
            pltpu.make_async_copy(source.at[:, pl.ds(low, 2)], target.at[:, pl.ds(0, 2)], sems.at[step - 1, 0]),
            pltpu.make_async_copy(source.at[:, pl.ds(high, 2)], target.at[:, pl.ds(2, 2)], sems.at[step - 1, 1]),
        ]
        for copy in copies:
            copy.start()
        return copies

    def stage(source, target, step, shift):
        def pair(k, carry):
            step_row(source, target, step + 2 * k, tiles + 1, shift)
            step_row(source, target, step + 2 * k + 1, tiles + 1, shift)
            return carry

        lax.fori_loop(0, (width_cells - 2 * step) // 2, pair, 0)

    stage(sa_ref, sb_ref, 1, 0)
    kept2 = hand_on(sb_ref, s2_hbm, 1)
    stage(sb_ref, sa_ref, 2, 0)
    kept3 = hand_on(sa_ref, s3_hbm, 2)
    for copy in kept2:
        copy.wait()
    stage(sa_ref, sb_ref, 3, 4)
    kept4 = hand_on(sb_ref, s4_hbm, 3)

    def last(y, carry):
        flow_row(sb_ref, flow_ref, y, tiles)
        final_row(sb_ref, final_ref, y, 0, tiles, width_cells)
        return carry

    lax.fori_loop(STEPS, width_cells - STEPS, last, 0)
    for copy in kept3 + kept4:
        copy.wait()


def outer_kernel(
    depth_cells, width_cells, parity_ref, r_hbm, h_ref, ya_ref, yb_ref, ca_ref, cb_ref,
    final_in, flow_in, s2_in, s3_in, s4_in, out_hbm, vort_ref,
    r_ref, sa_ref, sb_ref, flow_ref, out_ref, plain_ref, sems,
):
    tiles = depth_cells // 8
    rows = row_index()
    odd_image = jnp.full((8, 128), parity_ref[1], jnp.int32) == 1

    moves = [
        (r_hbm.at[:, pl.ds(0, 2)], r_ref.at[:, pl.ds(0, 2)]),
        (r_hbm.at[:, pl.ds(width_cells - 2, 2)], r_ref.at[:, pl.ds(2, 2)]),
    ]
    for step, source, target in ((1, s2_in, sb_ref), (2, s3_in, sa_ref), (3, s4_in, sb_ref)):
        moves.append((source.at[:, pl.ds(0, 2)], target.at[:, pl.ds(HALO + step, 2)]))
        moves.append((source.at[:, pl.ds(2, 2)], target.at[:, pl.ds(HALO + width_cells - 2 - step, 2)]))
    inner = pl.ds(STEPS, width_cells - 2 * STEPS)
    moves.append((flow_in.at[:, inner], flow_ref.at[:, pl.ds(HALO + STEPS, width_cells - 2 * STEPS)]))
    moves.append((final_in, out_ref))
    copies = [pltpu.make_async_copy(a, b, sems.at[k]) for k, (a, b) in enumerate(moves)]
    for copy in copies:
        copy.start()

    low_face = face_list(0, 1)
    high_face = face_list(width_cells - 1, -1)
    for index in range(0, len(low_face), 2):
        corner_a, corner_b = wide(ca_ref[index // 2]), wide(cb_ref[index // 2])
        for k in range(2):
            (yl, pl_), (yh, ph) = low_face[index + k], high_face[index + k]
            ca, cb = corner_a[8 * k : 8 * k + 8], corner_b[8 * k : 8 * k + 8]
            low = [jnp.where(odd_image, ca, cb)]
            high = [jnp.where(odd_image, cb, ca)]
            for c in range(depth_cells // 16):
                ya = wide(ya_ref[index + k, 16 * c : 16 * c + 16, :])
                yb = wide(yb_ref[index + k, 16 * c : 16 * c + 16, :])
                for half in range(2):
                    a, b = ya[8 * half : 8 * half + 8], yb[8 * half : 8 * half + 8]
                    low.append(jnp.where(odd_image, a, b))
                    high.append(jnp.where(odd_image, b, a))
            low = [decode(v, ph) for v in low]
            high = [decode(v, pl_) for v in high]
            put_streamed(sa_ref, ph, yh - width_cells + HALO, low[1:], low[0], rows)
            put_streamed(sa_ref, pl_, yl + width_cells + HALO, high[1:], high[0], rows)

    copies[0].wait()
    copies[1].wait()
    for k, y in enumerate((0, 1, width_cells - 2, width_cells - 1)):
        for p in range(Q):
            pieces = [r_ref[p, k, 8 * t : 8 * t + 8, :] for t in range(tiles)]
            put_streamed(sa_ref, p, y + HALO, pieces, decode(h_ref[p, y], p), rows)

    def stage(source, target, step, shift):
        reach = HALO - step

        def both(k, carry):
            step_row(source, target, HALO - reach + k, tiles + 1, shift)
            step_row(source, target, HALO + width_cells - step + k, tiles + 1, shift)
            return carry

        lax.fori_loop(0, HALO, both, 0)

    stage(sa_ref, sb_ref, 1, 0)
    copies[2].wait()
    copies[3].wait()
    stage(sb_ref, sa_ref, 2, 0)
    copies[4].wait()
    copies[5].wait()
    stage(sa_ref, sb_ref, 3, 4)
    copies[6].wait()
    copies[7].wait()
    copies[9].wait()

    def finish(k, carry):
        final_row(sb_ref, out_ref, HALO + k, HALO, tiles, width_cells)
        final_row(sb_ref, out_ref, HALO + width_cells - STEPS + k, HALO, tiles, width_cells)
        return carry

    lax.fori_loop(0, STEPS, finish, 0)
    keep_out = pltpu.make_async_copy(out_ref, out_hbm, sems.at[10])
    keep_out.start()

    def flows(k, carry):
        flow_row(sb_ref, flow_ref, HALO - 1 + k, tiles)
        flow_row(sb_ref, flow_ref, HALO + width_cells - STEPS + k, tiles)
        return carry

    lax.fori_loop(0, HALO, flows, 0)
    copies[8].wait()

    def spin_at(y, carry):
        for t in range(tiles):
            first = BASE + 8 * t

            def dx(axis):
                return (flow_ref[axis, y, first + 1 : first + 9, :] - flow_ref[axis, y, first - 1 : first + 7, :]) * 0.5

            def dy(axis):
                return (flow_ref[axis, y + 1, first : first + 8, :] - flow_ref[axis, y - 1, first : first + 8, :]) * 0.5

            def dz(axis):
                value = flow_ref[axis, y, first : first + 8, :]
                return (pltpu.roll(value, 127, 1) - pltpu.roll(value, 1, 1)) * 0.5

            sx = dy(2) - dz(1)
            sy = dz(0) - dx(2)
            sz = dx(1) - dy(0)
            plain_ref[pl.ds(8 * t * width_cells + y - HALO, 8, stride=width_cells), :] = jnp.sqrt(
                sx * sx + sy * sy + sz * sz
            )
        return carry

    lax.fori_loop(HALO, HALO + width_cells, spin_at, 0, unroll=2)

    def rounded(x, carry):
        at = pl.ds(pl.multiple_of(x * 16, 16), 16)
        vort_ref[at, :] = plain_ref[at, :].astype(jnp.bfloat16)
        return carry

    lax.fori_loop(0, depth_cells * width_cells // 16, rounded, 0, unroll=4)
    keep_out.wait()


BUMP_WIDTH = 0.15
LEVEL_OFFSET = 0.05
STRETCH = float(np.sqrt(np.log2(np.e)) / BUMP_WIDTH)
CENTRE = 4.0
LOG2E = float(np.log2(np.e))


def bump_tables(transfer, ray_cells):
    b = STRETCH * transfer[:, 0] - CENTRE
    fade = jnp.exp2(-b * b)
    strength = transfer[:, 1:] * fade[:, None]
    strength = strength.at[:, 0].multiply(LOG2E / ray_cells)
    return jnp.concatenate([(2.0 * b)[:, None], strength], axis=1)


BLOCK = 4


def render_kernel(depth_cells, width_cells, groups, pick_ref, table_ref, backward_ref, vort_ref, image_ref, place_ref, fade_ref):
    bumps = table_ref.shape[1] // 5

    def prepare(x, carry):
        at = pl.ds(pl.multiple_of(x * width_cells, width_cells), width_cells)
        value = vort_ref[at, :].astype(jnp.float32)
        level = value / (value + LEVEL_OFFSET)
        place = STRETCH * level - CENTRE
        fade = jnp.exp2(-place * place)
        for order, to in ((0, x), (1, depth_cells - 1 - x)):
            place_ref[order, to] = place
            fade_ref[order, to] = fade
        return carry

    lax.fori_loop(0, depth_cells, prepare, 0)

    def one(number, carry):
        group = number // 2
        slot = number % 2
        m = 2 * group + (pick_ref[0] + slot) % 2
        order = backward_ref[m]

        def cells(block, state):
            clear, red, green, blue = state
            at = pl.ds(block * BLOCK, BLOCK)
            place = place_ref[order, at]
            total = [None] * 4
            for k in range(bumps):
                bump = jnp.exp2(place * table_ref[m, k])
                for c in range(4):
                    term = bump * table_ref[m, (1 + c) * bumps + k]
                    total[c] = term if total[c] is None else total[c] + term
            fade = fade_ref[order, at]
            passing = jnp.exp2(-(total[0] * fade))
            for b in range(BLOCK):
                behind = clear * passing[b]
                weight = (clear - behind) * fade[b]
                clear = behind
                red = red + weight * total[1][b]
                green = green + weight * total[2][b]
                blue = blue + weight * total[3][b]
            return clear, red, green, blue

        zero = jnp.zeros((width_cells, 128), jnp.float32)
        clear, red, green, blue = lax.fori_loop(0, depth_cells // BLOCK, cells, (zero + 1.0, zero, zero, zero))
        image_ref[group, slot, 0] = red
        image_ref[group, slot, 1] = green
        image_ref[group, slot, 2] = blue
        image_ref[group, slot, 3] = clear
        return carry

    lax.fori_loop(0, 2 * groups, one, 0)


def composite(slabs, backward):
    chooser = backward[:, :, None] == 1
    count = slabs.shape[0]
    clear = 1.0
    color = [0.0] * 3
    for step in range(count):
        piece = [jnp.where(chooser, slabs[count - 1 - step, :, c], slabs[step, :, c]) for c in range(4)]
        color = [color[c] + clear * piece[c] for c in range(3)]
        clear = clear * piece[3]
    return jnp.stack(color + [1.0 - clear], axis=1)


GATHER_ROWS = 128


def first_rows_kernel(in_ref, out_ref):
    for m in range(out_ref.shape[0]):
        out_ref[m : m + 1, :] = in_ref[m * GATHER_ROWS : m * GATHER_ROWS + 1, :]


ANY = pl.BlockSpec(memory_space=pl.ANY)
VMEM = pl.BlockSpec(memory_space=pltpu.VMEM)
SMEM = pl.BlockSpec(memory_space=pltpu.SMEM)
GRANT = pltpu.CompilerParams(vmem_limit_bytes=58 * 1024 * 1024)


def cost(microseconds):
    return pl.CostEstimate(flops=0, bytes_accessed=int(microseconds * 3.69e6), transcendentals=0)


def partner(index, count, phase):
    return index ^ 1 if phase == 0 else (((index + 1) ^ 1) - 1) % count


def swap(value, axis, count, phase):
    return lax.ppermute(value, axis, [(i, partner(i, count, phase)) for i in range(count)])


def on_device(populations, transfer, direction):
    _, depth_cells, width_cells, lanes = populations.shape
    depth_count, image_count = lax.axis_size("depth"), lax.axis_size("image")
    ray_cells = depth_cells * depth_count
    cells = depth_cells * width_cells
    f32, i16 = jnp.float32, jnp.int16
    d, i = lax.axis_index("depth"), lax.axis_index("image")
    parity = jnp.stack([d % 2, i % 2]).astype(jnp.int32)
    faces = len(face_list(0, 1))

    bumps = transfer.shape[2]
    row = jnp.concatenate([transfer.reshape(-1), direction.astype(f32)])
    row = jnp.pad(row[None], ((0, GATHER_ROWS - 1), (0, lanes - row.shape[0])))
    gathered = lax.all_gather(row, "image", axis=0, tiled=True)

    x_shape = jax.ShapeDtypeStruct((len(X_PAIRS), width_cells // 2, 16, lanes), i16)
    y_shape = jax.ShapeDtypeStruct((faces, depth_cells, lanes), i16)
    c_shape = jax.ShapeDtypeStruct((faces // 2, 16, lanes), i16)
    turned, da, db, ia, ib = pl.pallas_call(
        functools.partial(first_kernel, depth_cells, width_cells),
        out_shape=(
            jax.ShapeDtypeStruct((Q, width_cells, depth_cells, lanes), f32),
            x_shape, x_shape, y_shape, y_shape,
        ),
        in_specs=[SMEM, ANY],
        out_specs=(ANY,) + (VMEM,) * 4,
        scratch_shapes=[
            pltpu.VMEM((Q, cells, lanes), f32),
            pltpu.VMEM((Q, width_cells, depth_cells, lanes), f32),
            pltpu.SemaphoreType.DMA((depth_cells // 8,)),
            pltpu.SemaphoreType.DMA,
        ],
        compiler_params=GRANT,
        cost_estimate=cost(12),
        name="first",
    )(parity, populations.reshape(Q, cells, lanes))

    xa = swap(da, "depth", depth_count, 0)
    xb = swap(db, "depth", depth_count, 1)
    ya = swap(ia, "image", image_count, 0)
    yb = swap(ib, "image", image_count, 1)
    halo, ca, cb = pl.pallas_call(
        functools.partial(corner_kernel, width_cells),
        out_shape=(jax.ShapeDtypeStruct((Q, width_cells, 8, lanes), f32), c_shape, c_shape),
        in_specs=[SMEM, VMEM, VMEM],
        out_specs=(VMEM,) * 3,
        compiler_params=GRANT,
        cost_estimate=cost(2),
        name="corner",
    )(parity, xa, xb)
    sent_a, sent_b = ca, cb
    ca = swap(sent_a, "image", image_count, 0)
    cb = swap(sent_b, "image", image_count, 1)

    depth_rows = depth_cells + 8 + 2 * PAD
    width_rows = width_cells + 2 * HALO
    side = jax.ShapeDtypeStruct((Q, 4, depth_rows, lanes), f32)
    inner_final, inner_flow, s2, s3, s4 = pl.pallas_call(
        functools.partial(inner_kernel, depth_cells, width_cells),
        out_shape=(
            jax.ShapeDtypeStruct((Q, cells, lanes), f32),
            jax.ShapeDtypeStruct((3, width_cells, depth_rows, lanes), f32),
            side, side, side,
        ),
        in_specs=[VMEM, VMEM],
        out_specs=(VMEM, VMEM, ANY, ANY, ANY),
        scratch_shapes=[
            pltpu.VMEM((Q, width_cells, depth_rows, lanes), f32),
            pltpu.VMEM((Q, width_cells, depth_rows, lanes), f32),
            pltpu.SemaphoreType.DMA((3, 2)),
        ],
        compiler_params=GRANT,
        cost_estimate=cost(12),
        name="inner",
    )(turned, halo)
    final, vorticity = pl.pallas_call(
        functools.partial(outer_kernel, depth_cells, width_cells),
        out_shape=(
            jax.ShapeDtypeStruct((Q, cells, lanes), f32),
            jax.ShapeDtypeStruct((cells, lanes), jnp.bfloat16),
        ),
        in_specs=[SMEM, ANY] + [VMEM] * 5 + [ANY] * 5,
        out_specs=(ANY, VMEM),
        scratch_shapes=[
            pltpu.VMEM((Q, 4, depth_cells, lanes), f32),
            pltpu.VMEM((Q, width_rows, depth_rows, lanes), f32),
            pltpu.VMEM((Q, width_rows, depth_rows, lanes), f32),
            pltpu.VMEM((3, width_rows, depth_rows, lanes), f32),
            pltpu.VMEM((Q, cells, lanes), f32),
            pltpu.VMEM((cells, lanes), f32),
            pltpu.SemaphoreType.DMA((11,)),
        ],
        compiler_params=GRANT,
        cost_estimate=cost(12),
        name="outer",
    )(parity, turned, halo, ya, yb, ca, cb, inner_final, inner_flow, s2, s3, s4)

    tables = pl.pallas_call(
        first_rows_kernel,
        out_shape=jax.ShapeDtypeStruct((image_count, lanes), f32),
        in_specs=[VMEM],
        out_specs=VMEM,
        cost_estimate=cost(1),
        name="rows",
    )(gathered)
    backward = tables[:, 5 * bumps].astype(jnp.int32)
    tables = bump_tables(tables[:, : 5 * bumps].reshape(-1, 5, bumps), ray_cells).reshape(-1, 5 * bumps)
    groups = depth_count
    partial = pl.pallas_call(
        functools.partial(render_kernel, depth_cells, width_cells, groups),
        out_shape=jax.ShapeDtypeStruct((groups, 2, 4, width_cells, lanes), f32),
        in_specs=[SMEM, SMEM, SMEM, VMEM],
        out_specs=VMEM,
        scratch_shapes=[
            pltpu.VMEM((2, depth_cells, width_cells, lanes), f32),
            pltpu.VMEM((2, depth_cells, width_cells, lanes), f32),
        ],
        compiler_params=GRANT,
        cost_estimate=cost(18),
        name="render",
    )((i % 2).astype(jnp.int32)[None], tables, backward, vorticity)
    slabs = lax.all_to_all(partial, "depth", 0, 0, tiled=True)
    mine = jnp.stack([backward[2 * d + (i + k) % 2] for k in range(2)])
    image = composite(slabs, mine[:, None])
    pieces = []
    for k in range(2):
        route = []
        for sd in range(depth_count):
            for si in range(image_count):
                route.append((sd * image_count + si, (si // 2) * image_count + 2 * sd + (si + k) % 2))
        pieces.append(lax.ppermute(image[k], ("depth", "image"), route))
    flip = (i % 2) == 1
    top = jnp.where(flip, pieces[1], pieces[0])
    bottom = jnp.where(flip, pieces[0], pieces[1])
    images = jnp.concatenate([top, bottom], axis=1)[None]
    return (
        final.reshape(populations.shape),
        vorticity.reshape(depth_cells, width_cells, lanes),
        images,
    )


def solution(mesh):
    in_specs = (P(None, "depth", "image", None), P("image", None, None), P("image"))
    out_specs = (
        P(None, "depth", "image", None),
        P("depth", "image", None),
        P("image", None, "depth", None),
    )
    return jax.shard_map(
        on_device, mesh=mesh, in_specs=in_specs, out_specs=out_specs, check_vma=False
    )
```

```python
import functools

import jax
import jax.numpy as jnp
import numpy as np
from jax import lax
from jax.experimental import pallas as pl
from jax.experimental.pallas import tpu as pltpu
from jax.sharding import PartitionSpec as P

VEL = (
    (0, 0, 0),
    (1, 0, 0), (-1, 0, 0), (0, 1, 0), (0, -1, 0), (0, 0, 1), (0, 0, -1),
    (1, 1, 0), (-1, -1, 0), (1, -1, 0), (-1, 1, 0),
    (1, 0, 1), (-1, 0, -1), (1, 0, -1), (-1, 0, 1),
    (0, 1, 1), (0, -1, -1), (0, 1, -1), (0, -1, 1),
)
WEIGHT = (1.0 / 3.0,) + (1.0 / 18.0,) * 6 + (1.0 / 36.0,) * 12
OMEGA = 1.25
Q = len(VEL)
STEPS = 4
HALO = STEPS + 1
AXIS_PAIRS = ((1, 2), (3, 4), (5, 6))
DIAG_PAIRS = ((7, 8), (9, 10), (11, 12), (13, 14), (15, 16), (17, 18))
SCALE = 8192.0

X_PAIRS = tuple(
    (a, b, 5) for a, b in zip((1, 7, 9, 11, 13), (2, 8, 10, 12, 14))
) + ((3, 4, 4), (5, 6, 4), (15, 16, 4), (17, 18, 4), (0, None, 4))


def low_rows(p):
    return 4 + VEL[p][0]


def face_list(nearest, step):
    sent = []
    for layer in range(1, HALO + 1):
        y = nearest + step * (layer - 1)
        for p in range(Q):
            inward = VEL[p][1] * (-step)
            if layer <= 4 + inward:
                sent.append((y, p))
    return sent


def momentum(f):
    s = {}
    d = {}
    for a, b in AXIS_PAIRS + DIAG_PAIRS:
        s[a] = f[a] + f[b]
        d[a] = f[a] - f[b]
    density = ((s[1] + s[3]) + (s[5] + s[7])) + ((s[9] + s[11]) + (s[13] + s[15])) + (s[17] + f[0])
    jx = (d[1] + d[7]) + (d[9] + d[11]) + d[13]
    jy = (d[3] + d[7]) - (d[9] - d[15]) + d[17]
    jz = (d[5] + d[11]) - (d[13] - d[15]) - d[17]
    return density, (jx, jy, jz), s, d


def collide(f):
    density, j, s, d = momentum(f)
    inverse = 1.0 / density
    u = [c * inverse for c in j]
    speed = j[0] * u[0] + j[1] * u[1] + j[2] * u[2]
    common = density - 1.5 * speed
    out = [None] * Q
    out[0] = (OMEGA * WEIGHT[0]) * common - (OMEGA - 1.0) * f[0]
    rest = 0.5 * (OMEGA - 1.0)
    for pairs, w in ((AXIS_PAIRS, WEIGHT[1]), (DIAG_PAIRS, WEIGHT[7])):
        base = (OMEGA * w) * common
        jw = [(3.0 * OMEGA * w) * c for c in j]
        uw = [1.5 * c for c in u]
        for a, b in pairs:
            project_j = None
            project_u = None
            for axis in range(3):
                c = VEL[a][axis]
                if c == 0:
                    continue
                if project_j is None:
                    assert c == 1
                    project_j, project_u = jw[axis], uw[axis]
                elif c > 0:
                    project_j, project_u = project_j + jw[axis], project_u + uw[axis]
                else:
                    project_j, project_u = project_j - jw[axis], project_u - uw[axis]
            even = (base + project_j * project_u) - rest * s[a]
            odd = project_j - rest * d[a]
            out[a] = even + odd
            out[b] = even - odd
    return out


def code(value, p):
    return value * (SCALE / WEIGHT[p]) + (32768.5 - SCALE)


def decode(value, p):
    return value * (WEIGHT[p] / SCALE) + WEIGHT[p]


def row_index():
    return lax.broadcasted_iota(jnp.int32, (8, 128), 0)


def pack16(first, second):
    return jnp.concatenate([first, second], axis=0).astype(jnp.int32).astype(jnp.int16)


def pack_code(first, second):
    whole = jnp.concatenate([first, second], axis=0).astype(jnp.int32)
    return (whole - 32768).astype(jnp.int16)


def wide(value):
    return value.astype(jnp.int32).astype(jnp.float32)


def collide_chunk(f_ref, r_ref, from_row, to_row, width_cells):
    def at_y(y, carry):
        f = [f_ref[p, pl.ds(from_row + y, 8, stride=width_cells), :] for p in range(Q)]
        out = collide(f)
        for p in range(Q):
            value = pltpu.roll(out[p], low_rows(p), 0)
            cz = VEL[p][2]
            r_ref[p, y, to_row : to_row + 8, :] = value if cz == 0 else pltpu.roll(value, cz % 128, 1)
        return carry

    lax.fori_loop(0, width_cells, at_y, 0, unroll=2)


def edge_kernel(depth_cells, width_cells, parity_ref, f_hbm, r_hbm, da_ref, db_ref, f_ref, r_ref, in_sems, out_sem):
    rows = row_index()
    chunk = 8 * width_cells
    loads = []
    for k, j in enumerate((0, depth_cells // 8 - 1)):
        loads.append(
            pltpu.make_async_copy(
                f_hbm.at[:, pl.ds(j * chunk, chunk)], f_ref.at[:, pl.ds(k * chunk, chunk)], in_sems.at[k]
            )
        )
    for load in loads:
        load.start()
    for k, load in enumerate(loads):
        load.wait()
        collide_chunk(f_ref, r_ref, k * chunk, 8 * k, width_cells)
    keep_r = pltpu.make_async_copy(r_ref, r_hbm, out_sem)
    keep_r.start()

    odd_depth = jnp.full((8, 128), parity_ref[0], jnp.int32) == 1

    def face_x(t, carry):
        for number, (a, b, n) in enumerate(X_PAIRS):
            da, db = [], []
            for k in range(2):
                y = 2 * t + k
                low, high = (r_ref[a, y, first : first + 8, :] for first in (0, 8))
                if b is not None:
                    other_low, other_high = (
                        pltpu.roll(r_ref[b, y, first : first + 8, :], n, 0) for first in (0, 8)
                    )
                    low = jnp.where(rows >= n, low, other_low)
                    high = jnp.where(rows < n, high, other_high)
                low, high = code(low, a), code(high, a)
                da.append(jnp.where(odd_depth, low, high))
                db.append(jnp.where(odd_depth, high, low))
            da_ref[number, t] = pack_code(*da)
            db_ref[number, t] = pack_code(*db)
        return carry

    lax.fori_loop(0, width_cells // 2, face_x, 0)
    keep_r.wait()


def middle_kernel(
    depth_cells, width_cells, parity_ref, f_hbm, edge_hbm, r_hbm, ia_ref, ib_ref, f_ref, r_ref, edge_ref, in_sems, out_sem
):
    chunk = 8 * width_cells
    tiles = depth_cells // 8
    loads = []
    for j in range(1, tiles - 1):
        loads.append(
            pltpu.make_async_copy(
                f_hbm.at[:, pl.ds(j * chunk, chunk)], f_ref.at[:, pl.ds((j - 1) * chunk, chunk)], in_sems.at[j]
            )
        )
    for side in range(2):
        first = side * (width_cells - HALO)
        loads.append(
            pltpu.make_async_copy(
                edge_hbm.at[:, pl.ds(first, HALO)], edge_ref.at[:, pl.ds(side * HALO, HALO)],
                in_sems.at[side * (tiles - 1)],
            )
        )
    for load in loads:
        load.start()
    for j in range(tiles - 2):
        loads[j].wait()
        collide_chunk(f_ref, r_ref, j * chunk, 8 * j, width_cells)
    keep_r = pltpu.make_async_copy(r_ref, r_hbm, out_sem)
    keep_r.start()
    for load in loads[tiles - 2 :]:
        load.wait()

    odd_image = jnp.full((8, 128), parity_ref[1], jnp.int32) == 1

    def piece(p, y, t):
        if t in (0, tiles - 1):
            row = y if y < HALO else y - (width_cells - 2 * HALO)
            first = 0 if t == 0 else 8
            return edge_ref[p, row, first : first + 8, :]
        return r_ref[p, y, 8 * t - 8 : 8 * t, :]

    low_face = face_list(0, 1)
    high_face = face_list(width_cells - 1, -1)
    for index, ((yl, pl_), (yh, ph)) in enumerate(zip(low_face, high_face)):
        for c in range(tiles // 2):
            a, b = [], []
            for t in (2 * c, 2 * c + 1):
                low = code(piece(pl_, yl, t), pl_)
                high = code(piece(ph, yh, t), ph)
                a.append(jnp.where(odd_image, low, high))
                b.append(jnp.where(odd_image, high, low))
            ia_ref[index, 16 * c : 16 * c + 16, :] = pack_code(*a)
            ib_ref[index, 16 * c : 16 * c + 16, :] = pack_code(*b)
    keep_r.wait()


def x_halo(low, high, n, second, rows):
    if second:
        low = pltpu.roll(low, 8 - n, 0)
        high = pltpu.roll(high, 8 - n, 0)
        n = 8 - n
    return jnp.where(rows < n, low, high)


X_PLACE = {}
for number_, (a_, b_, n_) in enumerate(X_PAIRS):
    X_PLACE[a_] = (number_, n_, False)
    if b_ is not None:
        X_PLACE[b_] = (number_, n_, True)


def corner_kernel(width_cells, parity_ref, xa_ref, xb_ref, h_ref, ca_ref, cb_ref):
    rows = row_index()
    odd_depth = jnp.full((8, 128), parity_ref[0], jnp.int32) == 1
    odd_image = jnp.full((8, 128), parity_ref[1], jnp.int32) == 1

    def halo(t, carry):
        for number, (a, b, n) in enumerate(X_PAIRS):
            va = wide(xa_ref[number, t])
            vb = wide(xb_ref[number, t])
            for k in range(2):
                pa, pb = va[8 * k : 8 * k + 8], vb[8 * k : 8 * k + 8]
                low = jnp.where(odd_depth, pa, pb)
                high = jnp.where(odd_depth, pb, pa)
                h_ref[a, 2 * t + k] = x_halo(low, high, n, False, rows)
                if b is not None:
                    h_ref[b, 2 * t + k] = x_halo(low, high, n, True, rows)
        return carry

    lax.fori_loop(0, width_cells // 2, halo, 0)
    low_face = face_list(0, 1)
    high_face = face_list(width_cells - 1, -1)
    for index in range(0, len(low_face), 2):
        a, b = [], []
        for (yl, pl_), (yh, ph) in zip(low_face[index : index + 2], high_face[index : index + 2]):
            low, high = h_ref[pl_, yl], h_ref[ph, yh]
            a.append(jnp.where(odd_image, low, high))
            b.append(jnp.where(odd_image, high, low))
        ca_ref[index // 2] = pack16(*a)
        cb_ref[index // 2] = pack16(*b)


PAD = 8


def put_streamed(target, p, y, pieces, halo, rows):
    n = low_rows(p)
    before = halo
    for t in range(len(pieces) + 1):
        here = pieces[t] if t < len(pieces) else halo
        target[p, y, PAD + 8 * t : PAD + 8 * t + 8, :] = jnp.where(rows < n, before, here)
        before = here


def step_row(source, target, y, wide_tiles, shift):
    for t in range(wide_tiles):
        first = PAD + 8 * t
        out = collide([source[p, y - VEL[p][1], first : first + 8, :] for p in range(Q)])
        for p in range(Q):
            cx, _, cz = VEL[p]
            value = out[p] if cz == 0 else pltpu.roll(out[p], cz % 128, 1)
            row = first + shift + cx
            target[p, y, row : row + 8, :] = value


BASE = PAD + 8


def flow_row(source, flow_ref, y, tiles):
    for t in range(-1, tiles + 1):
        first = BASE + 8 * t
        density, j, _, _ = momentum([source[p, y - VEL[p][1], first : first + 8, :] for p in range(Q)])
        inverse = 1.0 / density
        for axis in range(3):
            flow_ref[axis, y, first : first + 8, :] = j[axis] * inverse


def final_row(source, out_ref, y, origin, tiles, width_cells):
    for t in range(tiles):
        first = BASE + 8 * t
        for p in range(Q):
            out_ref[p, pl.ds(8 * t * width_cells + y - origin, 8, stride=width_cells), :] = source[
                p, y - VEL[p][1], first : first + 8, :
            ]


def spin_row(flow_ref, out_ref, y, origin, tiles, width_cells):
    for t in range(tiles):
        first = BASE + 8 * t

        def dx(axis):
            return (flow_ref[axis, y, first + 1 : first + 9, :] - flow_ref[axis, y, first - 1 : first + 7, :]) * 0.5

        def dy(axis):
            return (flow_ref[axis, y + 1, first : first + 8, :] - flow_ref[axis, y - 1, first : first + 8, :]) * 0.5

        def dz(axis):
            value = flow_ref[axis, y, first : first + 8, :]
            return (pltpu.roll(value, 127, 1) - pltpu.roll(value, 1, 1)) * 0.5

        sx = dy(2) - dz(1)
        sy = dz(0) - dx(2)
        sz = dx(1) - dy(0)
        out_ref[pl.ds(8 * t * width_cells + y - origin, 8, stride=width_cells), :] = jnp.sqrt(
            sx * sx + sy * sy + sz * sz
        )


def inner_kernel(
    depth_cells, width_cells, e_ref, r_ref, h_ref, final_ref, flow_ref, spin_ref, s2_hbm, s3_hbm, s4_hbm, sa_ref, sb_ref, sems
):
    tiles = depth_cells // 8
    rows = row_index()

    def own(y, carry):
        for p in range(Q):
            pieces = [r_ref[p, y, 8 * t : 8 * t + 8, :] for t in range(tiles - 2)]
            pieces = [e_ref[p, y, 0:8, :]] + pieces + [e_ref[p, y, 8:16, :]]
            put_streamed(sa_ref, p, y, pieces, decode(h_ref[p, y], p), rows)
        return carry

    lax.fori_loop(0, width_cells, own, 0)

    def hand_on(source, target, step):
        low, high = (step, width_cells - 2 - step)
        copies = [
            pltpu.make_async_copy(source.at[:, pl.ds(low, 2)], target.at[:, pl.ds(0, 2)], sems.at[step - 1, 0]),
            pltpu.make_async_copy(source.at[:, pl.ds(high, 2)], target.at[:, pl.ds(2, 2)], sems.at[step - 1, 1]),
        ]
        for copy in copies:
            copy.start()
        return copies

    def stage(source, target, step, shift):
        def pair(k, carry):
            step_row(source, target, step + 2 * k, tiles + 1, shift)
            step_row(source, target, step + 2 * k + 1, tiles + 1, shift)
            return carry

        lax.fori_loop(0, (width_cells - 2 * step) // 2, pair, 0)

    stage(sa_ref, sb_ref, 1, 0)
    kept2 = hand_on(sb_ref, s2_hbm, 1)
    stage(sb_ref, sa_ref, 2, 0)
    kept3 = hand_on(sa_ref, s3_hbm, 2)
    for copy in kept2:
        copy.wait()
    stage(sa_ref, sb_ref, 3, 4)
    kept4 = hand_on(sb_ref, s4_hbm, 3)

    def last(y, carry):
        flow_row(sb_ref, flow_ref, y, tiles)
        final_row(sb_ref, final_ref, y, 0, tiles, width_cells)
        return carry

    lax.fori_loop(STEPS, width_cells - STEPS, last, 0)

    def spins(y, carry):
        spin_row(flow_ref, spin_ref, y, 0, tiles, width_cells)
        return carry

    lax.fori_loop(HALO, width_cells - HALO, spins, 0, unroll=2)
    for copy in kept3 + kept4:
        copy.wait()


def outer_kernel(
    depth_cells, width_cells, parity_ref, e_hbm, r_hbm, h_ref, ya_ref, yb_ref, ca_ref, cb_ref,
    final_in, flow_in, spin_in, s2_in, s3_in, s4_in, out_hbm, vort_ref,
    e_ref, r_ref, sa_ref, sb_ref, flow_ref, out_ref, plain_ref, sems,
):
    tiles = depth_cells // 8
    rows = row_index()
    odd_image = jnp.full((8, 128), parity_ref[1], jnp.int32) == 1

    moves = []
    for source, target in ((e_hbm, e_ref), (r_hbm, r_ref)):
        moves.append((source.at[:, pl.ds(0, 2)], target.at[:, pl.ds(0, 2)]))
        moves.append((source.at[:, pl.ds(width_cells - 2, 2)], target.at[:, pl.ds(2, 2)]))
    for step, source, target in ((1, s2_in, sb_ref), (2, s3_in, sa_ref), (3, s4_in, sb_ref)):
        moves.append((source.at[:, pl.ds(0, 2)], target.at[:, pl.ds(HALO + step, 2)]))
        moves.append((source.at[:, pl.ds(2, 2)], target.at[:, pl.ds(HALO + width_cells - 2 - step, 2)]))
    inner = pl.ds(STEPS, width_cells - 2 * STEPS)
    moves.append((flow_in.at[:, inner], flow_ref.at[:, pl.ds(HALO + STEPS, width_cells - 2 * STEPS)]))
    moves.append((final_in, out_ref))
    moves.append((spin_in, plain_ref))
    copies = [pltpu.make_async_copy(a, b, sems.at[k]) for k, (a, b) in enumerate(moves)]
    for copy in copies:
        copy.start()

    low_face = face_list(0, 1)
    high_face = face_list(width_cells - 1, -1)
    for index in range(0, len(low_face), 2):
        corner_a, corner_b = wide(ca_ref[index // 2]), wide(cb_ref[index // 2])
        for k in range(2):
            (yl, pl_), (yh, ph) = low_face[index + k], high_face[index + k]
            ca, cb = corner_a[8 * k : 8 * k + 8], corner_b[8 * k : 8 * k + 8]
            low = [jnp.where(odd_image, ca, cb)]
            high = [jnp.where(odd_image, cb, ca)]
            for c in range(depth_cells // 16):
                ya = wide(ya_ref[index + k, 16 * c : 16 * c + 16, :])
                yb = wide(yb_ref[index + k, 16 * c : 16 * c + 16, :])
                for half in range(2):
                    a, b = ya[8 * half : 8 * half + 8], yb[8 * half : 8 * half + 8]
                    low.append(jnp.where(odd_image, a, b))
                    high.append(jnp.where(odd_image, b, a))
            low = [decode(v, ph) for v in low]
            high = [decode(v, pl_) for v in high]
            put_streamed(sa_ref, ph, yh - width_cells + HALO, low[1:], low[0], rows)
            put_streamed(sa_ref, pl_, yl + width_cells + HALO, high[1:], high[0], rows)

    for copy in copies[:4]:
        copy.wait()
    for k, y in enumerate((0, 1, width_cells - 2, width_cells - 1)):
        for p in range(Q):
            pieces = [r_ref[p, k, 8 * t : 8 * t + 8, :] for t in range(tiles - 2)]
            pieces = [e_ref[p, k, 0:8, :]] + pieces + [e_ref[p, k, 8:16, :]]
            put_streamed(sa_ref, p, y + HALO, pieces, decode(h_ref[p, y], p), rows)

    def stage(source, target, step, shift):
        reach = HALO - step

        def both(k, carry):
            step_row(source, target, HALO - reach + k, tiles + 1, shift)
            step_row(source, target, HALO + width_cells - step + k, tiles + 1, shift)
            return carry

        lax.fori_loop(0, HALO, both, 0)

    stage(sa_ref, sb_ref, 1, 0)
    for copy in copies[4:6]:
        copy.wait()
    stage(sb_ref, sa_ref, 2, 0)
    for copy in copies[6:8]:
        copy.wait()
    stage(sa_ref, sb_ref, 3, 4)
    for copy in copies[8:13]:
        copy.wait()

    def finish(k, carry):
        final_row(sb_ref, out_ref, HALO + k, HALO, tiles, width_cells)
        final_row(sb_ref, out_ref, HALO + width_cells - STEPS + k, HALO, tiles, width_cells)
        return carry

    lax.fori_loop(0, STEPS, finish, 0)
    keep_out = pltpu.make_async_copy(out_ref, out_hbm, sems.at[13])
    keep_out.start()

    def flows(k, carry):
        flow_row(sb_ref, flow_ref, HALO - 1 + k, tiles)
        flow_row(sb_ref, flow_ref, HALO + width_cells - STEPS + k, tiles)
        return carry

    lax.fori_loop(0, HALO, flows, 0)

    def spins(k, carry):
        spin_row(flow_ref, plain_ref, HALO + k, HALO, tiles, width_cells)
        spin_row(flow_ref, plain_ref, width_cells + k, HALO, tiles, width_cells)
        return carry

    lax.fori_loop(0, HALO, spins, 0)

    def rounded(x, carry):
        at = pl.ds(pl.multiple_of(x * 16, 16), 16)
        vort_ref[at, :] = plain_ref[at, :].astype(jnp.bfloat16)
        return carry

    lax.fori_loop(0, depth_cells * width_cells // 16, rounded, 0, unroll=4)
    keep_out.wait()


BUMP_WIDTH = 0.15
LEVEL_OFFSET = 0.05
STRETCH = float(np.sqrt(np.log2(np.e)) / BUMP_WIDTH)
CENTRE = 4.0
LOG2E = float(np.log2(np.e))


def bump_tables(transfer, ray_cells):
    b = STRETCH * transfer[:, 0] - CENTRE
    fade = jnp.exp2(-b * b)
    strength = transfer[:, 1:] * fade[:, None]
    strength = strength.at[:, 0].multiply(LOG2E / ray_cells)
    return jnp.concatenate([(2.0 * b)[:, None], strength], axis=1)


BLOCK = 4


def render_kernel(depth_cells, width_cells, groups, bumps, pick_ref, table_ref, vort_ref, image_ref, place_ref, fade_ref):
    def prepare(x, carry):
        at = pl.ds(pl.multiple_of(x * width_cells, width_cells), width_cells)
        value = vort_ref[at, :].astype(jnp.float32)
        level = value / (value + LEVEL_OFFSET)
        place = STRETCH * level - CENTRE
        fade = jnp.exp2(-place * place)
        for order, to in ((0, x), (1, depth_cells - 1 - x)):
            place_ref[order, to] = place
            fade_ref[order, to] = fade
        return carry

    lax.fori_loop(0, depth_cells, prepare, 0)

    def one(number, carry):
        group = number // 2
        slot = number % 2
        m = 2 * group + (pick_ref[0] + slot) % 2
        order = jnp.where(table_ref[m, 0, 5 * bumps] > 0.5, 1, 0)

        def cells(block, state):
            clear, red, green, blue = state
            at = pl.ds(block * BLOCK, BLOCK)
            place = place_ref[order, at]
            total = [None] * 4
            for k in range(bumps):
                bump = jnp.exp2(place * table_ref[m, 0, k])
                for c in range(4):
                    term = bump * table_ref[m, 0, (1 + c) * bumps + k]
                    total[c] = term if total[c] is None else total[c] + term
            fade = fade_ref[order, at]
            passing = jnp.exp2(-(total[0] * fade))
            for b in range(BLOCK):
                behind = clear * passing[b]
                weight = (clear - behind) * fade[b]
                clear = behind
                red = red + weight * total[1][b]
                green = green + weight * total[2][b]
                blue = blue + weight * total[3][b]
            return clear, red, green, blue

        zero = jnp.zeros((width_cells, 128), jnp.float32)
        clear, red, green, blue = lax.fori_loop(0, depth_cells // BLOCK, cells, (zero + 1.0, zero, zero, zero))
        image_ref[group, slot, 0] = red
        image_ref[group, slot, 1] = green
        image_ref[group, slot, 2] = blue
        image_ref[group, slot, 3] = clear
        return carry

    lax.fori_loop(0, 2 * groups, one, 0)


def composite(slabs, backward):
    chooser = backward[:, :, None] > 0.5
    count = slabs.shape[0]
    clear = 1.0
    color = [0.0] * 3
    for step in range(count):
        piece = [jnp.where(chooser, slabs[count - 1 - step, :, c], slabs[step, :, c]) for c in range(4)]
        color = [color[c] + clear * piece[c] for c in range(3)]
        clear = clear * piece[3]
    return jnp.stack(color + [1.0 - clear], axis=1)


ANY = pl.BlockSpec(memory_space=pl.ANY)
VMEM = pl.BlockSpec(memory_space=pltpu.VMEM)
SMEM = pl.BlockSpec(memory_space=pltpu.SMEM)
GRANT = pltpu.CompilerParams(vmem_limit_bytes=58 * 1024 * 1024)


def cost(microseconds):
    return pl.CostEstimate(flops=0, bytes_accessed=int(microseconds * 3.69e6), transcendentals=0)


def partner(index, count, phase):
    return index ^ 1 if phase == 0 else (((index + 1) ^ 1) - 1) % count


def swap(value, axis, count, phase):
    return lax.ppermute(value, axis, [(i, partner(i, count, phase)) for i in range(count)])


def on_device(populations, transfer, direction):
    _, depth_cells, width_cells, lanes = populations.shape
    depth_count, image_count = lax.axis_size("depth"), lax.axis_size("image")
    ray_cells = depth_cells * depth_count
    cells = depth_cells * width_cells
    f32, i16 = jnp.float32, jnp.int16
    d, i = lax.axis_index("depth"), lax.axis_index("image")
    parity = jnp.stack([d % 2, i % 2]).astype(jnp.int32)
    faces = len(face_list(0, 1))

    x_shape = jax.ShapeDtypeStruct((len(X_PAIRS), width_cells // 2, 16, lanes), i16)
    y_shape = jax.ShapeDtypeStruct((faces, depth_cells, lanes), i16)
    c_shape = jax.ShapeDtypeStruct((faces // 2, 16, lanes), i16)
    half = (depth_cells - 16, 16)
    field = populations.reshape(Q, cells, lanes)
    edge, da, db = pl.pallas_call(
        functools.partial(edge_kernel, depth_cells, width_cells),
        out_shape=(jax.ShapeDtypeStruct((Q, width_cells, half[1], lanes), f32), x_shape, x_shape),
        in_specs=[SMEM, ANY],
        out_specs=(ANY, VMEM, VMEM),
        scratch_shapes=[
            pltpu.VMEM((Q, half[1] * width_cells, lanes), f32),
            pltpu.VMEM((Q, width_cells, half[1], lanes), f32),
            pltpu.SemaphoreType.DMA((2,)),
            pltpu.SemaphoreType.DMA,
        ],
        compiler_params=GRANT,
        cost_estimate=cost(6),
        name="edge",
    )(parity, field)
    middle, ia, ib = pl.pallas_call(
        functools.partial(middle_kernel, depth_cells, width_cells),
        out_shape=(jax.ShapeDtypeStruct((Q, width_cells, half[0], lanes), f32), y_shape, y_shape),
        in_specs=[SMEM, ANY, ANY],
        out_specs=(ANY, VMEM, VMEM),
        scratch_shapes=[
            pltpu.VMEM((Q, half[0] * width_cells, lanes), f32),
            pltpu.VMEM((Q, width_cells, half[0], lanes), f32),
            pltpu.VMEM((Q, 2 * HALO, half[1], lanes), f32),
            pltpu.SemaphoreType.DMA((depth_cells // 8,)),
            pltpu.SemaphoreType.DMA,
        ],
        compiler_params=GRANT,
        cost_estimate=cost(6),
        name="middle",
    )(parity, field, edge)

    xa = swap(da, "depth", depth_count, 0)
    xb = swap(db, "depth", depth_count, 1)
    ya = swap(ia, "image", image_count, 0)
    yb = swap(ib, "image", image_count, 1)
    halo, ca, cb = pl.pallas_call(
        functools.partial(corner_kernel, width_cells),
        out_shape=(jax.ShapeDtypeStruct((Q, width_cells, 8, lanes), f32), c_shape, c_shape),
        in_specs=[SMEM, VMEM, VMEM],
        out_specs=(VMEM,) * 3,
        compiler_params=GRANT,
        cost_estimate=cost(2),
        name="corner",
    )(parity, xa, xb)
    sent_a, sent_b = ca, cb
    ca = swap(sent_a, "image", image_count, 0)
    cb = swap(sent_b, "image", image_count, 1)

    depth_rows = depth_cells + 8 + 2 * PAD
    width_rows = width_cells + 2 * HALO
    side = jax.ShapeDtypeStruct((Q, 4, depth_rows, lanes), f32)
    inner_final, inner_flow, inner_spin, s2, s3, s4 = pl.pallas_call(
        functools.partial(inner_kernel, depth_cells, width_cells),
        out_shape=(
            jax.ShapeDtypeStruct((Q, cells, lanes), f32),
            jax.ShapeDtypeStruct((3, width_cells, depth_rows, lanes), f32),
            jax.ShapeDtypeStruct((cells, lanes), f32),
            side, side, side,
        ),
        in_specs=[VMEM] * 3,
        out_specs=(VMEM, VMEM, VMEM, ANY, ANY, ANY),
        scratch_shapes=[
            pltpu.VMEM((Q, width_cells, depth_rows, lanes), f32),
            pltpu.VMEM((Q, width_cells, depth_rows, lanes), f32),
            pltpu.SemaphoreType.DMA((3, 2)),
        ],
        compiler_params=GRANT,
        cost_estimate=cost(12),
        name="inner",
    )(edge, middle, halo)

    bumps = transfer.shape[2]
    row = jnp.concatenate([bump_tables(transfer, ray_cells).reshape(-1), direction.astype(f32)])
    row = jnp.pad(row, (0, lanes - row.shape[0]))
    row, _ = lax.optimization_barrier((row, inner_spin))
    tables = lax.all_to_all(
        jnp.broadcast_to(row, (image_count, 8, lanes)), "image", 0, 0, tiled=True
    )
    final, vorticity = pl.pallas_call(
        functools.partial(outer_kernel, depth_cells, width_cells),
        out_shape=(
            jax.ShapeDtypeStruct((Q, cells, lanes), f32),
            jax.ShapeDtypeStruct((cells, lanes), jnp.bfloat16),
        ),
        in_specs=[SMEM, ANY, ANY] + [VMEM] * 5 + [ANY] * 6,
        out_specs=(ANY, VMEM),
        scratch_shapes=[
            pltpu.VMEM((Q, 4, half[1], lanes), f32),
            pltpu.VMEM((Q, 4, half[0], lanes), f32),
            pltpu.VMEM((Q, width_rows, depth_rows, lanes), f32),
            pltpu.VMEM((Q, width_rows, depth_rows, lanes), f32),
            pltpu.VMEM((3, width_rows, depth_rows, lanes), f32),
            pltpu.VMEM((Q, cells, lanes), f32),
            pltpu.VMEM((cells, lanes), f32),
            pltpu.SemaphoreType.DMA((14,)),
        ],
        compiler_params=GRANT,
        cost_estimate=cost(12),
        name="outer",
    )(parity, edge, middle, halo, ya, yb, ca, cb, inner_final, inner_flow, inner_spin, s2, s3, s4)

    groups = depth_count
    partial = pl.pallas_call(
        functools.partial(render_kernel, depth_cells, width_cells, groups, bumps),
        out_shape=jax.ShapeDtypeStruct((groups, 2, 4, width_cells, lanes), f32),
        in_specs=[SMEM, SMEM, VMEM],
        out_specs=VMEM,
        scratch_shapes=[
            pltpu.VMEM((2, depth_cells, width_cells, lanes), f32),
            pltpu.VMEM((2, depth_cells, width_cells, lanes), f32),
        ],
        compiler_params=GRANT,
        cost_estimate=cost(18),
        name="render",
    )((i % 2).astype(jnp.int32)[None], tables, vorticity)
    slabs = lax.all_to_all(partial, "depth", 0, 0, tiled=True)
    mine = jnp.stack([tables[2 * d + (i + k) % 2, 0, 5 * bumps] for k in range(2)])
    image = composite(slabs, mine[:, None])
    pieces = []
    for k in range(2):
        route = []
        for sd in range(depth_count):
            for si in range(image_count):
                route.append((sd * image_count + si, (si // 2) * image_count + 2 * sd + (si + k) % 2))
        pieces.append(lax.ppermute(image[k], ("depth", "image"), route))
    flip = (i % 2) == 1
    top = jnp.where(flip, pieces[1], pieces[0])
    bottom = jnp.where(flip, pieces[0], pieces[1])
    images = jnp.concatenate([top, bottom], axis=1)[None]
    return (
        final.reshape(populations.shape),
        vorticity.reshape(depth_cells, width_cells, lanes),
        images,
    )


def solution(mesh):
    in_specs = (P(None, "depth", "image", None), P("image", None, None), P("image"))
    out_specs = (
        P(None, "depth", "image", None),
        P("depth", "image", None),
        P("image", None, "depth", None),
    )
    return jax.shard_map(
        on_device, mesh=mesh, in_specs=in_specs, out_specs=out_specs, check_vma=False
    )
```

```python
import functools

import jax
import jax.numpy as jnp
import numpy as np
from jax import lax
from jax.experimental import pallas as pl
from jax.experimental.pallas import tpu as pltpu
from jax.sharding import PartitionSpec as P

VEL = (
    (0, 0, 0),
    (1, 0, 0), (-1, 0, 0), (0, 1, 0), (0, -1, 0), (0, 0, 1), (0, 0, -1),
    (1, 1, 0), (-1, -1, 0), (1, -1, 0), (-1, 1, 0),
    (1, 0, 1), (-1, 0, -1), (1, 0, -1), (-1, 0, 1),
    (0, 1, 1), (0, -1, -1), (0, 1, -1), (0, -1, 1),
)
WEIGHT = (1.0 / 3.0,) + (1.0 / 18.0,) * 6 + (1.0 / 36.0,) * 12
OMEGA = 1.25
Q = len(VEL)
STEPS = 4
HALO = STEPS + 1
AXIS_PAIRS = ((1, 2), (3, 4), (5, 6))
DIAG_PAIRS = ((7, 8), (9, 10), (11, 12), (13, 14), (15, 16), (17, 18))
SCALE = 8192.0

X_PAIRS = tuple(
    (a, b, 5) for a, b in zip((1, 7, 9, 11, 13), (2, 8, 10, 12, 14))
) + ((3, 4, 4), (5, 6, 4), (15, 16, 4), (17, 18, 4), (0, None, 4))


def low_rows(p):
    return 4 + VEL[p][0]


def face_list(nearest, step):
    sent = []
    for layer in range(1, HALO + 1):
        y = nearest + step * (layer - 1)
        for p in range(Q):
            inward = VEL[p][1] * (-step)
            if layer <= 4 + inward:
                sent.append((y, p))
    return sent


def momentum(f):
    s = {}
    d = {}
    for a, b in AXIS_PAIRS + DIAG_PAIRS:
        s[a] = f[a] + f[b]
        d[a] = f[a] - f[b]
    density = ((s[1] + s[3]) + (s[5] + s[7])) + ((s[9] + s[11]) + (s[13] + s[15])) + (s[17] + f[0])
    jx = (d[1] + d[7]) + (d[9] + d[11]) + d[13]
    jy = (d[3] + d[7]) - (d[9] - d[15]) + d[17]
    jz = (d[5] + d[11]) - (d[13] - d[15]) - d[17]
    return density, (jx, jy, jz), s, d


def collide(f):
    density, j, s, d = momentum(f)
    inverse = 1.0 / density
    u = [c * inverse for c in j]
    speed = j[0] * u[0] + j[1] * u[1] + j[2] * u[2]
    common = density - 1.5 * speed
    out = [None] * Q
    out[0] = (OMEGA * WEIGHT[0]) * common - (OMEGA - 1.0) * f[0]
    rest = 0.5 * (OMEGA - 1.0)
    for pairs, w in ((AXIS_PAIRS, WEIGHT[1]), (DIAG_PAIRS, WEIGHT[7])):
        base = (OMEGA * w) * common
        jw = [(3.0 * OMEGA * w) * c for c in j]
        uw = [1.5 * c for c in u]
        for a, b in pairs:
            project_j = None
            project_u = None
            for axis in range(3):
                c = VEL[a][axis]
                if c == 0:
                    continue
                if project_j is None:
                    assert c == 1
                    project_j, project_u = jw[axis], uw[axis]
                elif c > 0:
                    project_j, project_u = project_j + jw[axis], project_u + uw[axis]
                else:
                    project_j, project_u = project_j - jw[axis], project_u - uw[axis]
            even = (base + project_j * project_u) - rest * s[a]
            odd = project_j - rest * d[a]
            out[a] = even + odd
            out[b] = even - odd
    return out


def code(value, p):
    return value * (SCALE / WEIGHT[p]) + (32768.5 - SCALE)


def decode(value, p):
    return value * (WEIGHT[p] / SCALE) + WEIGHT[p]


def row_index():
    return lax.broadcasted_iota(jnp.int32, (8, 128), 0)


def pack16(first, second):
    return jnp.concatenate([first, second], axis=0).astype(jnp.int32).astype(jnp.int16)


def pack_code(first, second):
    whole = jnp.concatenate([first, second], axis=0).astype(jnp.int32)
    return (whole - 32768).astype(jnp.int16)


def wide(value):
    return value.astype(jnp.int32).astype(jnp.float32)


def collide_chunk(f_ref, r_ref, from_row, to_row, width_cells):
    def at_y(y, carry):
        f = [f_ref[p, pl.ds(from_row + y, 8, stride=width_cells), :] for p in range(Q)]
        out = collide(f)
        for p in range(Q):
            value = pltpu.roll(out[p], low_rows(p), 0)
            cz = VEL[p][2]
            r_ref[p, y, to_row : to_row + 8, :] = value if cz == 0 else pltpu.roll(value, cz % 128, 1)
        return carry

    lax.fori_loop(0, width_cells, at_y, 0, unroll=8)


def edge_kernel(depth_cells, width_cells, parity_ref, f_hbm, r_hbm, da_ref, db_ref, f_ref, r_ref, in_sems, out_sem):
    rows = row_index()
    chunk = 8 * width_cells
    loads = []
    for k, j in enumerate((0, depth_cells // 8 - 1)):
        loads.append(
            pltpu.make_async_copy(
                f_hbm.at[:, pl.ds(j * chunk, chunk)], f_ref.at[:, pl.ds(k * chunk, chunk)], in_sems.at[k]
            )
        )
    for load in loads:
        load.start()
    for k, load in enumerate(loads):
        load.wait()
        collide_chunk(f_ref, r_ref, k * chunk, 8 * k, width_cells)
    keep_r = pltpu.make_async_copy(r_ref, r_hbm, out_sem)
    keep_r.start()

    odd_depth = jnp.full((8, 128), parity_ref[0], jnp.int32) == 1

    def face_x(t, carry):
        for number, (a, b, n) in enumerate(X_PAIRS):
            da, db = [], []
            for k in range(2):
                y = 2 * t + k
                low, high = (r_ref[a, y, first : first + 8, :] for first in (0, 8))
                if b is not None:
                    other_low, other_high = (
                        pltpu.roll(r_ref[b, y, first : first + 8, :], n, 0) for first in (0, 8)
                    )
                    low = jnp.where(rows >= n, low, other_low)
                    high = jnp.where(rows < n, high, other_high)
                low, high = code(low, a), code(high, a)
                da.append(jnp.where(odd_depth, low, high))
                db.append(jnp.where(odd_depth, high, low))
            da_ref[number, t] = pack_code(*da)
            db_ref[number, t] = pack_code(*db)
        return carry

    lax.fori_loop(0, width_cells // 2, face_x, 0, unroll=2)
    keep_r.wait()


def middle_kernel(
    depth_cells, width_cells, parity_ref, f_hbm, edge_hbm, r_hbm, ia_ref, ib_ref, f_ref, r_ref, edge_ref, in_sems, out_sem
):
    chunk = 8 * width_cells
    tiles = depth_cells // 8
    loads = []
    for j in range(1, tiles - 1):
        loads.append(
            pltpu.make_async_copy(
                f_hbm.at[:, pl.ds(j * chunk, chunk)], f_ref.at[:, pl.ds((j - 1) * chunk, chunk)], in_sems.at[j]
            )
        )
    for side in range(2):
        first = side * (width_cells - HALO)
        loads.append(
            pltpu.make_async_copy(
                edge_hbm.at[:, pl.ds(first, HALO)], edge_ref.at[:, pl.ds(side * HALO, HALO)],
                in_sems.at[side * (tiles - 1)],
            )
        )
    for load in loads:
        load.start()
    for j in range(tiles - 2):
        loads[j].wait()
        collide_chunk(f_ref, r_ref, j * chunk, 8 * j, width_cells)
    keep_r = pltpu.make_async_copy(r_ref, r_hbm, out_sem)
    keep_r.start()
    for load in loads[tiles - 2 :]:
        load.wait()

    odd_image = jnp.full((8, 128), parity_ref[1], jnp.int32) == 1

    def piece(p, y, t):
        if t in (0, tiles - 1):
            row = y if y < HALO else y - (width_cells - 2 * HALO)
            first = 0 if t == 0 else 8
            return edge_ref[p, row, first : first + 8, :]
        return r_ref[p, y, 8 * t - 8 : 8 * t, :]

    low_face = face_list(0, 1)
    high_face = face_list(width_cells - 1, -1)
    for index, ((yl, pl_), (yh, ph)) in enumerate(zip(low_face, high_face)):
        for c in range(tiles // 2):
            a, b = [], []
            for t in (2 * c, 2 * c + 1):
                low = code(piece(pl_, yl, t), pl_)
                high = code(piece(ph, yh, t), ph)
                a.append(jnp.where(odd_image, low, high))
                b.append(jnp.where(odd_image, high, low))
            ia_ref[index, 16 * c : 16 * c + 16, :] = pack_code(*a)
            ib_ref[index, 16 * c : 16 * c + 16, :] = pack_code(*b)
    keep_r.wait()


def x_halo(low, high, n, second, rows):
    if second:
        low = pltpu.roll(low, 8 - n, 0)
        high = pltpu.roll(high, 8 - n, 0)
        n = 8 - n
    return jnp.where(rows < n, low, high)


X_PLACE = {}
for number_, (a_, b_, n_) in enumerate(X_PAIRS):
    X_PLACE[a_] = (number_, n_, False)
    if b_ is not None:
        X_PLACE[b_] = (number_, n_, True)


def corner_kernel(width_cells, parity_ref, xa_ref, xb_ref, h_ref, ca_ref, cb_ref):
    rows = row_index()
    odd_depth = jnp.full((8, 128), parity_ref[0], jnp.int32) == 1
    odd_image = jnp.full((8, 128), parity_ref[1], jnp.int32) == 1

    def halo(t, carry):
        for number, (a, b, n) in enumerate(X_PAIRS):
            va = wide(xa_ref[number, t])
            vb = wide(xb_ref[number, t])
            for k in range(2):
                pa, pb = va[8 * k : 8 * k + 8], vb[8 * k : 8 * k + 8]
                low = jnp.where(odd_depth, pa, pb)
                high = jnp.where(odd_depth, pb, pa)
                h_ref[a, 2 * t + k] = x_halo(low, high, n, False, rows)
                if b is not None:
                    h_ref[b, 2 * t + k] = x_halo(low, high, n, True, rows)
        return carry

    lax.fori_loop(0, width_cells // 2, halo, 0)
    low_face = face_list(0, 1)
    high_face = face_list(width_cells - 1, -1)
    for index in range(0, len(low_face), 2):
        a, b = [], []
        for (yl, pl_), (yh, ph) in zip(low_face[index : index + 2], high_face[index : index + 2]):
            low, high = h_ref[pl_, yl], h_ref[ph, yh]
            a.append(jnp.where(odd_image, low, high))
            b.append(jnp.where(odd_image, high, low))
        ca_ref[index // 2] = pack16(*a)
        cb_ref[index // 2] = pack16(*b)


PAD = 8


def put_streamed(target, p, y, pieces, halo, rows):
    n = low_rows(p)
    before = halo
    for t in range(len(pieces) + 1):
        here = pieces[t] if t < len(pieces) else halo
        target[p, y, PAD + 8 * t : PAD + 8 * t + 8, :] = jnp.where(rows < n, before, here)
        before = here


def step_row(source, target, y, wide_tiles, shift):
    for t in range(wide_tiles):
        first = PAD + 8 * t
        out = collide([source[p, y - VEL[p][1], first : first + 8, :] for p in range(Q)])
        for p in range(Q):
            cx, _, cz = VEL[p]
            value = out[p] if cz == 0 else pltpu.roll(out[p], cz % 128, 1)
            row = first + shift + cx
            target[p, y, row : row + 8, :] = value


BASE = PAD + 8


def flow_row(source, flow_ref, y, tiles):
    for t in range(-1, tiles + 1):
        first = BASE + 8 * t
        density, j, _, _ = momentum([source[p, y - VEL[p][1], first : first + 8, :] for p in range(Q)])
        inverse = 1.0 / density
        for axis in range(3):
            flow_ref[axis, y, first : first + 8, :] = j[axis] * inverse


def final_row(source, out_ref, y, origin, tiles, width_cells):
    for t in range(tiles):
        first = BASE + 8 * t
        for p in range(Q):
            out_ref[p, pl.ds(8 * t * width_cells + y - origin, 8, stride=width_cells), :] = source[
                p, y - VEL[p][1], first : first + 8, :
            ]


def spin_row(flow_ref, out_ref, y, origin, tiles, width_cells):
    for t in range(tiles):
        first = BASE + 8 * t

        def dx(axis):
            return (flow_ref[axis, y, first + 1 : first + 9, :] - flow_ref[axis, y, first - 1 : first + 7, :]) * 0.5

        def dy(axis):
            return (flow_ref[axis, y + 1, first : first + 8, :] - flow_ref[axis, y - 1, first : first + 8, :]) * 0.5

        def dz(axis):
            value = flow_ref[axis, y, first : first + 8, :]
            return (pltpu.roll(value, 127, 1) - pltpu.roll(value, 1, 1)) * 0.5

        sx = dy(2) - dz(1)
        sy = dz(0) - dx(2)
        sz = dx(1) - dy(0)
        out_ref[pl.ds(8 * t * width_cells + y - origin, 8, stride=width_cells), :] = jnp.sqrt(
            sx * sx + sy * sy + sz * sz
        )


def inner_kernel(
    depth_cells, width_cells, e_hbm, r_hbm, h_ref, sa_ref, sb_ref, final_ref, flow_ref, plain_ref, e_ref, r_ref, sems
):
    tiles = depth_cells // 8
    rows = row_index()

    def own(y, carry):
        for p in range(Q):
            pieces = [r_ref[p, y, 8 * t : 8 * t + 8, :] for t in range(tiles - 2)]
            pieces = [e_ref[p, y, 0:8, :]] + pieces + [e_ref[p, y, 8:16, :]]
            put_streamed(sa_ref, p, y + HALO, pieces, decode(h_ref[p, y], p), rows)
        return carry

    parts = 4
    count = width_cells // parts
    loads = []
    for part in range(parts):
        at = pl.ds(part * count, count)
        loads.append(
            [
                pltpu.make_async_copy(e_hbm.at[:, at], e_ref.at[:, at], sems.at[part, 0]),
                pltpu.make_async_copy(r_hbm.at[:, at], r_ref.at[:, at], sems.at[part, 1]),
            ]
        )
        for load in loads[-1]:
            load.start()
    for part in range(parts):
        for load in loads[part]:
            load.wait()
        lax.fori_loop(part * count, (part + 1) * count, own, 0)

    def stage(source, target, step, shift):
        def pair(k, carry):
            step_row(source, target, HALO + step + 2 * k, tiles + 1, shift)
            step_row(source, target, HALO + step + 2 * k + 1, tiles + 1, shift)
            return carry

        lax.fori_loop(0, (width_cells - 2 * step) // 2, pair, 0)

    stage(sa_ref, sb_ref, 1, 0)
    stage(sb_ref, sa_ref, 2, 0)
    stage(sa_ref, sb_ref, 3, 4)

    def last(y, carry):
        flow_row(sb_ref, flow_ref, y, tiles)
        final_row(sb_ref, final_ref, y, HALO, tiles, width_cells)
        return carry

    lax.fori_loop(HALO + STEPS, HALO + width_cells - STEPS, last, 0, unroll=2)

    def spins(y, carry):
        spin_row(flow_ref, plain_ref, y, HALO, tiles, width_cells)
        return carry

    lax.fori_loop(2 * HALO, width_cells, spins, 0, unroll=2)


def outer_kernel(
    depth_cells, width_cells, parity_ref, ya_ref, yb_ref, ca_ref, cb_ref,
    sa_in, sb_in, final_in, flow_in, plain_in,
    out_hbm, vort_ref, sa_ref, sb_ref, out_ref, flow_ref, plain_ref, out_sem,
):
    tiles = depth_cells // 8
    rows = row_index()
    odd_image = jnp.full((8, 128), parity_ref[1], jnp.int32) == 1

    low_face = face_list(0, 1)
    high_face = face_list(width_cells - 1, -1)
    for index in range(0, len(low_face), 2):
        corner_a, corner_b = wide(ca_ref[index // 2]), wide(cb_ref[index // 2])
        for k in range(2):
            (yl, pl_), (yh, ph) = low_face[index + k], high_face[index + k]
            ca, cb = corner_a[8 * k : 8 * k + 8], corner_b[8 * k : 8 * k + 8]
            low = [jnp.where(odd_image, ca, cb)]
            high = [jnp.where(odd_image, cb, ca)]
            for c in range(depth_cells // 16):
                ya = wide(ya_ref[index + k, 16 * c : 16 * c + 16, :])
                yb = wide(yb_ref[index + k, 16 * c : 16 * c + 16, :])
                for half in range(2):
                    a, b = ya[8 * half : 8 * half + 8], yb[8 * half : 8 * half + 8]
                    low.append(jnp.where(odd_image, a, b))
                    high.append(jnp.where(odd_image, b, a))
            low = [decode(v, ph) for v in low]
            high = [decode(v, pl_) for v in high]
            put_streamed(sa_ref, ph, yh - width_cells + HALO, low[1:], low[0], rows)
            put_streamed(sa_ref, pl_, yl + width_cells + HALO, high[1:], high[0], rows)

    def stage(source, target, step, shift):
        reach = HALO - step

        def both(k, carry):
            step_row(source, target, HALO - reach + k, tiles + 1, shift)
            step_row(source, target, HALO + width_cells - step + k, tiles + 1, shift)
            return carry

        lax.fori_loop(0, HALO, both, 0)

    stage(sa_ref, sb_ref, 1, 0)
    stage(sb_ref, sa_ref, 2, 0)
    stage(sa_ref, sb_ref, 3, 4)

    def finish(k, carry):
        final_row(sb_ref, out_ref, HALO + k, HALO, tiles, width_cells)
        final_row(sb_ref, out_ref, HALO + width_cells - STEPS + k, HALO, tiles, width_cells)
        return carry

    lax.fori_loop(0, STEPS, finish, 0)
    keep_out = pltpu.make_async_copy(out_ref, out_hbm, out_sem)
    keep_out.start()

    def flows(k, carry):
        flow_row(sb_ref, flow_ref, HALO - 1 + k, tiles)
        flow_row(sb_ref, flow_ref, HALO + width_cells - STEPS + k, tiles)
        return carry

    lax.fori_loop(0, HALO, flows, 0)

    def spins(k, carry):
        spin_row(flow_ref, plain_ref, HALO + k, HALO, tiles, width_cells)
        spin_row(flow_ref, plain_ref, width_cells + k, HALO, tiles, width_cells)
        return carry

    lax.fori_loop(0, HALO, spins, 0)

    def rounded(x, carry):
        at = pl.ds(pl.multiple_of(x * 16, 16), 16)
        vort_ref[at, :] = plain_ref[at, :].astype(jnp.bfloat16)
        return carry

    lax.fori_loop(0, depth_cells * width_cells // 16, rounded, 0, unroll=4)
    keep_out.wait()


BUMP_WIDTH = 0.15
LEVEL_OFFSET = 0.05
STRETCH = float(np.sqrt(np.log2(np.e)) / BUMP_WIDTH)
CENTRE = 4.0
LOG2E = float(np.log2(np.e))


def bump_tables(transfer, ray_cells):
    b = STRETCH * transfer[:, 0] - CENTRE
    fade = jnp.exp2(-b * b)
    strength = transfer[:, 1:] * fade[:, None]
    strength = strength.at[:, 0].multiply(LOG2E / ray_cells)
    return jnp.concatenate([(2.0 * b)[:, None], strength], axis=1)


BLOCK = 4


def render_kernel(depth_cells, width_cells, functions, bumps, table_ref, vort_ref, image_ref, place_ref, fade_ref):
    def prepare(x, carry):
        at = pl.ds(pl.multiple_of(x * width_cells, width_cells), width_cells)
        value = vort_ref[at, :].astype(jnp.float32)
        level = value / (value + LEVEL_OFFSET)
        place = STRETCH * level - CENTRE
        fade = jnp.exp2(-place * place)
        for order, to in ((0, x), (1, depth_cells - 1 - x)):
            place_ref[order, to] = place
            fade_ref[order, to] = fade
        return carry

    lax.fori_loop(0, depth_cells, prepare, 0)

    def one(m, carry):
        order = jnp.where(table_ref[m, 0, 5 * bumps] > 0.5, 1, 0)

        def cells(block, state):
            clear, red, green, blue = state
            at = pl.ds(block * BLOCK, BLOCK)
            place = place_ref[order, at]
            total = [None] * 4
            for k in range(bumps):
                bump = jnp.exp2(place * table_ref[m, 0, k])
                for c in range(4):
                    term = bump * table_ref[m, 0, (1 + c) * bumps + k]
                    total[c] = term if total[c] is None else total[c] + term
            fade = fade_ref[order, at]
            passing = jnp.exp2(-(total[0] * fade))
            for b in range(BLOCK):
                behind = clear * passing[b]
                weight = (clear - behind) * fade[b]
                clear = behind
                red = red + weight * total[1][b]
                green = green + weight * total[2][b]
                blue = blue + weight * total[3][b]
            return clear, red, green, blue

        zero = jnp.zeros((width_cells, 128), jnp.float32)
        clear, red, green, blue = lax.fori_loop(0, depth_cells // BLOCK, cells, (zero + 1.0, zero, zero, zero))
        image_ref[m, 0] = red
        image_ref[m, 1] = green
        image_ref[m, 2] = blue
        image_ref[m, 3] = clear
        return carry

    lax.fori_loop(0, functions, one, 0)


def composite(slabs, backward):
    count = slabs.shape[0]
    clear = 1.0
    color = [0.0] * 3
    for step in range(count):
        piece = [jnp.where(backward, slabs[count - 1 - step, :, c], slabs[step, :, c]) for c in range(4)]
        color = [color[c] + clear * piece[c] for c in range(3)]
        clear = clear * piece[3]
    return jnp.stack(color + [1.0 - clear])


HBM = pl.BlockSpec(memory_space=pltpu.HBM)
VMEM = pl.BlockSpec(memory_space=pltpu.VMEM)
SMEM = pl.BlockSpec(memory_space=pltpu.SMEM)
GRANT = pltpu.CompilerParams(vmem_limit_bytes=14 * 1024 * 1024)


def cost(microseconds):
    return pl.CostEstimate(flops=0, bytes_accessed=int(microseconds * 3.69e6), transcendentals=0)


def in_hbm(value):
    return pltpu.with_memory_space_constraint(value, pltpu.HBM)


def partner(index, count, phase):
    return index ^ 1 if phase == 0 else (((index + 1) ^ 1) - 1) % count


def swap(value, axis, count, phase):
    return lax.ppermute(value, axis, [(i, partner(i, count, phase)) for i in range(count)])


def on_device(populations, transfer, direction):
    _, depth_cells, width_cells, lanes = populations.shape
    depth_count, image_count = lax.axis_size("depth"), lax.axis_size("image")
    ray_cells = depth_cells * depth_count
    cells = depth_cells * width_cells
    f32, i16 = jnp.float32, jnp.int16
    d, i = lax.axis_index("depth"), lax.axis_index("image")
    parity = jnp.stack([d % 2, i % 2]).astype(jnp.int32)
    faces = len(face_list(0, 1))

    x_shape = jax.ShapeDtypeStruct((len(X_PAIRS), width_cells // 2, 16, lanes), i16)
    y_shape = jax.ShapeDtypeStruct((faces, depth_cells, lanes), i16)
    c_shape = jax.ShapeDtypeStruct((faces // 2, 16, lanes), i16)
    half = (depth_cells - 16, 16)
    field = pltpu.with_memory_space_constraint(populations.reshape(Q, cells, lanes), pltpu.HBM)
    edge, da, db = pl.pallas_call(
        functools.partial(edge_kernel, depth_cells, width_cells),
        out_shape=(pltpu.HBM((Q, width_cells, half[1], lanes), f32), x_shape, x_shape),
        in_specs=[SMEM, HBM],
        out_specs=(HBM, VMEM, VMEM),
        scratch_shapes=[
            pltpu.VMEM((Q, half[1] * width_cells, lanes), f32),
            pltpu.VMEM((Q, width_cells, half[1], lanes), f32),
            pltpu.SemaphoreType.DMA((2,)),
            pltpu.SemaphoreType.DMA,
        ],
        compiler_params=GRANT,
        cost_estimate=cost(6),
        name="edge",
    )(parity, field)
    middle, ia, ib = pl.pallas_call(
        functools.partial(middle_kernel, depth_cells, width_cells),
        out_shape=(pltpu.HBM((Q, width_cells, half[0], lanes), f32), y_shape, y_shape),
        in_specs=[SMEM, HBM, HBM],
        out_specs=(HBM, VMEM, VMEM),
        scratch_shapes=[
            pltpu.VMEM((Q, half[0] * width_cells, lanes), f32),
            pltpu.VMEM((Q, width_cells, half[0], lanes), f32),
            pltpu.VMEM((Q, 2 * HALO, half[1], lanes), f32),
            pltpu.SemaphoreType.DMA((depth_cells // 8,)),
            pltpu.SemaphoreType.DMA,
        ],
        compiler_params=GRANT,
        cost_estimate=cost(6),
        name="middle",
    )(parity, field, in_hbm(edge))

    xa = swap(da, "depth", depth_count, 0)
    xb = swap(db, "depth", depth_count, 1)
    ya = swap(ia, "image", image_count, 0)
    yb = swap(ib, "image", image_count, 1)
    halo, ca, cb = pl.pallas_call(
        functools.partial(corner_kernel, width_cells),
        out_shape=(jax.ShapeDtypeStruct((Q, width_cells, 8, lanes), f32), c_shape, c_shape),
        in_specs=[SMEM, VMEM, VMEM],
        out_specs=(VMEM,) * 3,
        compiler_params=GRANT,
        cost_estimate=cost(2),
        name="corner",
    )(parity, xa, xb)
    sent_a, sent_b = ca, cb
    ca = swap(sent_a, "image", image_count, 0)
    cb = swap(sent_b, "image", image_count, 1)

    depth_rows = depth_cells + 8 + 2 * PAD
    width_rows = width_cells + 2 * HALO
    stages = (
        pltpu.VMEM((Q, width_rows, depth_rows, lanes), f32),
        pltpu.VMEM((Q, width_rows, depth_rows, lanes), f32),
        pltpu.VMEM((Q, cells, lanes), f32),
        pltpu.VMEM((3, width_rows, depth_rows, lanes), f32),
        pltpu.VMEM((cells, lanes), f32),
    )
    state = pl.pallas_call(
        functools.partial(inner_kernel, depth_cells, width_cells),
        out_shape=stages,
        in_specs=[HBM, HBM, VMEM],
        out_specs=(VMEM,) * 5,
        scratch_shapes=[
            pltpu.VMEM((Q, width_cells, half[1], lanes), f32),
            pltpu.VMEM((Q, width_cells, half[0], lanes), f32),
            pltpu.SemaphoreType.DMA((4, 2)),
        ],
        compiler_params=GRANT,
        cost_estimate=cost(12),
        name="inner",
    )(in_hbm(edge), in_hbm(middle), halo)

    bumps = transfer.shape[2]
    row = jnp.concatenate([bump_tables(transfer, ray_cells).reshape(-1), direction.astype(f32)])
    row = jnp.pad(row, (0, lanes - row.shape[0]))
    row, _ = lax.optimization_barrier((row, halo))
    tables = lax.all_to_all(
        jnp.broadcast_to(row, (image_count, 8, lanes)), "image", 0, 0, tiled=True
    )
    final, vorticity, *_ = pl.pallas_call(
        functools.partial(outer_kernel, depth_cells, width_cells),
        out_shape=(
            jax.ShapeDtypeStruct((Q, cells, lanes), f32),
            jax.ShapeDtypeStruct((cells, lanes), jnp.bfloat16),
            *stages,
        ),
        in_specs=[SMEM] + [VMEM] * 9,
        out_specs=(HBM,) + (VMEM,) * 6,
        scratch_shapes=[pltpu.SemaphoreType.DMA],
        input_output_aliases={5 + k: 2 + k for k in range(5)},
        compiler_params=GRANT,
        cost_estimate=cost(12),
        name="outer",
    )(parity, ya, yb, ca, cb, *state)

    functions = image_count
    partial = pl.pallas_call(
        functools.partial(render_kernel, depth_cells, width_cells, functions, bumps),
        out_shape=jax.ShapeDtypeStruct((functions, 4, width_cells, lanes), f32),
        in_specs=[SMEM, VMEM],
        out_specs=VMEM,
        scratch_shapes=[
            pltpu.VMEM((2, depth_cells, width_cells, lanes), f32),
            pltpu.VMEM((2, depth_cells, width_cells, lanes), f32),
        ],
        compiler_params=GRANT,
        cost_estimate=cost(16),
        name="render",
    )(tables, vorticity)
    halves = image_count // depth_count
    groups = [
        [sd * image_count + halves * row + side for sd in range(depth_count) for side in range(halves)]
        for row in range(depth_count)
    ]
    slabs = lax.all_to_all(
        partial, ("depth", "image"), 0, 0, axis_index_groups=groups, tiled=True
    ).reshape(depth_count, halves, 4, width_cells, lanes)
    image = composite(slabs, tables[halves * d + i % halves, 0, 5 * bumps] > 0.5)
    route = [
        (sd * image_count + si, (si // halves) * image_count + halves * sd + si % halves)
        for sd in range(depth_count)
        for si in range(image_count)
    ]
    images = lax.ppermute(image, ("depth", "image"), route)
    images = images.reshape(1, 4, halves * width_cells, lanes)
    return (
        final.reshape(populations.shape),
        vorticity.reshape(depth_cells, width_cells, lanes),
        images,
    )


def solution(mesh):
    in_specs = (P(None, "depth", "image", None), P("image", None, None), P("image"))
    out_specs = (
        P(None, "depth", "image", None),
        P("depth", "image", None),
        P("image", None, "depth", None),
    )
    return jax.shard_map(
        on_device, mesh=mesh, in_specs=in_specs, out_specs=out_specs, check_vma=False
    )
```

```python
import functools

import jax
import jax.numpy as jnp
import numpy as np
from jax import lax
from jax.experimental import pallas as pl
from jax.experimental.pallas import tpu as pltpu
from jax.sharding import PartitionSpec as P

VEL = (
    (0, 0, 0),
    (1, 0, 0), (-1, 0, 0), (0, 1, 0), (0, -1, 0), (0, 0, 1), (0, 0, -1),
    (1, 1, 0), (-1, -1, 0), (1, -1, 0), (-1, 1, 0),
    (1, 0, 1), (-1, 0, -1), (1, 0, -1), (-1, 0, 1),
    (0, 1, 1), (0, -1, -1), (0, 1, -1), (0, -1, 1),
)
WEIGHT = (1.0 / 3.0,) + (1.0 / 18.0,) * 6 + (1.0 / 36.0,) * 12
OMEGA = 1.25
Q = len(VEL)
STEPS = 4
HALO = STEPS + 1
AXIS_PAIRS = ((1, 2), (3, 4), (5, 6))
DIAG_PAIRS = ((7, 8), (9, 10), (11, 12), (13, 14), (15, 16), (17, 18))
SCALE = 8192.0

X_PAIRS = tuple(
    (a, b, 5) for a, b in zip((1, 7, 9, 11, 13), (2, 8, 10, 12, 14))
) + ((3, 4, 4), (5, 6, 4), (15, 16, 4), (17, 18, 4), (0, None, 4))


def low_rows(p):
    return 4 + VEL[p][0]


def face_list(nearest, step):
    sent = []
    for layer in range(1, HALO + 1):
        y = nearest + step * (layer - 1)
        for p in range(Q):
            inward = VEL[p][1] * (-step)
            if layer <= 4 + inward:
                sent.append((y, p))
    return sent


def momentum(f):
    s = {}
    d = {}
    for a, b in AXIS_PAIRS + DIAG_PAIRS:
        s[a] = f[a] + f[b]
        d[a] = f[a] - f[b]
    density = ((s[1] + s[3]) + (s[5] + s[7])) + ((s[9] + s[11]) + (s[13] + s[15])) + (s[17] + f[0])
    jx = (d[1] + d[7]) + (d[9] + d[11]) + d[13]
    jy = (d[3] + d[7]) - (d[9] - d[15]) + d[17]
    jz = (d[5] + d[11]) - (d[13] - d[15]) - d[17]
    return density, (jx, jy, jz), s, d


def collide(f):
    density, j, s, d = momentum(f)
    inverse = 1.0 / density
    u = [c * inverse for c in j]
    speed = j[0] * u[0] + j[1] * u[1] + j[2] * u[2]
    common = density - 1.5 * speed
    out = [None] * Q
    out[0] = (OMEGA * WEIGHT[0]) * common - (OMEGA - 1.0) * f[0]
    rest = 0.5 * (OMEGA - 1.0)
    for pairs, w in ((AXIS_PAIRS, WEIGHT[1]), (DIAG_PAIRS, WEIGHT[7])):
        base = (OMEGA * w) * common
        jw = [(3.0 * OMEGA * w) * c for c in j]
        uw = [1.5 * c for c in u]
        for a, b in pairs:
            project_j = None
            project_u = None
            for axis in range(3):
                c = VEL[a][axis]
                if c == 0:
                    continue
                if project_j is None:
                    assert c == 1
                    project_j, project_u = jw[axis], uw[axis]
                elif c > 0:
                    project_j, project_u = project_j + jw[axis], project_u + uw[axis]
                else:
                    project_j, project_u = project_j - jw[axis], project_u - uw[axis]
            even = (base + project_j * project_u) - rest * s[a]
            odd = project_j - rest * d[a]
            out[a] = even + odd
            out[b] = even - odd
    return out


def code(value, p):
    return value * (SCALE / WEIGHT[p]) + (32768.5 - SCALE)


def decode(value, p):
    return value * (WEIGHT[p] / SCALE) + WEIGHT[p]


def row_index():
    return lax.broadcasted_iota(jnp.int32, (8, 128), 0)


def pack16(first, second):
    return jnp.concatenate([first, second], axis=0).astype(jnp.int32).astype(jnp.int16)


def pack_code(first, second):
    whole = jnp.concatenate([first, second], axis=0).astype(jnp.int32)
    return (whole - 32768).astype(jnp.int16)


def wide(value):
    return value.astype(jnp.int32).astype(jnp.float32)


def collide_chunk(f_ref, r_ref, from_row, to_row, width_cells):
    def at_y(y, carry):
        f = [f_ref[p, pl.ds(from_row + y, 8, stride=width_cells), :] for p in range(Q)]
        out = collide(f)
        for p in range(Q):
            value = pltpu.roll(out[p], low_rows(p), 0)
            cz = VEL[p][2]
            r_ref[p, y, to_row : to_row + 8, :] = value if cz == 0 else pltpu.roll(value, cz % 128, 1)
        return carry

    lax.fori_loop(0, width_cells, at_y, 0, unroll=8)


def edge_kernel(depth_cells, width_cells, parity_ref, f_hbm, r_hbm, da_ref, db_ref, f_ref, r_ref, in_sems, out_sem):
    rows = row_index()
    chunk = 8 * width_cells
    loads = []
    for k, j in enumerate((0, depth_cells // 8 - 1)):
        loads.append(
            pltpu.make_async_copy(
                f_hbm.at[:, pl.ds(j * chunk, chunk)], f_ref.at[:, pl.ds(k * chunk, chunk)], in_sems.at[k]
            )
        )
    for load in loads:
        load.start()
    for k, load in enumerate(loads):
        load.wait()
        collide_chunk(f_ref, r_ref, k * chunk, 8 * k, width_cells)
    keep_r = pltpu.make_async_copy(r_ref, r_hbm, out_sem)
    keep_r.start()

    odd_depth = jnp.full((8, 128), parity_ref[0], jnp.int32) == 1

    def face_x(t, carry):
        for number, (a, b, n) in enumerate(X_PAIRS):
            da, db = [], []
            for k in range(2):
                y = 2 * t + k
                low, high = (r_ref[a, y, first : first + 8, :] for first in (0, 8))
                if b is not None:
                    other_low, other_high = (
                        pltpu.roll(r_ref[b, y, first : first + 8, :], n, 0) for first in (0, 8)
                    )
                    low = jnp.where(rows >= n, low, other_low)
                    high = jnp.where(rows < n, high, other_high)
                low, high = code(low, a), code(high, a)
                da.append(jnp.where(odd_depth, low, high))
                db.append(jnp.where(odd_depth, high, low))
            da_ref[number, t] = pack_code(*da)
            db_ref[number, t] = pack_code(*db)
        return carry

    lax.fori_loop(0, width_cells // 2, face_x, 0, unroll=2)
    keep_r.wait()


def middle_kernel(
    depth_cells, width_cells, parity_ref, f_hbm, edge_hbm, r_hbm, ia_ref, ib_ref, f_ref, r_ref, edge_ref, in_sems, out_sem
):
    chunk = 8 * width_cells
    tiles = depth_cells // 8
    loads = []
    for j in range(1, tiles - 1):
        loads.append(
            pltpu.make_async_copy(
                f_hbm.at[:, pl.ds(j * chunk, chunk)], f_ref.at[:, pl.ds((j - 1) * chunk, chunk)], in_sems.at[j]
            )
        )
    for side in range(2):
        first = side * (width_cells - HALO)
        loads.append(
            pltpu.make_async_copy(
                edge_hbm.at[:, pl.ds(first, HALO)], edge_ref.at[:, pl.ds(side * HALO, HALO)],
                in_sems.at[side * (tiles - 1)],
            )
        )
    for load in loads:
        load.start()
    for j in range(tiles - 2):
        loads[j].wait()
        collide_chunk(f_ref, r_ref, j * chunk, 8 * j, width_cells)
    keep_r = pltpu.make_async_copy(r_ref, r_hbm, out_sem)
    keep_r.start()
    for load in loads[tiles - 2 :]:
        load.wait()

    odd_image = jnp.full((8, 128), parity_ref[1], jnp.int32) == 1

    def piece(p, y, t):
        if t in (0, tiles - 1):
            row = y if y < HALO else y - (width_cells - 2 * HALO)
            first = 0 if t == 0 else 8
            return edge_ref[p, row, first : first + 8, :]
        return r_ref[p, y, 8 * t - 8 : 8 * t, :]

    low_face = face_list(0, 1)
    high_face = face_list(width_cells - 1, -1)
    for index, ((yl, pl_), (yh, ph)) in enumerate(zip(low_face, high_face)):
        for c in range(tiles // 2):
            a, b = [], []
            for t in (2 * c, 2 * c + 1):
                low = code(piece(pl_, yl, t), pl_)
                high = code(piece(ph, yh, t), ph)
                a.append(jnp.where(odd_image, low, high))
                b.append(jnp.where(odd_image, high, low))
            ia_ref[index, 16 * c : 16 * c + 16, :] = pack_code(*a)
            ib_ref[index, 16 * c : 16 * c + 16, :] = pack_code(*b)
    keep_r.wait()


def x_halo(low, high, n, second, rows):
    if second:
        low = pltpu.roll(low, 8 - n, 0)
        high = pltpu.roll(high, 8 - n, 0)
        n = 8 - n
    return jnp.where(rows < n, low, high)


X_PLACE = {}
for number_, (a_, b_, n_) in enumerate(X_PAIRS):
    X_PLACE[a_] = (number_, n_, False)
    if b_ is not None:
        X_PLACE[b_] = (number_, n_, True)


def corner_kernel(width_cells, parity_ref, xa_ref, xb_ref, h_hbm, ca_ref, cb_ref, h_ref, out_sem):
    rows = row_index()
    odd_depth = jnp.full((8, 128), parity_ref[0], jnp.int32) == 1
    odd_image = jnp.full((8, 128), parity_ref[1], jnp.int32) == 1

    def halo(t, carry):
        for number, (a, b, n) in enumerate(X_PAIRS):
            va = wide(xa_ref[number, t])
            vb = wide(xb_ref[number, t])
            for k in range(2):
                pa, pb = va[8 * k : 8 * k + 8], vb[8 * k : 8 * k + 8]
                low = jnp.where(odd_depth, pa, pb)
                high = jnp.where(odd_depth, pb, pa)
                h_ref[a, 2 * t + k] = x_halo(low, high, n, False, rows)
                if b is not None:
                    h_ref[b, 2 * t + k] = x_halo(low, high, n, True, rows)
        return carry

    lax.fori_loop(0, width_cells // 2, halo, 0)
    keep_h = pltpu.make_async_copy(h_ref, h_hbm, out_sem)
    keep_h.start()
    low_face = face_list(0, 1)
    high_face = face_list(width_cells - 1, -1)
    for index in range(0, len(low_face), 2):
        a, b = [], []
        for (yl, pl_), (yh, ph) in zip(low_face[index : index + 2], high_face[index : index + 2]):
            low, high = h_ref[pl_, yl], h_ref[ph, yh]
            a.append(jnp.where(odd_image, low, high))
            b.append(jnp.where(odd_image, high, low))
        ca_ref[index // 2] = pack16(*a)
        cb_ref[index // 2] = pack16(*b)
    keep_h.wait()


PAD = 8


def put_streamed(target, p, y, pieces, halo, rows):
    n = low_rows(p)
    before = halo
    for t in range(len(pieces) + 1):
        here = pieces[t] if t < len(pieces) else halo
        target[p, y, PAD + 8 * t : PAD + 8 * t + 8, :] = jnp.where(rows < n, before, here)
        before = here


def step_row(source, target, y, wide_tiles, shift):
    for t in range(wide_tiles):
        first = PAD + 8 * t
        out = collide([source[p, y - VEL[p][1], first : first + 8, :] for p in range(Q)])
        for p in range(Q):
            cx, _, cz = VEL[p]
            value = out[p] if cz == 0 else pltpu.roll(out[p], cz % 128, 1)
            row = first + shift + cx
            target[p, y, row : row + 8, :] = value


BASE = PAD + 8


def flow_row(source, flow_ref, y, tiles):
    for t in range(-1, tiles + 1):
        first = BASE + 8 * t
        density, j, _, _ = momentum([source[p, y - VEL[p][1], first : first + 8, :] for p in range(Q)])
        inverse = 1.0 / density
        for axis in range(3):
            flow_ref[axis, y, first : first + 8, :] = j[axis] * inverse


def final_row(source, out_ref, y, origin, tiles, width_cells):
    for t in range(tiles):
        first = BASE + 8 * t
        for p in range(Q):
            out_ref[p, pl.ds(8 * t * width_cells + y - origin, 8, stride=width_cells), :] = source[
                p, y - VEL[p][1], first : first + 8, :
            ]


def spin_row(flow_ref, out_ref, y, origin, tiles, width_cells):
    for t in range(tiles):
        first = BASE + 8 * t

        def dx(axis):
            return (flow_ref[axis, y, first + 1 : first + 9, :] - flow_ref[axis, y, first - 1 : first + 7, :]) * 0.5

        def dy(axis):
            return (flow_ref[axis, y + 1, first : first + 8, :] - flow_ref[axis, y - 1, first : first + 8, :]) * 0.5

        def dz(axis):
            value = flow_ref[axis, y, first : first + 8, :]
            return (pltpu.roll(value, 127, 1) - pltpu.roll(value, 1, 1)) * 0.5

        sx = dy(2) - dz(1)
        sy = dz(0) - dx(2)
        sz = dx(1) - dy(0)
        out_ref[pl.ds(8 * t * width_cells + y - origin, 8, stride=width_cells), :] = jnp.sqrt(
            sx * sx + sy * sy + sz * sz
        )


def inner_kernel(
    depth_cells, width_cells, e_hbm, r_hbm, h_hbm, sa_ref, sb_ref, final_ref, flow_ref, plain_ref, e_ref, r_ref, h_ref, sems
):
    tiles = depth_cells // 8
    rows = row_index()

    def own(y, carry):
        for p in range(Q):
            pieces = [r_ref[p, y, 8 * t : 8 * t + 8, :] for t in range(tiles - 2)]
            pieces = [e_ref[p, y, 0:8, :]] + pieces + [e_ref[p, y, 8:16, :]]
            put_streamed(sa_ref, p, y + HALO, pieces, decode(h_ref[p, y], p), rows)
        return carry

    parts = 4
    count = width_cells // parts
    loads = []
    for part in range(parts):
        at = pl.ds(part * count, count)
        loads.append(
            [
                pltpu.make_async_copy(e_hbm.at[:, at], e_ref.at[:, at], sems.at[part, 0]),
                pltpu.make_async_copy(r_hbm.at[:, at], r_ref.at[:, at], sems.at[part, 1]),
                pltpu.make_async_copy(h_hbm.at[:, at], h_ref.at[:, at], sems.at[part, 2]),
            ]
        )
        for load in loads[-1]:
            load.start()
    for part in range(parts):
        for load in loads[part]:
            load.wait()
        lax.fori_loop(part * count, (part + 1) * count, own, 0)

    def stage(source, target, step, shift):
        def pair(k, carry):
            step_row(source, target, HALO + step + 2 * k, tiles + 1, shift)
            step_row(source, target, HALO + step + 2 * k + 1, tiles + 1, shift)
            return carry

        lax.fori_loop(0, (width_cells - 2 * step) // 2, pair, 0)

    stage(sa_ref, sb_ref, 1, 0)
    stage(sb_ref, sa_ref, 2, 0)
    stage(sa_ref, sb_ref, 3, 4)

    def last(y, carry):
        flow_row(sb_ref, flow_ref, y, tiles)
        final_row(sb_ref, final_ref, y, HALO, tiles, width_cells)
        return carry

    lax.fori_loop(HALO + STEPS, HALO + width_cells - STEPS, last, 0, unroll=2)

    def spins(y, carry):
        spin_row(flow_ref, plain_ref, y, HALO, tiles, width_cells)
        return carry

    lax.fori_loop(2 * HALO, width_cells, spins, 0, unroll=2)


def outer_kernel(
    depth_cells, width_cells, parity_ref, ya_ref, yb_ref, ca_ref, cb_ref,
    sa_in, sb_in, final_in, flow_in, plain_in,
    out_hbm, vort_ref, sa_ref, sb_ref, out_ref, flow_ref, plain_ref, out_sem,
):
    tiles = depth_cells // 8
    rows = row_index()
    odd_image = jnp.full((8, 128), parity_ref[1], jnp.int32) == 1

    low_face = face_list(0, 1)
    high_face = face_list(width_cells - 1, -1)
    for index in range(0, len(low_face), 2):
        corner_a, corner_b = wide(ca_ref[index // 2]), wide(cb_ref[index // 2])
        for k in range(2):
            (yl, pl_), (yh, ph) = low_face[index + k], high_face[index + k]
            ca, cb = corner_a[8 * k : 8 * k + 8], corner_b[8 * k : 8 * k + 8]
            low = [jnp.where(odd_image, ca, cb)]
            high = [jnp.where(odd_image, cb, ca)]
            for c in range(depth_cells // 16):
                ya = wide(ya_ref[index + k, 16 * c : 16 * c + 16, :])
                yb = wide(yb_ref[index + k, 16 * c : 16 * c + 16, :])
                for half in range(2):
                    a, b = ya[8 * half : 8 * half + 8], yb[8 * half : 8 * half + 8]
                    low.append(jnp.where(odd_image, a, b))
                    high.append(jnp.where(odd_image, b, a))
            low = [decode(v, ph) for v in low]
            high = [decode(v, pl_) for v in high]
            put_streamed(sa_ref, ph, yh - width_cells + HALO, low[1:], low[0], rows)
            put_streamed(sa_ref, pl_, yl + width_cells + HALO, high[1:], high[0], rows)

    def stage(source, target, step, shift):
        reach = HALO - step

        def both(k, carry):
            step_row(source, target, HALO - reach + k, tiles + 1, shift)
            step_row(source, target, HALO + width_cells - step + k, tiles + 1, shift)
            return carry

        lax.fori_loop(0, HALO, both, 0, unroll=HALO)

    stage(sa_ref, sb_ref, 1, 0)
    stage(sb_ref, sa_ref, 2, 0)
    stage(sa_ref, sb_ref, 3, 4)

    def finish(k, carry):
        final_row(sb_ref, out_ref, HALO + k, HALO, tiles, width_cells)
        final_row(sb_ref, out_ref, HALO + width_cells - STEPS + k, HALO, tiles, width_cells)
        return carry

    lax.fori_loop(0, STEPS, finish, 0)
    keep_out = pltpu.make_async_copy(out_ref, out_hbm, out_sem)
    keep_out.start()

    def flows(k, carry):
        flow_row(sb_ref, flow_ref, HALO - 1 + k, tiles)
        flow_row(sb_ref, flow_ref, HALO + width_cells - STEPS + k, tiles)
        return carry

    lax.fori_loop(0, HALO, flows, 0)

    def spins(k, carry):
        spin_row(flow_ref, plain_ref, HALO + k, HALO, tiles, width_cells)
        spin_row(flow_ref, plain_ref, width_cells + k, HALO, tiles, width_cells)
        return carry

    lax.fori_loop(0, HALO, spins, 0)

    def rounded(x, carry):
        at = pl.ds(pl.multiple_of(x * 16, 16), 16)
        vort_ref[at, :] = plain_ref[at, :].astype(jnp.bfloat16)
        return carry

    lax.fori_loop(0, depth_cells * width_cells // 16, rounded, 0, unroll=4)
    keep_out.wait()


BUMP_WIDTH = 0.15
LEVEL_OFFSET = 0.05
STRETCH = float(np.sqrt(np.log2(np.e)) / BUMP_WIDTH)
CENTRE = 4.0
LOG2E = float(np.log2(np.e))


def bump_tables(transfer, ray_cells):
    b = STRETCH * transfer[:, 0] - CENTRE
    fade = jnp.exp2(-b * b)
    strength = transfer[:, 1:] * fade[:, None]
    strength = strength.at[:, 0].multiply(LOG2E / ray_cells)
    return jnp.concatenate([(2.0 * b)[:, None], strength], axis=1)


BLOCK = 4


def render_kernel(depth_cells, width_cells, functions, bumps, table_ref, plain_ref, image_ref, place_ref, fade_ref):
    def prepare(x, carry):
        at = pl.ds(pl.multiple_of(x * width_cells, width_cells), width_cells)
        value = plain_ref[at, :].astype(jnp.bfloat16).astype(jnp.float32)
        level = value / (value + LEVEL_OFFSET)
        place = STRETCH * level - CENTRE
        fade = jnp.exp2(-place * place)
        for order, to in ((0, x), (1, depth_cells - 1 - x)):
            place_ref[order, to] = place
            fade_ref[order, to] = fade
        return carry

    lax.fori_loop(0, depth_cells, prepare, 0)

    def one(m, carry):
        order = jnp.where(table_ref[m, 0, 5 * bumps] > 0.5, 1, 0)

        def cells(block, state):
            clear, red, green, blue = state
            at = pl.ds(block * BLOCK, BLOCK)
            place = place_ref[order, at]
            total = [None] * 4
            for k in range(bumps):
                bump = jnp.exp2(place * table_ref[m, 0, k])
                for c in range(4):
                    term = bump * table_ref[m, 0, (1 + c) * bumps + k]
                    total[c] = term if total[c] is None else total[c] + term
            fade = fade_ref[order, at]
            passing = jnp.exp2(-(total[0] * fade))
            for b in range(BLOCK):
                behind = clear * passing[b]
                weight = (clear - behind) * fade[b]
                clear = behind
                red = red + weight * total[1][b]
                green = green + weight * total[2][b]
                blue = blue + weight * total[3][b]
            return clear, red, green, blue

        zero = jnp.zeros((width_cells, 128), jnp.float32)
        clear, red, green, blue = lax.fori_loop(0, depth_cells // BLOCK, cells, (zero + 1.0, zero, zero, zero))
        image_ref[m, 0] = red
        image_ref[m, 1] = green
        image_ref[m, 2] = blue
        image_ref[m, 3] = clear
        return carry

    lax.fori_loop(0, functions, one, 0)


def composite_kernel(slabs, halves, order_ref, piece_ref, image_ref):
    backward = order_ref[0] > 0.5
    width_cells = piece_ref.shape[3]
    for side in range(halves):
        at = slice(side * width_cells, (side + 1) * width_cells)
        clear = jnp.ones(piece_ref.shape[3:], jnp.float32)
        color = [jnp.zeros_like(clear) for c in range(3)]
        for step in range(slabs):
            slab = jnp.where(backward, slabs - 1 - step, step)
            color = [color[c] + clear * piece_ref[slab, side, c] for c in range(3)]
            clear = clear * piece_ref[slab, side, 3]
        for c in range(3):
            image_ref[c, at, :] = color[c]
        image_ref[3, at, :] = 1.0 - clear


HBM = pl.BlockSpec(memory_space=pltpu.HBM)
VMEM = pl.BlockSpec(memory_space=pltpu.VMEM)
SMEM = pl.BlockSpec(memory_space=pltpu.SMEM)
GRANT = pltpu.CompilerParams(vmem_limit_bytes=14 * 1024 * 1024)


def cost(microseconds):
    return pl.CostEstimate(flops=0, bytes_accessed=int(microseconds * 3.69e6), transcendentals=0)


def in_hbm(value):
    return pltpu.with_memory_space_constraint(value, pltpu.HBM)


def in_vmem(value):
    return pltpu.with_memory_space_constraint(value, pltpu.VMEM)


def partner(index, count, phase):
    return index ^ 1 if phase == 0 else (((index + 1) ^ 1) - 1) % count


def swap(value, axis, count, phase):
    return lax.ppermute(value, axis, [(i, partner(i, count, phase)) for i in range(count)])


def on_device(populations, transfer, direction):
    _, depth_cells, width_cells, lanes = populations.shape
    depth_count, image_count = lax.axis_size("depth"), lax.axis_size("image")
    ray_cells = depth_cells * depth_count
    cells = depth_cells * width_cells
    f32, i16 = jnp.float32, jnp.int16
    d, i = lax.axis_index("depth"), lax.axis_index("image")
    parity = jnp.stack([d % 2, i % 2]).astype(jnp.int32)
    faces = len(face_list(0, 1))

    x_shape = jax.ShapeDtypeStruct((len(X_PAIRS), width_cells // 2, 16, lanes), i16)
    y_shape = jax.ShapeDtypeStruct((faces, depth_cells, lanes), i16)
    c_shape = jax.ShapeDtypeStruct((faces // 2, 16, lanes), i16)
    half = (depth_cells - 16, 16)
    field = pltpu.with_memory_space_constraint(populations.reshape(Q, cells, lanes), pltpu.HBM)
    edge, da, db = pl.pallas_call(
        functools.partial(edge_kernel, depth_cells, width_cells),
        out_shape=(pltpu.HBM((Q, width_cells, half[1], lanes), f32), x_shape, x_shape),
        in_specs=[SMEM, HBM],
        out_specs=(HBM, VMEM, VMEM),
        scratch_shapes=[
            pltpu.VMEM((Q, half[1] * width_cells, lanes), f32),
            pltpu.VMEM((Q, width_cells, half[1], lanes), f32),
            pltpu.SemaphoreType.DMA((2,)),
            pltpu.SemaphoreType.DMA,
        ],
        compiler_params=GRANT,
        cost_estimate=cost(6),
        name="edge",
    )(parity, field)
    middle, ia, ib = pl.pallas_call(
        functools.partial(middle_kernel, depth_cells, width_cells),
        out_shape=(pltpu.HBM((Q, width_cells, half[0], lanes), f32), y_shape, y_shape),
        in_specs=[SMEM, HBM, HBM],
        out_specs=(HBM, VMEM, VMEM),
        scratch_shapes=[
            pltpu.VMEM((Q, half[0] * width_cells, lanes), f32),
            pltpu.VMEM((Q, width_cells, half[0], lanes), f32),
            pltpu.VMEM((Q, 2 * HALO, half[1], lanes), f32),
            pltpu.SemaphoreType.DMA((depth_cells // 8,)),
            pltpu.SemaphoreType.DMA,
        ],
        compiler_params=GRANT,
        cost_estimate=cost(6),
        name="middle",
    )(parity, field, in_hbm(edge))

    xa = swap(da, "depth", depth_count, 0)
    xb = swap(db, "depth", depth_count, 1)
    ya = swap(ia, "image", image_count, 0)
    yb = swap(ib, "image", image_count, 1)
    halo, ca, cb = pl.pallas_call(
        functools.partial(corner_kernel, width_cells),
        out_shape=(pltpu.HBM((Q, width_cells, 8, lanes), f32), c_shape, c_shape),
        in_specs=[SMEM, VMEM, VMEM],
        out_specs=(HBM, VMEM, VMEM),
        scratch_shapes=[pltpu.VMEM((Q, width_cells, 8, lanes), f32), pltpu.SemaphoreType.DMA],
        compiler_params=GRANT,
        cost_estimate=cost(2),
        name="corner",
    )(parity, xa, xb)
    sent_a, sent_b = ca, cb
    ca = swap(sent_a, "image", image_count, 0)
    cb = swap(sent_b, "image", image_count, 1)

    depth_rows = depth_cells + 8 + 2 * PAD
    width_rows = width_cells + 2 * HALO
    stages = (
        pltpu.VMEM((Q, width_rows, depth_rows, lanes), f32),
        pltpu.VMEM((Q, width_rows, depth_rows, lanes), f32),
        pltpu.VMEM((Q, cells, lanes), f32),
        pltpu.VMEM((3, width_rows, depth_rows, lanes), f32),
        pltpu.VMEM((cells, lanes), f32),
    )
    state = pl.pallas_call(
        functools.partial(inner_kernel, depth_cells, width_cells),
        out_shape=stages,
        in_specs=[HBM] * 3,
        out_specs=(VMEM,) * 5,
        scratch_shapes=[
            pltpu.VMEM((Q, width_cells, half[1], lanes), f32),
            pltpu.VMEM((Q, width_cells, half[0], lanes), f32),
            pltpu.VMEM((Q, width_cells, 8, lanes), f32),
            pltpu.SemaphoreType.DMA((4, 3)),
        ],
        compiler_params=GRANT,
        cost_estimate=cost(12),
        name="inner",
    )(in_hbm(edge), in_hbm(middle), in_hbm(halo))

    bumps = transfer.shape[2]
    row = jnp.concatenate([bump_tables(transfer, ray_cells).reshape(-1), direction.astype(f32)])
    row = jnp.pad(row, (0, lanes - row.shape[0]))
    row, _ = lax.optimization_barrier((row, halo))
    tables = lax.all_to_all(
        jnp.broadcast_to(row, (image_count, 8, lanes)), "image", 0, 0, tiled=True
    )
    final, vorticity, *_, plain = pl.pallas_call(
        functools.partial(outer_kernel, depth_cells, width_cells),
        out_shape=(
            jax.ShapeDtypeStruct((Q, cells, lanes), f32),
            jax.ShapeDtypeStruct((cells, lanes), jnp.bfloat16),
            *stages,
        ),
        in_specs=[SMEM] + [VMEM] * 9,
        out_specs=(HBM,) + (VMEM,) * 6,
        scratch_shapes=[pltpu.SemaphoreType.DMA],
        input_output_aliases={5 + k: 2 + k for k in range(5)},
        compiler_params=GRANT,
        cost_estimate=cost(12),
        name="outer",
    )(parity, ya, yb, ca, cb, *state)

    functions = image_count
    partial = pl.pallas_call(
        functools.partial(render_kernel, depth_cells, width_cells, functions, bumps),
        out_shape=jax.ShapeDtypeStruct((functions, 4, width_cells, lanes), f32),
        in_specs=[SMEM, VMEM],
        out_specs=VMEM,
        scratch_shapes=[
            pltpu.VMEM((2, depth_cells, width_cells, lanes), f32),
            pltpu.VMEM((2, depth_cells, width_cells, lanes), f32),
        ],
        compiler_params=GRANT,
        cost_estimate=cost(16),
        name="render",
    )(tables, in_vmem(plain))
    halves = image_count // depth_count
    groups = [
        [sd * image_count + halves * row + side for sd in range(depth_count) for side in range(halves)]
        for row in range(depth_count)
    ]
    slabs = lax.all_to_all(
        partial, ("depth", "image"), 0, 0, axis_index_groups=groups, tiled=True
    ).reshape(depth_count, halves, 4, width_cells, lanes)
    image = pl.pallas_call(
        functools.partial(composite_kernel, depth_count, halves),
        out_shape=jax.ShapeDtypeStruct((4, halves * width_cells, lanes), f32),
        in_specs=[SMEM, VMEM],
        out_specs=VMEM,
        cost_estimate=cost(1),
        name="composite",
    )(tables[halves * d + i % halves, 0, 5 * bumps][None], in_vmem(slabs))
    route = [
        (sd * image_count + si, (si // halves) * image_count + halves * sd + si % halves)
        for sd in range(depth_count)
        for si in range(image_count)
    ]
    images = lax.ppermute(image, ("depth", "image"), route)
    images = images[None]
    return (
        final.reshape(populations.shape),
        vorticity.reshape(depth_cells, width_cells, lanes),
        images,
    )


def solution(mesh):
    in_specs = (P(None, "depth", "image", None), P("image", None, None), P("image"))
    out_specs = (
        P(None, "depth", "image", None),
        P("depth", "image", None),
        P("image", None, "depth", None),
    )
    return jax.shard_map(
        on_device, mesh=mesh, in_specs=in_specs, out_specs=out_specs, check_vma=False
    )
```

```python
import functools

import jax
import jax.numpy as jnp
import numpy as np
from jax import lax
from jax.experimental import pallas as pl
from jax.experimental.pallas import tpu as pltpu
from jax.sharding import PartitionSpec as P

VEL = (
    (0, 0, 0),
    (1, 0, 0), (-1, 0, 0), (0, 1, 0), (0, -1, 0), (0, 0, 1), (0, 0, -1),
    (1, 1, 0), (-1, -1, 0), (1, -1, 0), (-1, 1, 0),
    (1, 0, 1), (-1, 0, -1), (1, 0, -1), (-1, 0, 1),
    (0, 1, 1), (0, -1, -1), (0, 1, -1), (0, -1, 1),
)
WEIGHT = (1.0 / 3.0,) + (1.0 / 18.0,) * 6 + (1.0 / 36.0,) * 12
OMEGA = 1.25
Q = len(VEL)
STEPS = 4
HALO = STEPS + 1
AXIS_PAIRS = ((1, 2), (3, 4), (5, 6))
DIAG_PAIRS = ((7, 8), (9, 10), (11, 12), (13, 14), (15, 16), (17, 18))
SCALE = 8192.0

X_PAIRS = tuple(
    (a, b, 5) for a, b in zip((1, 7, 9, 11, 13), (2, 8, 10, 12, 14))
) + ((3, 4, 4), (5, 6, 4), (15, 16, 4), (17, 18, 4), (0, None, 4))


def low_rows(p):
    return 4 + VEL[p][0]


def face_list(nearest, step):
    sent = []
    for layer in range(1, HALO + 1):
        y = nearest + step * (layer - 1)
        for p in range(Q):
            inward = VEL[p][1] * (-step)
            if layer <= 4 + inward:
                sent.append((y, p))
    return sent


def momentum(f):
    s = {}
    d = {}
    for a, b in AXIS_PAIRS + DIAG_PAIRS:
        s[a] = f[a] + f[b]
        d[a] = f[a] - f[b]
    density = ((s[1] + s[3]) + (s[5] + s[7])) + ((s[9] + s[11]) + (s[13] + s[15])) + (s[17] + f[0])
    jx = (d[1] + d[7]) + (d[9] + d[11]) + d[13]
    jy = (d[3] + d[7]) - (d[9] - d[15]) + d[17]
    jz = (d[5] + d[11]) - (d[13] - d[15]) - d[17]
    return density, (jx, jy, jz), s, d


def collide(f):
    density, j, s, d = momentum(f)
    inverse = 1.0 / density
    u = [c * inverse for c in j]
    speed = j[0] * u[0] + j[1] * u[1] + j[2] * u[2]
    common = density - 1.5 * speed
    out = [None] * Q
    out[0] = (OMEGA * WEIGHT[0]) * common - (OMEGA - 1.0) * f[0]
    rest = 0.5 * (OMEGA - 1.0)
    for pairs, w in ((AXIS_PAIRS, WEIGHT[1]), (DIAG_PAIRS, WEIGHT[7])):
        base = (OMEGA * w) * common
        jw = [(3.0 * OMEGA * w) * c for c in j]
        uw = [1.5 * c for c in u]
        for a, b in pairs:
            project_j = None
            project_u = None
            for axis in range(3):
                c = VEL[a][axis]
                if c == 0:
                    continue
                if project_j is None:
                    assert c == 1
                    project_j, project_u = jw[axis], uw[axis]
                elif c > 0:
                    project_j, project_u = project_j + jw[axis], project_u + uw[axis]
                else:
                    project_j, project_u = project_j - jw[axis], project_u - uw[axis]
            even = (base + project_j * project_u) - rest * s[a]
            odd = project_j - rest * d[a]
            out[a] = even + odd
            out[b] = even - odd
    return out


def code(value, p):
    return value * (SCALE / WEIGHT[p]) + (32768.5 - SCALE)


def decode(value, p):
    return value * (WEIGHT[p] / SCALE) + WEIGHT[p]


def row_index():
    return lax.broadcasted_iota(jnp.int32, (8, 128), 0)


def pack16(first, second):
    return jnp.concatenate([first, second], axis=0).astype(jnp.int32).astype(jnp.int16)


def pack_code(first, second):
    whole = jnp.concatenate([first, second], axis=0).astype(jnp.int32)
    return (whole - 32768).astype(jnp.int16)


def wide(value):
    return value.astype(jnp.int32).astype(jnp.float32)


def collide_chunk(f_ref, r_ref, from_row, to_row, width_cells):
    def at_y(y, carry):
        f = [f_ref[p, pl.ds(from_row + y, 8, stride=width_cells), :] for p in range(Q)]
        out = collide(f)
        for p in range(Q):
            value = pltpu.roll(out[p], low_rows(p), 0)
            cz = VEL[p][2]
            r_ref[p, y, to_row : to_row + 8, :] = value if cz == 0 else pltpu.roll(value, cz % 128, 1)
        return carry

    lax.fori_loop(0, width_cells, at_y, 0, unroll=8)


def keep_chunk(r_ref, r_hbm, k, sems):
    at = pl.ds(8 * k, 8)
    copy = pltpu.make_async_copy(r_ref.at[:, :, at], r_hbm.at[:, :, at], sems.at[k])
    copy.start()
    return copy


def edge_kernel(depth_cells, width_cells, parity_ref, f_hbm, r_hbm, da_ref, db_ref, f_ref, r_ref, in_sems, out_sems):
    rows = row_index()
    chunk = 8 * width_cells
    loads = []
    for k, j in enumerate((0, depth_cells // 8 - 1)):
        loads.append(
            pltpu.make_async_copy(
                f_hbm.at[:, pl.ds(j * chunk, chunk)], f_ref.at[:, pl.ds(k * chunk, chunk)], in_sems.at[k]
            )
        )
    for load in loads:
        load.start()
    keeps = []
    for k, load in enumerate(loads):
        load.wait()
        collide_chunk(f_ref, r_ref, k * chunk, 8 * k, width_cells)
        keeps.append(keep_chunk(r_ref, r_hbm, k, out_sems))

    odd_depth = jnp.full((8, 128), parity_ref[0], jnp.int32) == 1

    def face_x(t, carry):
        for number, (a, b, n) in enumerate(X_PAIRS):
            da, db = [], []
            for k in range(2):
                y = 2 * t + k
                low, high = (r_ref[a, y, first : first + 8, :] for first in (0, 8))
                if b is not None:
                    other_low, other_high = (
                        pltpu.roll(r_ref[b, y, first : first + 8, :], n, 0) for first in (0, 8)
                    )
                    low = jnp.where(rows >= n, low, other_low)
                    high = jnp.where(rows < n, high, other_high)
                low, high = code(low, a), code(high, a)
                da.append(jnp.where(odd_depth, low, high))
                db.append(jnp.where(odd_depth, high, low))
            da_ref[number, t] = pack_code(*da)
            db_ref[number, t] = pack_code(*db)
        return carry

    lax.fori_loop(0, width_cells // 2, face_x, 0, unroll=2)
    for keep in keeps:
        keep.wait()


def middle_kernel(
    depth_cells, width_cells, parity_ref, f_hbm, edge_hbm, r_hbm, ia_ref, ib_ref, f_ref, r_ref, edge_ref, in_sems, out_sems
):
    chunk = 8 * width_cells
    tiles = depth_cells // 8
    loads = []
    for j in range(1, tiles - 1):
        loads.append(
            pltpu.make_async_copy(
                f_hbm.at[:, pl.ds(j * chunk, chunk)], f_ref.at[:, pl.ds((j - 1) * chunk, chunk)], in_sems.at[j]
            )
        )
    for side in range(2):
        first = side * (width_cells - HALO)
        loads.append(
            pltpu.make_async_copy(
                edge_hbm.at[:, pl.ds(first, HALO)], edge_ref.at[:, pl.ds(side * HALO, HALO)],
                in_sems.at[side * (tiles - 1)],
            )
        )
    for load in loads:
        load.start()
    keeps = []
    for j in range(tiles - 2):
        loads[j].wait()
        collide_chunk(f_ref, r_ref, j * chunk, 8 * j, width_cells)
        keeps.append(keep_chunk(r_ref, r_hbm, j, out_sems))
    for load in loads[tiles - 2 :]:
        load.wait()

    odd_image = jnp.full((8, 128), parity_ref[1], jnp.int32) == 1

    def piece(p, y, t):
        if t in (0, tiles - 1):
            row = y if y < HALO else y - (width_cells - 2 * HALO)
            first = 0 if t == 0 else 8
            return edge_ref[p, row, first : first + 8, :]
        return r_ref[p, y, 8 * t - 8 : 8 * t, :]

    low_face = face_list(0, 1)
    high_face = face_list(width_cells - 1, -1)
    for index, ((yl, pl_), (yh, ph)) in enumerate(zip(low_face, high_face)):
        for c in range(tiles // 2):
            a, b = [], []
            for t in (2 * c, 2 * c + 1):
                low = code(piece(pl_, yl, t), pl_)
                high = code(piece(ph, yh, t), ph)
                a.append(jnp.where(odd_image, low, high))
                b.append(jnp.where(odd_image, high, low))
            ia_ref[index, 16 * c : 16 * c + 16, :] = pack_code(*a)
            ib_ref[index, 16 * c : 16 * c + 16, :] = pack_code(*b)
    for keep in keeps:
        keep.wait()


def x_halo(low, high, n, second, rows):
    if second:
        low = pltpu.roll(low, 8 - n, 0)
        high = pltpu.roll(high, 8 - n, 0)
        n = 8 - n
    return jnp.where(rows < n, low, high)


X_PLACE = {}
for number_, (a_, b_, n_) in enumerate(X_PAIRS):
    X_PLACE[a_] = (number_, n_, False)
    if b_ is not None:
        X_PLACE[b_] = (number_, n_, True)


def corner_kernel(width_cells, parity_ref, xa_ref, xb_ref, h_hbm, ca_ref, cb_ref, h_ref, out_sem):
    rows = row_index()
    odd_depth = jnp.full((8, 128), parity_ref[0], jnp.int32) == 1
    odd_image = jnp.full((8, 128), parity_ref[1], jnp.int32) == 1

    def halo(t, carry):
        for number, (a, b, n) in enumerate(X_PAIRS):
            va = wide(xa_ref[number, t])
            vb = wide(xb_ref[number, t])
            for k in range(2):
                pa, pb = va[8 * k : 8 * k + 8], vb[8 * k : 8 * k + 8]
                low = jnp.where(odd_depth, pa, pb)
                high = jnp.where(odd_depth, pb, pa)
                h_ref[a, 2 * t + k] = x_halo(low, high, n, False, rows)
                if b is not None:
                    h_ref[b, 2 * t + k] = x_halo(low, high, n, True, rows)
        return carry

    lax.fori_loop(0, width_cells // 2, halo, 0)
    keep_h = pltpu.make_async_copy(h_ref, h_hbm, out_sem)
    keep_h.start()
    low_face = face_list(0, 1)
    high_face = face_list(width_cells - 1, -1)
    for index in range(0, len(low_face), 2):
        a, b = [], []
        for (yl, pl_), (yh, ph) in zip(low_face[index : index + 2], high_face[index : index + 2]):
            low, high = h_ref[pl_, yl], h_ref[ph, yh]
            a.append(jnp.where(odd_image, low, high))
            b.append(jnp.where(odd_image, high, low))
        ca_ref[index // 2] = pack16(*a)
        cb_ref[index // 2] = pack16(*b)
    keep_h.wait()


PAD = 8


def put_streamed(target, p, y, pieces, halo, rows):
    n = low_rows(p)
    before = halo
    for t in range(len(pieces) + 1):
        here = pieces[t] if t < len(pieces) else halo
        target[p, y, PAD + 8 * t : PAD + 8 * t + 8, :] = jnp.where(rows < n, before, here)
        before = here


def step_row(source, target, y, wide_tiles, shift):
    for t in range(wide_tiles):
        first = PAD + 8 * t
        out = collide([source[p, y - VEL[p][1], first : first + 8, :] for p in range(Q)])
        for p in range(Q):
            cx, _, cz = VEL[p]
            value = out[p] if cz == 0 else pltpu.roll(out[p], cz % 128, 1)
            row = first + shift + cx
            target[p, y, row : row + 8, :] = value


BASE = PAD + 8


def flow_row(source, flow_ref, y, tiles):
    for t in range(-1, tiles + 1):
        first = BASE + 8 * t
        density, j, _, _ = momentum([source[p, y - VEL[p][1], first : first + 8, :] for p in range(Q)])
        inverse = 1.0 / density
        for axis in range(3):
            flow_ref[axis, y, first : first + 8, :] = j[axis] * inverse


def final_row(source, out_ref, y, origin, tiles, width_cells):
    for t in range(tiles):
        first = BASE + 8 * t
        for p in range(Q):
            out_ref[p, pl.ds(8 * t * width_cells + y - origin, 8, stride=width_cells), :] = source[
                p, y - VEL[p][1], first : first + 8, :
            ]


def spin_row(flow_ref, out_ref, y, origin, tiles, width_cells):
    for t in range(tiles):
        first = BASE + 8 * t

        def dx(axis):
            return (flow_ref[axis, y, first + 1 : first + 9, :] - flow_ref[axis, y, first - 1 : first + 7, :]) * 0.5

        def dy(axis):
            return (flow_ref[axis, y + 1, first : first + 8, :] - flow_ref[axis, y - 1, first : first + 8, :]) * 0.5

        def dz(axis):
            value = flow_ref[axis, y, first : first + 8, :]
            return (pltpu.roll(value, 127, 1) - pltpu.roll(value, 1, 1)) * 0.5

        sx = dy(2) - dz(1)
        sy = dz(0) - dx(2)
        sz = dx(1) - dy(0)
        out_ref[pl.ds(8 * t * width_cells + y - origin, 8, stride=width_cells), :] = jnp.sqrt(
            sx * sx + sy * sy + sz * sz
        )


def inner_kernel(
    depth_cells, width_cells, e_hbm, r_hbm, h_hbm, sa_ref, sb_ref, final_ref, flow_ref, plain_ref, e_ref, r_ref, h_ref, sems
):
    tiles = depth_cells // 8
    rows = row_index()

    def own(y, carry):
        for p in range(Q):
            pieces = [r_ref[p, y, 8 * t : 8 * t + 8, :] for t in range(tiles - 2)]
            pieces = [e_ref[p, y, 0:8, :]] + pieces + [e_ref[p, y, 8:16, :]]
            put_streamed(sa_ref, p, y + HALO, pieces, decode(h_ref[p, y], p), rows)
        return carry

    parts = 4
    count = width_cells // parts
    loads = []
    for part in range(parts):
        at = pl.ds(part * count, count)
        loads.append(
            [
                pltpu.make_async_copy(e_hbm.at[:, at], e_ref.at[:, at], sems.at[part, 0]),
                pltpu.make_async_copy(r_hbm.at[:, at], r_ref.at[:, at], sems.at[part, 1]),
                pltpu.make_async_copy(h_hbm.at[:, at], h_ref.at[:, at], sems.at[part, 2]),
            ]
        )
        for load in loads[-1]:
            load.start()
    for part in range(parts):
        for load in loads[part]:
            load.wait()
        lax.fori_loop(part * count, (part + 1) * count, own, 0)

    def stage(source, target, step, shift):
        def pair(k, carry):
            step_row(source, target, HALO + step + 2 * k, tiles + 1, shift)
            step_row(source, target, HALO + step + 2 * k + 1, tiles + 1, shift)
            return carry

        lax.fori_loop(0, (width_cells - 2 * step) // 2, pair, 0, unroll=True)

    stage(sa_ref, sb_ref, 1, 0)
    stage(sb_ref, sa_ref, 2, 0)
    stage(sa_ref, sb_ref, 3, 4)

    def last(y, carry):
        flow_row(sb_ref, flow_ref, y, tiles)
        final_row(sb_ref, final_ref, y, HALO, tiles, width_cells)
        return carry

    lax.fori_loop(HALO + STEPS, HALO + width_cells - STEPS, last, 0, unroll=2)

    def spins(y, carry):
        spin_row(flow_ref, plain_ref, y, HALO, tiles, width_cells)
        return carry

    lax.fori_loop(2 * HALO, width_cells, spins, 0, unroll=2)


def outer_kernel(
    depth_cells, width_cells, parity_ref, ya_ref, yb_ref, ca_ref, cb_ref,
    sa_in, sb_in, final_in, flow_in, plain_in,
    out_hbm, vort_ref, sa_ref, sb_ref, out_ref, flow_ref, plain_ref, out_sem,
):
    tiles = depth_cells // 8
    rows = row_index()
    odd_image = jnp.full((8, 128), parity_ref[1], jnp.int32) == 1

    low_face = face_list(0, 1)
    high_face = face_list(width_cells - 1, -1)
    for index in range(0, len(low_face), 2):
        corner_a, corner_b = wide(ca_ref[index // 2]), wide(cb_ref[index // 2])
        for k in range(2):
            (yl, pl_), (yh, ph) = low_face[index + k], high_face[index + k]
            ca, cb = corner_a[8 * k : 8 * k + 8], corner_b[8 * k : 8 * k + 8]
            low = [jnp.where(odd_image, ca, cb)]
            high = [jnp.where(odd_image, cb, ca)]
            for c in range(depth_cells // 16):
                ya = wide(ya_ref[index + k, 16 * c : 16 * c + 16, :])
                yb = wide(yb_ref[index + k, 16 * c : 16 * c + 16, :])
                for half in range(2):
                    a, b = ya[8 * half : 8 * half + 8], yb[8 * half : 8 * half + 8]
                    low.append(jnp.where(odd_image, a, b))
                    high.append(jnp.where(odd_image, b, a))
            low = [decode(v, ph) for v in low]
            high = [decode(v, pl_) for v in high]
            put_streamed(sa_ref, ph, yh - width_cells + HALO, low[1:], low[0], rows)
            put_streamed(sa_ref, pl_, yl + width_cells + HALO, high[1:], high[0], rows)

    def stage(source, target, step, shift):
        reach = HALO - step

        def both(k, carry):
            step_row(source, target, HALO - reach + k, tiles + 1, shift)
            step_row(source, target, HALO + width_cells - step + k, tiles + 1, shift)
            return carry

        lax.fori_loop(0, HALO, both, 0, unroll=HALO)

    stage(sa_ref, sb_ref, 1, 0)
    stage(sb_ref, sa_ref, 2, 0)
    stage(sa_ref, sb_ref, 3, 4)

    def finish(k, carry):
        final_row(sb_ref, out_ref, HALO + k, HALO, tiles, width_cells)
        final_row(sb_ref, out_ref, HALO + width_cells - STEPS + k, HALO, tiles, width_cells)
        return carry

    lax.fori_loop(0, STEPS, finish, 0)
    keep_out = pltpu.make_async_copy(out_ref, out_hbm, out_sem)
    keep_out.start()

    def flows(k, carry):
        flow_row(sb_ref, flow_ref, HALO - 1 + k, tiles)
        flow_row(sb_ref, flow_ref, HALO + width_cells - STEPS + k, tiles)
        return carry

    lax.fori_loop(0, HALO, flows, 0)

    def spins(k, carry):
        spin_row(flow_ref, plain_ref, HALO + k, HALO, tiles, width_cells)
        spin_row(flow_ref, plain_ref, width_cells + k, HALO, tiles, width_cells)
        return carry

    lax.fori_loop(0, HALO, spins, 0)

    def rounded(x, carry):
        at = pl.ds(pl.multiple_of(x * 16, 16), 16)
        vort_ref[at, :] = plain_ref[at, :].astype(jnp.bfloat16)
        return carry

    lax.fori_loop(0, depth_cells * width_cells // 16, rounded, 0, unroll=4)
    keep_out.wait()


BUMP_WIDTH = 0.15
LEVEL_OFFSET = 0.05
STRETCH = float(np.sqrt(np.log2(np.e)) / BUMP_WIDTH)
CENTRE = 4.0
LOG2E = float(np.log2(np.e))


def bump_tables(transfer, ray_cells):
    b = STRETCH * transfer[:, 0] - CENTRE
    fade = jnp.exp2(-b * b)
    strength = transfer[:, 1:] * fade[:, None]
    strength = strength.at[:, 0].multiply(LOG2E / ray_cells)
    return jnp.concatenate([(2.0 * b)[:, None], strength], axis=1)


BLOCK = 4


def render_kernel(depth_cells, width_cells, functions, bumps, table_ref, plain_ref, image_ref, place_ref, fade_ref):
    def prepare(x, carry):
        at = pl.ds(pl.multiple_of(x * width_cells, width_cells), width_cells)
        value = plain_ref[at, :].astype(jnp.bfloat16).astype(jnp.float32)
        level = value / (value + LEVEL_OFFSET)
        place = STRETCH * level - CENTRE
        fade = jnp.exp2(-place * place)
        for order, to in ((0, x), (1, depth_cells - 1 - x)):
            place_ref[order, to] = place
            fade_ref[order, to] = fade
        return carry

    lax.fori_loop(0, depth_cells, prepare, 0)

    def one(m, carry):
        order = jnp.where(table_ref[m, 0, 5 * bumps] > 0.5, 1, 0)

        def cells(block, state):
            clear, red, green, blue = state
            at = pl.ds(block * BLOCK, BLOCK)
            place = place_ref[order, at]
            total = [None] * 4
            for k in range(bumps):
                bump = jnp.exp2(place * table_ref[m, 0, k])
                for c in range(4):
                    term = bump * table_ref[m, 0, (1 + c) * bumps + k]
                    total[c] = term if total[c] is None else total[c] + term
            fade = fade_ref[order, at]
            passing = jnp.exp2(-(total[0] * fade))
            for b in range(BLOCK):
                behind = clear * passing[b]
                weight = (clear - behind) * fade[b]
                clear = behind
                red = red + weight * total[1][b]
                green = green + weight * total[2][b]
                blue = blue + weight * total[3][b]
            return clear, red, green, blue

        zero = jnp.zeros((width_cells, 128), jnp.float32)
        clear, red, green, blue = lax.fori_loop(0, depth_cells // BLOCK, cells, (zero + 1.0, zero, zero, zero), unroll=2)
        image_ref[m, 0] = red
        image_ref[m, 1] = green
        image_ref[m, 2] = blue
        image_ref[m, 3] = clear
        return carry

    lax.fori_loop(0, functions, one, 0)


def composite_kernel(slabs, halves, order_ref, piece_ref, image_ref):
    backward = order_ref[0] > 0.5
    width_cells = piece_ref.shape[3]
    for side in range(halves):
        at = slice(side * width_cells, (side + 1) * width_cells)
        clear = jnp.ones(piece_ref.shape[3:], jnp.float32)
        color = [jnp.zeros_like(clear) for c in range(3)]
        for step in range(slabs):
            slab = jnp.where(backward, slabs - 1 - step, step)
            color = [color[c] + clear * piece_ref[slab, side, c] for c in range(3)]
            clear = clear * piece_ref[slab, side, 3]
        for c in range(3):
            image_ref[c, at, :] = color[c]
        image_ref[3, at, :] = 1.0 - clear


HBM = pl.BlockSpec(memory_space=pltpu.HBM)
VMEM = pl.BlockSpec(memory_space=pltpu.VMEM)
SMEM = pl.BlockSpec(memory_space=pltpu.SMEM)
GRANT = pltpu.CompilerParams(vmem_limit_bytes=14 * 1024 * 1024)


def cost(microseconds):
    return pl.CostEstimate(flops=0, bytes_accessed=int(microseconds * 3.69e6), transcendentals=0)


def in_hbm(value):
    return pltpu.with_memory_space_constraint(value, pltpu.HBM)


def in_vmem(value):
    return pltpu.with_memory_space_constraint(value, pltpu.VMEM)


def partner(index, count, phase):
    return index ^ 1 if phase == 0 else (((index + 1) ^ 1) - 1) % count


def swap(value, axis, count, phase):
    return lax.ppermute(value, axis, [(i, partner(i, count, phase)) for i in range(count)])


def on_device(populations, transfer, direction):
    _, depth_cells, width_cells, lanes = populations.shape
    depth_count, image_count = lax.axis_size("depth"), lax.axis_size("image")
    ray_cells = depth_cells * depth_count
    cells = depth_cells * width_cells
    f32, i16 = jnp.float32, jnp.int16
    d, i = lax.axis_index("depth"), lax.axis_index("image")
    parity = jnp.stack([d % 2, i % 2]).astype(jnp.int32)
    faces = len(face_list(0, 1))

    x_shape = jax.ShapeDtypeStruct((len(X_PAIRS), width_cells // 2, 16, lanes), i16)
    y_shape = jax.ShapeDtypeStruct((faces, depth_cells, lanes), i16)
    c_shape = jax.ShapeDtypeStruct((faces // 2, 16, lanes), i16)
    half = (depth_cells - 16, 16)
    field = pltpu.with_memory_space_constraint(populations.reshape(Q, cells, lanes), pltpu.HBM)
    edge, da, db = pl.pallas_call(
        functools.partial(edge_kernel, depth_cells, width_cells),
        out_shape=(pltpu.HBM((Q, width_cells, half[1], lanes), f32), x_shape, x_shape),
        in_specs=[SMEM, HBM],
        out_specs=(HBM, VMEM, VMEM),
        scratch_shapes=[
            pltpu.VMEM((Q, half[1] * width_cells, lanes), f32),
            pltpu.VMEM((Q, width_cells, half[1], lanes), f32),
            pltpu.SemaphoreType.DMA((2,)),
            pltpu.SemaphoreType.DMA((2,)),
        ],
        compiler_params=GRANT,
        cost_estimate=cost(6),
        name="edge",
    )(parity, field)
    middle, ia, ib = pl.pallas_call(
        functools.partial(middle_kernel, depth_cells, width_cells),
        out_shape=(pltpu.HBM((Q, width_cells, half[0], lanes), f32), y_shape, y_shape),
        in_specs=[SMEM, HBM, HBM],
        out_specs=(HBM, VMEM, VMEM),
        scratch_shapes=[
            pltpu.VMEM((Q, half[0] * width_cells, lanes), f32),
            pltpu.VMEM((Q, width_cells, half[0], lanes), f32),
            pltpu.VMEM((Q, 2 * HALO, half[1], lanes), f32),
            pltpu.SemaphoreType.DMA((depth_cells // 8,)),
            pltpu.SemaphoreType.DMA((depth_cells // 8 - 2,)),
        ],
        compiler_params=GRANT,
        cost_estimate=cost(6),
        name="middle",
    )(parity, field, in_hbm(edge))

    xa = swap(da, "depth", depth_count, 0)
    xb = swap(db, "depth", depth_count, 1)
    ya = swap(ia, "image", image_count, 0)
    yb = swap(ib, "image", image_count, 1)
    halo, ca, cb = pl.pallas_call(
        functools.partial(corner_kernel, width_cells),
        out_shape=(pltpu.HBM((Q, width_cells, 8, lanes), f32), c_shape, c_shape),
        in_specs=[SMEM, VMEM, VMEM],
        out_specs=(HBM, VMEM, VMEM),
        scratch_shapes=[pltpu.VMEM((Q, width_cells, 8, lanes), f32), pltpu.SemaphoreType.DMA],
        compiler_params=GRANT,
        cost_estimate=cost(2),
        name="corner",
    )(parity, xa, xb)
    sent_a, sent_b = ca, cb
    ca = swap(sent_a, "image", image_count, 0)
    cb = swap(sent_b, "image", image_count, 1)

    depth_rows = depth_cells + 8 + 2 * PAD
    width_rows = width_cells + 2 * HALO
    stages = (
        pltpu.VMEM((Q, width_rows, depth_rows, lanes), f32),
        pltpu.VMEM((Q, width_rows, depth_rows, lanes), f32),
        pltpu.VMEM((Q, cells, lanes), f32),
        pltpu.VMEM((3, width_rows, depth_rows, lanes), f32),
        pltpu.VMEM((cells, lanes), f32),
    )
    state = pl.pallas_call(
        functools.partial(inner_kernel, depth_cells, width_cells),
        out_shape=stages,
        in_specs=[HBM] * 3,
        out_specs=(VMEM,) * 5,
        scratch_shapes=[
            pltpu.VMEM((Q, width_cells, half[1], lanes), f32),
            pltpu.VMEM((Q, width_cells, half[0], lanes), f32),
            pltpu.VMEM((Q, width_cells, 8, lanes), f32),
            pltpu.SemaphoreType.DMA((4, 3)),
        ],
        compiler_params=GRANT,
        cost_estimate=cost(12),
        name="inner",
    )(in_hbm(edge), in_hbm(middle), in_hbm(halo))

    bumps = transfer.shape[2]
    row = jnp.concatenate([bump_tables(transfer, ray_cells).reshape(-1), direction.astype(f32)])
    row = jnp.pad(row, (0, lanes - row.shape[0]))
    row, _ = lax.optimization_barrier((row, halo))
    tables = lax.all_to_all(
        jnp.broadcast_to(row, (image_count, 8, lanes)), "image", 0, 0, tiled=True
    )
    final, vorticity, *_, plain = pl.pallas_call(
        functools.partial(outer_kernel, depth_cells, width_cells),
        out_shape=(
            jax.ShapeDtypeStruct((Q, cells, lanes), f32),
            jax.ShapeDtypeStruct((cells, lanes), jnp.bfloat16),
            *stages,
        ),
        in_specs=[SMEM] + [VMEM] * 9,
        out_specs=(HBM,) + (VMEM,) * 6,
        scratch_shapes=[pltpu.SemaphoreType.DMA],
        input_output_aliases={5 + k: 2 + k for k in range(5)},
        compiler_params=GRANT,
        cost_estimate=cost(12),
        name="outer",
    )(parity, ya, yb, ca, cb, *state)

    functions = image_count
    partial = pl.pallas_call(
        functools.partial(render_kernel, depth_cells, width_cells, functions, bumps),
        out_shape=jax.ShapeDtypeStruct((functions, 4, width_cells, lanes), f32),
        in_specs=[SMEM, VMEM],
        out_specs=VMEM,
        scratch_shapes=[
            pltpu.VMEM((2, depth_cells, width_cells, lanes), f32),
            pltpu.VMEM((2, depth_cells, width_cells, lanes), f32),
        ],
        compiler_params=GRANT,
        cost_estimate=cost(16),
        name="render",
    )(tables, in_vmem(plain))
    halves = image_count // depth_count
    groups = [
        [sd * image_count + halves * row + side for sd in range(depth_count) for side in range(halves)]
        for row in range(depth_count)
    ]
    slabs = lax.all_to_all(
        partial, ("depth", "image"), 0, 0, axis_index_groups=groups, tiled=True
    ).reshape(depth_count, halves, 4, width_cells, lanes)
    image = pl.pallas_call(
        functools.partial(composite_kernel, depth_count, halves),
        out_shape=jax.ShapeDtypeStruct((4, halves * width_cells, lanes), f32),
        in_specs=[SMEM, VMEM],
        out_specs=VMEM,
        cost_estimate=cost(1),
        name="composite",
    )(tables[halves * d + i % halves, 0, 5 * bumps][None], in_vmem(slabs))
    route = [
        (sd * image_count + si, (si // halves) * image_count + halves * sd + si % halves)
        for sd in range(depth_count)
        for si in range(image_count)
    ]
    images = lax.ppermute(image, ("depth", "image"), route)
    images = images[None]
    return (
        final.reshape(populations.shape),
        vorticity.reshape(depth_cells, width_cells, lanes),
        images,
    )


def solution(mesh):
    in_specs = (P(None, "depth", "image", None), P("image", None, None), P("image"))
    out_specs = (
        P(None, "depth", "image", None),
        P("depth", "image", None),
        P("image", None, "depth", None),
    )
    return jax.shard_map(
        on_device, mesh=mesh, in_specs=in_specs, out_specs=out_specs, check_vma=False
    )
```

```python
import functools

import jax
import jax.numpy as jnp
import numpy as np
from jax import lax
from jax.experimental import pallas as pl
from jax.experimental.pallas import tpu as pltpu
from jax.sharding import PartitionSpec as P

VEL = (
    (0, 0, 0),
    (1, 0, 0), (-1, 0, 0), (0, 1, 0), (0, -1, 0), (0, 0, 1), (0, 0, -1),
    (1, 1, 0), (-1, -1, 0), (1, -1, 0), (-1, 1, 0),
    (1, 0, 1), (-1, 0, -1), (1, 0, -1), (-1, 0, 1),
    (0, 1, 1), (0, -1, -1), (0, 1, -1), (0, -1, 1),
)
WEIGHT = (1.0 / 3.0,) + (1.0 / 18.0,) * 6 + (1.0 / 36.0,) * 12
OMEGA = 1.25
Q = len(VEL)
STEPS = 4
HALO = STEPS + 1
AXIS_PAIRS = ((1, 2), (3, 4), (5, 6))
DIAG_PAIRS = ((7, 8), (9, 10), (11, 12), (13, 14), (15, 16), (17, 18))
SCALE = 8192.0

FACE_PARTS = 2

X_PAIRS = tuple(
    (a, b, 5) for a, b in zip((1, 7, 9, 11, 13), (2, 8, 10, 12, 14))
) + ((3, 4, 4), (5, 6, 4), (15, 16, 4), (17, 18, 4), (0, None, 4))


def low_rows(p):
    return 4 + VEL[p][0]


def face_list(nearest, step):
    sent = []
    for layer in range(1, HALO + 1):
        y = nearest + step * (layer - 1)
        for p in range(Q):
            inward = VEL[p][1] * (-step)
            if layer <= 4 + inward:
                sent.append((y, p))
    return sent


def momentum(f):
    s = {}
    d = {}
    for a, b in AXIS_PAIRS + DIAG_PAIRS:
        s[a] = f[a] + f[b]
        d[a] = f[a] - f[b]
    density = ((s[1] + s[3]) + (s[5] + s[7])) + ((s[9] + s[11]) + (s[13] + s[15])) + (s[17] + f[0])
    jx = (d[1] + d[7]) + (d[9] + d[11]) + d[13]
    jy = (d[3] + d[7]) - (d[9] - d[15]) + d[17]
    jz = (d[5] + d[11]) - (d[13] - d[15]) - d[17]
    return density, (jx, jy, jz), s, d


def collide(f):
    density, j, s, d = momentum(f)
    inverse = 1.0 / density
    u = [c * inverse for c in j]
    speed = j[0] * u[0] + j[1] * u[1] + j[2] * u[2]
    common = density - 1.5 * speed
    out = [None] * Q
    out[0] = (OMEGA * WEIGHT[0]) * common - (OMEGA - 1.0) * f[0]
    rest = 0.5 * (OMEGA - 1.0)
    for pairs, w in ((AXIS_PAIRS, WEIGHT[1]), (DIAG_PAIRS, WEIGHT[7])):
        base = (OMEGA * w) * common
        jw = [(3.0 * OMEGA * w) * c for c in j]
        uw = [1.5 * c for c in u]
        for a, b in pairs:
            project_j = None
            project_u = None
            for axis in range(3):
                c = VEL[a][axis]
                if c == 0:
                    continue
                if project_j is None:
                    assert c == 1
                    project_j, project_u = jw[axis], uw[axis]
                elif c > 0:
                    project_j, project_u = project_j + jw[axis], project_u + uw[axis]
                else:
                    project_j, project_u = project_j - jw[axis], project_u - uw[axis]
            even = (base + project_j * project_u) - rest * s[a]
            odd = project_j - rest * d[a]
            out[a] = even + odd
            out[b] = even - odd
    return out


def code(value, p):
    return value * (SCALE / WEIGHT[p]) + (32768.5 - SCALE)


def decode(value, p):
    return value * (WEIGHT[p] / SCALE) + WEIGHT[p]


def row_index():
    return lax.broadcasted_iota(jnp.int32, (8, 128), 0)


def pack16(first, second):
    return jnp.concatenate([first, second], axis=0).astype(jnp.int32).astype(jnp.int16)


def pack_code(first, second):
    whole = jnp.concatenate([first, second], axis=0).astype(jnp.int32)
    return (whole - 32768).astype(jnp.int16)


def wide(value):
    return value.astype(jnp.int32).astype(jnp.float32)


def collide_chunk(f_ref, r_ref, from_row, to_row, width_cells):
    def at_y(y, carry):
        f = [f_ref[p, pl.ds(from_row + y, 8, stride=width_cells), :] for p in range(Q)]
        out = collide(f)
        for p in range(Q):
            value = pltpu.roll(out[p], low_rows(p), 0)
            cz = VEL[p][2]
            r_ref[p, y, to_row : to_row + 8, :] = value if cz == 0 else pltpu.roll(value, cz % 128, 1)
        return carry

    lax.fori_loop(0, width_cells, at_y, 0, unroll=8)


def keep_chunk(r_ref, r_hbm, k, sems):
    at = pl.ds(8 * k, 8)
    copy = pltpu.make_async_copy(r_ref.at[:, :, at], r_hbm.at[:, :, at], sems.at[k])
    copy.start()
    return copy


def edge_kernel(depth_cells, width_cells, parity_ref, f_hbm, r_hbm, da_ref, db_ref, f_ref, r_ref, in_sems, out_sems):
    rows = row_index()
    chunk = 8 * width_cells
    loads = []
    for k, j in enumerate((0, depth_cells // 8 - 1)):
        loads.append(
            pltpu.make_async_copy(
                f_hbm.at[:, pl.ds(j * chunk, chunk)], f_ref.at[:, pl.ds(k * chunk, chunk)], in_sems.at[k]
            )
        )
    for load in loads:
        load.start()
    keeps = []
    for k, load in enumerate(loads):
        load.wait()
        collide_chunk(f_ref, r_ref, k * chunk, 8 * k, width_cells)
        keeps.append(keep_chunk(r_ref, r_hbm, k, out_sems))

    odd_depth = jnp.full((8, 128), parity_ref[0], jnp.int32) == 1

    def face_x(t, carry):
        for number, (a, b, n) in enumerate(X_PAIRS):
            da, db = [], []
            for k in range(2):
                y = 2 * t + k
                low, high = (r_ref[a, y, first : first + 8, :] for first in (0, 8))
                if b is not None:
                    other_low, other_high = (
                        pltpu.roll(r_ref[b, y, first : first + 8, :], n, 0) for first in (0, 8)
                    )
                    low = jnp.where(rows >= n, low, other_low)
                    high = jnp.where(rows < n, high, other_high)
                low, high = code(low, a), code(high, a)
                da.append(jnp.where(odd_depth, low, high))
                db.append(jnp.where(odd_depth, high, low))
            da_ref[number, t] = pack_code(*da)
            db_ref[number, t] = pack_code(*db)
        return carry

    lax.fori_loop(0, width_cells // 2, face_x, 0, unroll=2)
    for keep in keeps:
        keep.wait()


def middle_kernel(
    depth_cells, width_cells, parity_ref, f_hbm, edge_hbm, r_hbm, ia_hbm, ib_hbm, f_ref, r_ref, edge_ref, ia_ref, ib_ref,
    in_sems, out_sems, face_sems
):
    chunk = 8 * width_cells
    tiles = depth_cells // 8
    loads = []
    for j in range(1, tiles - 1):
        loads.append(
            pltpu.make_async_copy(
                f_hbm.at[:, pl.ds(j * chunk, chunk)], f_ref.at[:, pl.ds((j - 1) * chunk, chunk)], in_sems.at[j]
            )
        )
    for side in range(2):
        first = side * (width_cells - HALO)
        loads.append(
            pltpu.make_async_copy(
                edge_hbm.at[:, pl.ds(first, HALO)], edge_ref.at[:, pl.ds(side * HALO, HALO)],
                in_sems.at[side * (tiles - 1)],
            )
        )
    for load in loads:
        load.start()
    keeps = []
    for j in range(tiles - 2):
        loads[j].wait()
        collide_chunk(f_ref, r_ref, j * chunk, 8 * j, width_cells)
        keeps.append(keep_chunk(r_ref, r_hbm, j, out_sems))
    for load in loads[tiles - 2 :]:
        load.wait()

    odd_image = jnp.full((8, 128), parity_ref[1], jnp.int32) == 1

    def piece(p, y, t):
        if t in (0, tiles - 1):
            row = y if y < HALO else y - (width_cells - 2 * HALO)
            first = 0 if t == 0 else 8
            return edge_ref[p, row, first : first + 8, :]
        return r_ref[p, y, 8 * t - 8 : 8 * t, :]

    low_face = face_list(0, 1)
    high_face = face_list(width_cells - 1, -1)
    part = len(low_face) // FACE_PARTS
    for index, ((yl, pl_), (yh, ph)) in enumerate(zip(low_face, high_face)):
        for c in range(tiles // 2):
            a, b = [], []
            for t in (2 * c, 2 * c + 1):
                low = code(piece(pl_, yl, t), pl_)
                high = code(piece(ph, yh, t), ph)
                a.append(jnp.where(odd_image, low, high))
                b.append(jnp.where(odd_image, high, low))
            ia_ref[index, 16 * c : 16 * c + 16, :] = pack_code(*a)
            ib_ref[index, 16 * c : 16 * c + 16, :] = pack_code(*b)
        if (index + 1) % part == 0:
            at = pl.ds(index + 1 - part, part)
            for k, (source, target) in enumerate(((ia_ref, ia_hbm), (ib_ref, ib_hbm))):
                keeps.append(pltpu.make_async_copy(source.at[at], target.at[at], face_sems.at[k, index // part]))
                keeps[-1].start()
    for keep in keeps:
        keep.wait()


def x_halo(low, high, n, second, rows):
    if second:
        low = pltpu.roll(low, 8 - n, 0)
        high = pltpu.roll(high, 8 - n, 0)
        n = 8 - n
    return jnp.where(rows < n, low, high)


X_PLACE = {}
for number_, (a_, b_, n_) in enumerate(X_PAIRS):
    X_PLACE[a_] = (number_, n_, False)
    if b_ is not None:
        X_PLACE[b_] = (number_, n_, True)


def corner_kernel(width_cells, parity_ref, xa_ref, xb_ref, h_hbm, ca_ref, cb_ref, h_ref, out_sem):
    rows = row_index()
    odd_depth = jnp.full((8, 128), parity_ref[0], jnp.int32) == 1
    odd_image = jnp.full((8, 128), parity_ref[1], jnp.int32) == 1

    def halo(t, carry):
        for number, (a, b, n) in enumerate(X_PAIRS):
            va = wide(xa_ref[number, t])
            vb = wide(xb_ref[number, t])
            for k in range(2):
                pa, pb = va[8 * k : 8 * k + 8], vb[8 * k : 8 * k + 8]
                low = jnp.where(odd_depth, pa, pb)
                high = jnp.where(odd_depth, pb, pa)
                h_ref[a, 2 * t + k] = x_halo(low, high, n, False, rows)
                if b is not None:
                    h_ref[b, 2 * t + k] = x_halo(low, high, n, True, rows)
        return carry

    lax.fori_loop(0, width_cells // 2, halo, 0)
    keep_h = pltpu.make_async_copy(h_ref, h_hbm, out_sem)
    keep_h.start()
    low_face = face_list(0, 1)
    high_face = face_list(width_cells - 1, -1)
    for index in range(0, len(low_face), 2):
        a, b = [], []
        for (yl, pl_), (yh, ph) in zip(low_face[index : index + 2], high_face[index : index + 2]):
            low, high = h_ref[pl_, yl], h_ref[ph, yh]
            a.append(jnp.where(odd_image, low, high))
            b.append(jnp.where(odd_image, high, low))
        ca_ref[index // 2] = pack16(*a)
        cb_ref[index // 2] = pack16(*b)
    keep_h.wait()


PAD = 8


def put_streamed(target, p, y, pieces, halo, rows):
    n = low_rows(p)
    before = halo
    for t in range(len(pieces) + 1):
        here = pieces[t] if t < len(pieces) else halo
        target[p, y, PAD + 8 * t : PAD + 8 * t + 8, :] = jnp.where(rows < n, before, here)
        before = here


def step_row(source, target, y, wide_tiles, shift):
    for t in range(wide_tiles):
        first = PAD + 8 * t
        out = collide([source[p, y - VEL[p][1], first : first + 8, :] for p in range(Q)])
        for p in range(Q):
            cx, _, cz = VEL[p]
            value = out[p] if cz == 0 else pltpu.roll(out[p], cz % 128, 1)
            row = first + shift + cx
            target[p, y, row : row + 8, :] = value


BASE = PAD + 8


def flow_row(source, flow_ref, y, tiles):
    for t in range(-1, tiles + 1):
        first = BASE + 8 * t
        density, j, _, _ = momentum([source[p, y - VEL[p][1], first : first + 8, :] for p in range(Q)])
        inverse = 1.0 / density
        for axis in range(3):
            flow_ref[axis, y, first : first + 8, :] = j[axis] * inverse


def final_row(source, out_ref, y, origin, tiles, width_cells):
    for t in range(tiles):
        first = BASE + 8 * t
        for p in range(Q):
            out_ref[p, pl.ds(8 * t * width_cells + y - origin, 8, stride=width_cells), :] = source[
                p, y - VEL[p][1], first : first + 8, :
            ]


def spin_row(flow_ref, out_ref, y, origin, tiles, width_cells):
    for t in range(tiles):
        first = BASE + 8 * t

        def dx(axis):
            return (flow_ref[axis, y, first + 1 : first + 9, :] - flow_ref[axis, y, first - 1 : first + 7, :]) * 0.5

        def dy(axis):
            return (flow_ref[axis, y + 1, first : first + 8, :] - flow_ref[axis, y - 1, first : first + 8, :]) * 0.5

        def dz(axis):
            value = flow_ref[axis, y, first : first + 8, :]
            return (pltpu.roll(value, 127, 1) - pltpu.roll(value, 1, 1)) * 0.5

        sx = dy(2) - dz(1)
        sy = dz(0) - dx(2)
        sz = dx(1) - dy(0)
        out_ref[pl.ds(8 * t * width_cells + y - origin, 8, stride=width_cells), :] = jnp.sqrt(
            sx * sx + sy * sy + sz * sz
        )


def inner_kernel(
    depth_cells, width_cells, e_hbm, r_hbm, h_hbm, sa_ref, sb_ref, final_ref, flow_ref, plain_ref, e_ref, r_ref, h_ref, sems
):
    tiles = depth_cells // 8
    rows = row_index()

    def own(y, carry):
        for p in range(Q):
            pieces = [r_ref[p, y, 8 * t : 8 * t + 8, :] for t in range(tiles - 2)]
            pieces = [e_ref[p, y, 0:8, :]] + pieces + [e_ref[p, y, 8:16, :]]
            put_streamed(sa_ref, p, y + HALO, pieces, decode(h_ref[p, y], p), rows)
        return carry

    parts = 4
    count = width_cells // parts
    loads = []
    for part in range(parts):
        at = pl.ds(part * count, count)
        loads.append(
            [
                pltpu.make_async_copy(e_hbm.at[:, at], e_ref.at[:, at], sems.at[part, 0]),
                pltpu.make_async_copy(r_hbm.at[:, at], r_ref.at[:, at], sems.at[part, 1]),
                pltpu.make_async_copy(h_hbm.at[:, at], h_ref.at[:, at], sems.at[part, 2]),
            ]
        )
        for load in loads[-1]:
            load.start()
    for part in range(parts):
        for load in loads[part]:
            load.wait()
        lax.fori_loop(part * count, (part + 1) * count, own, 0)

    def stage(source, target, step, shift):
        def pair(k, carry):
            step_row(source, target, HALO + step + 2 * k, tiles + 1, shift)
            step_row(source, target, HALO + step + 2 * k + 1, tiles + 1, shift)
            return carry

        lax.fori_loop(0, (width_cells - 2 * step) // 2, pair, 0, unroll=True)

    stage(sa_ref, sb_ref, 1, 0)
    stage(sb_ref, sa_ref, 2, 0)
    stage(sa_ref, sb_ref, 3, 4)

    def last(y, carry):
        flow_row(sb_ref, flow_ref, y, tiles)
        final_row(sb_ref, final_ref, y, HALO, tiles, width_cells)
        return carry

    lax.fori_loop(HALO + STEPS, HALO + width_cells - STEPS, last, 0, unroll=2)

    def spins(y, carry):
        spin_row(flow_ref, plain_ref, y, HALO, tiles, width_cells)
        return carry

    lax.fori_loop(2 * HALO, width_cells, spins, 0, unroll=2)


def outer_kernel(
    depth_cells, width_cells, parity_ref, ya_hbm, yb_hbm, ca_ref, cb_ref,
    sa_in, sb_in, final_in, flow_in, plain_in,
    out_hbm, vort_ref, sa_ref, sb_ref, out_ref, flow_ref, plain_ref, ya_ref, yb_ref, out_sem, face_sems,
):
    tiles = depth_cells // 8
    rows = row_index()
    odd_image = jnp.full((8, 128), parity_ref[1], jnp.int32) == 1

    low_face = face_list(0, 1)
    high_face = face_list(width_cells - 1, -1)
    part = len(low_face) // FACE_PARTS
    loads = []
    for n in range(FACE_PARTS):
        at = pl.ds(n * part, part)
        loads.append(
            [
                pltpu.make_async_copy(source.at[at], target.at[at], face_sems.at[k, n])
                for k, (source, target) in enumerate(((ya_hbm, ya_ref), (yb_hbm, yb_ref)))
            ]
        )
        for load in loads[-1]:
            load.start()
    for index in range(0, len(low_face), 2):
        if index % part == 0:
            for load in loads[index // part]:
                load.wait()
        corner_a, corner_b = wide(ca_ref[index // 2]), wide(cb_ref[index // 2])
        for k in range(2):
            (yl, pl_), (yh, ph) = low_face[index + k], high_face[index + k]
            ca, cb = corner_a[8 * k : 8 * k + 8], corner_b[8 * k : 8 * k + 8]
            low = [jnp.where(odd_image, ca, cb)]
            high = [jnp.where(odd_image, cb, ca)]
            for c in range(depth_cells // 16):
                ya = wide(ya_ref[index + k, 16 * c : 16 * c + 16, :])
                yb = wide(yb_ref[index + k, 16 * c : 16 * c + 16, :])
                for half in range(2):
                    a, b = ya[8 * half : 8 * half + 8], yb[8 * half : 8 * half + 8]
                    low.append(jnp.where(odd_image, a, b))
                    high.append(jnp.where(odd_image, b, a))
            low = [decode(v, ph) for v in low]
            high = [decode(v, pl_) for v in high]
            put_streamed(sa_ref, ph, yh - width_cells + HALO, low[1:], low[0], rows)
            put_streamed(sa_ref, pl_, yl + width_cells + HALO, high[1:], high[0], rows)

    def stage(source, target, step, shift):
        reach = HALO - step

        def both(k, carry):
            step_row(source, target, HALO - reach + k, tiles + 1, shift)
            step_row(source, target, HALO + width_cells - step + k, tiles + 1, shift)
            return carry

        lax.fori_loop(0, HALO, both, 0, unroll=HALO)

    stage(sa_ref, sb_ref, 1, 0)
    stage(sb_ref, sa_ref, 2, 0)
    stage(sa_ref, sb_ref, 3, 4)

    def finish(k, carry):
        final_row(sb_ref, out_ref, HALO + k, HALO, tiles, width_cells)
        final_row(sb_ref, out_ref, HALO + width_cells - STEPS + k, HALO, tiles, width_cells)
        return carry

    lax.fori_loop(0, STEPS, finish, 0)
    keep_out = pltpu.make_async_copy(out_ref, out_hbm, out_sem)
    keep_out.start()

    def flows(k, carry):
        flow_row(sb_ref, flow_ref, HALO - 1 + k, tiles)
        flow_row(sb_ref, flow_ref, HALO + width_cells - STEPS + k, tiles)
        return carry

    lax.fori_loop(0, HALO, flows, 0)

    def spins(k, carry):
        spin_row(flow_ref, plain_ref, HALO + k, HALO, tiles, width_cells)
        spin_row(flow_ref, plain_ref, width_cells + k, HALO, tiles, width_cells)
        return carry

    lax.fori_loop(0, HALO, spins, 0)

    def rounded(x, carry):
        at = pl.ds(pl.multiple_of(x * 16, 16), 16)
        vort_ref[at, :] = plain_ref[at, :].astype(jnp.bfloat16)
        return carry

    lax.fori_loop(0, depth_cells * width_cells // 16, rounded, 0, unroll=4)
    keep_out.wait()


BUMP_WIDTH = 0.15
LEVEL_OFFSET = 0.05
STRETCH = float(np.sqrt(np.log2(np.e)) / BUMP_WIDTH)
CENTRE = 4.0
LOG2E = float(np.log2(np.e))


def bump_tables(transfer, ray_cells):
    b = STRETCH * transfer[:, 0] - CENTRE
    fade = jnp.exp2(-b * b)
    strength = transfer[:, 1:] * fade[:, None]
    strength = strength.at[:, 0].multiply(LOG2E / ray_cells)
    return jnp.concatenate([(2.0 * b)[:, None], strength], axis=1)


BLOCK = 4


def render_kernel(depth_cells, width_cells, functions, bumps, table_ref, plain_ref, image_ref, place_ref, fade_ref):
    def prepare(x, carry):
        at = pl.ds(pl.multiple_of(x * width_cells, width_cells), width_cells)
        value = plain_ref[at, :].astype(jnp.bfloat16).astype(jnp.float32)
        level = value / (value + LEVEL_OFFSET)
        place = STRETCH * level - CENTRE
        fade = jnp.exp2(-place * place)
        for order, to in ((0, x), (1, depth_cells - 1 - x)):
            place_ref[order, to] = place
            fade_ref[order, to] = fade
        return carry

    lax.fori_loop(0, depth_cells, prepare, 0)

    def one(m, carry):
        order = jnp.where(table_ref[m, 0, 5 * bumps] > 0.5, 1, 0)

        def cells(block, state):
            clear, red, green, blue = state
            at = pl.ds(block * BLOCK, BLOCK)
            place = place_ref[order, at]
            total = [None] * 4
            for k in range(bumps):
                bump = jnp.exp2(place * table_ref[m, 0, k])
                for c in range(4):
                    term = bump * table_ref[m, 0, (1 + c) * bumps + k]
                    total[c] = term if total[c] is None else total[c] + term
            fade = fade_ref[order, at]
            passing = jnp.exp2(-(total[0] * fade))
            for b in range(BLOCK):
                behind = clear * passing[b]
                weight = (clear - behind) * fade[b]
                clear = behind
                red = red + weight * total[1][b]
                green = green + weight * total[2][b]
                blue = blue + weight * total[3][b]
            return clear, red, green, blue

        zero = jnp.zeros((width_cells, 128), jnp.float32)
        clear, red, green, blue = lax.fori_loop(0, depth_cells // BLOCK, cells, (zero + 1.0, zero, zero, zero), unroll=2)
        image_ref[m, 0] = red
        image_ref[m, 1] = green
        image_ref[m, 2] = blue
        image_ref[m, 3] = clear
        return carry

    lax.fori_loop(0, functions, one, 0)


def composite_kernel(slabs, halves, order_ref, piece_ref, image_ref):
    backward = order_ref[0] > 0.5
    width_cells = piece_ref.shape[3]
    for side in range(halves):
        at = slice(side * width_cells, (side + 1) * width_cells)
        clear = jnp.ones(piece_ref.shape[3:], jnp.float32)
        color = [jnp.zeros_like(clear) for c in range(3)]
        for step in range(slabs):
            slab = jnp.where(backward, slabs - 1 - step, step)
            color = [color[c] + clear * piece_ref[slab, side, c] for c in range(3)]
            clear = clear * piece_ref[slab, side, 3]
        for c in range(3):
            image_ref[c, at, :] = color[c]
        image_ref[3, at, :] = 1.0 - clear


HBM = pl.BlockSpec(memory_space=pltpu.HBM)
VMEM = pl.BlockSpec(memory_space=pltpu.VMEM)
SMEM = pl.BlockSpec(memory_space=pltpu.SMEM)
GRANT = pltpu.CompilerParams(vmem_limit_bytes=14 * 1024 * 1024)


def cost(microseconds):
    return pl.CostEstimate(flops=0, bytes_accessed=int(microseconds * 3.69e6), transcendentals=0)


def in_hbm(value):
    return pltpu.with_memory_space_constraint(value, pltpu.HBM)


def in_vmem(value):
    return pltpu.with_memory_space_constraint(value, pltpu.VMEM)


def partner(index, count, phase):
    return index ^ 1 if phase == 0 else (((index + 1) ^ 1) - 1) % count


def swap(value, axis, count, phase):
    return lax.ppermute(value, axis, [(i, partner(i, count, phase)) for i in range(count)])


def on_device(populations, transfer, direction):
    _, depth_cells, width_cells, lanes = populations.shape
    depth_count, image_count = lax.axis_size("depth"), lax.axis_size("image")
    ray_cells = depth_cells * depth_count
    cells = depth_cells * width_cells
    f32, i16 = jnp.float32, jnp.int16
    d, i = lax.axis_index("depth"), lax.axis_index("image")
    parity = jnp.stack([d % 2, i % 2]).astype(jnp.int32)
    faces = len(face_list(0, 1))

    x_shape = jax.ShapeDtypeStruct((len(X_PAIRS), width_cells // 2, 16, lanes), i16)
    y_shape = jax.ShapeDtypeStruct((faces, depth_cells, lanes), i16)
    c_shape = jax.ShapeDtypeStruct((faces // 2, 16, lanes), i16)
    half = (depth_cells - 16, 16)
    field = pltpu.with_memory_space_constraint(populations.reshape(Q, cells, lanes), pltpu.HBM)
    edge, da, db = pl.pallas_call(
        functools.partial(edge_kernel, depth_cells, width_cells),
        out_shape=(pltpu.HBM((Q, width_cells, half[1], lanes), f32), x_shape, x_shape),
        in_specs=[SMEM, HBM],
        out_specs=(HBM, VMEM, VMEM),
        scratch_shapes=[
            pltpu.VMEM((Q, half[1] * width_cells, lanes), f32),
            pltpu.VMEM((Q, width_cells, half[1], lanes), f32),
            pltpu.SemaphoreType.DMA((2,)),
            pltpu.SemaphoreType.DMA((2,)),
        ],
        compiler_params=GRANT,
        cost_estimate=cost(6),
        name="edge",
    )(parity, field)
    middle, ia, ib = pl.pallas_call(
        functools.partial(middle_kernel, depth_cells, width_cells),
        out_shape=(pltpu.HBM((Q, width_cells, half[0], lanes), f32), pltpu.HBM(y_shape.shape, i16), pltpu.HBM(y_shape.shape, i16)),
        in_specs=[SMEM, HBM, HBM],
        out_specs=(HBM,) * 3,
        scratch_shapes=[
            pltpu.VMEM((Q, half[0] * width_cells, lanes), f32),
            pltpu.VMEM((Q, width_cells, half[0], lanes), f32),
            pltpu.VMEM((Q, 2 * HALO, half[1], lanes), f32),
            pltpu.VMEM(y_shape.shape, i16),
            pltpu.VMEM(y_shape.shape, i16),
            pltpu.SemaphoreType.DMA((depth_cells // 8,)),
            pltpu.SemaphoreType.DMA((depth_cells // 8 - 2,)),
            pltpu.SemaphoreType.DMA((2, FACE_PARTS)),
        ],
        compiler_params=GRANT,
        cost_estimate=cost(6),
        name="middle",
    )(parity, field, in_hbm(edge))

    xa = swap(da, "depth", depth_count, 0)
    xb = swap(db, "depth", depth_count, 1)
    ya = swap(ia, "image", image_count, 0)
    yb = swap(ib, "image", image_count, 1)
    halo, ca, cb = pl.pallas_call(
        functools.partial(corner_kernel, width_cells),
        out_shape=(pltpu.HBM((Q, width_cells, 8, lanes), f32), c_shape, c_shape),
        in_specs=[SMEM, VMEM, VMEM],
        out_specs=(HBM, VMEM, VMEM),
        scratch_shapes=[pltpu.VMEM((Q, width_cells, 8, lanes), f32), pltpu.SemaphoreType.DMA],
        compiler_params=GRANT,
        cost_estimate=cost(2),
        name="corner",
    )(parity, xa, xb)
    sent_a, sent_b = ca, cb
    ca = swap(sent_a, "image", image_count, 0)
    cb = swap(sent_b, "image", image_count, 1)

    depth_rows = depth_cells + 8 + 2 * PAD
    width_rows = width_cells + 2 * HALO
    stages = (
        pltpu.VMEM((Q, width_rows, depth_rows, lanes), f32),
        pltpu.VMEM((Q, width_rows, depth_rows, lanes), f32),
        pltpu.VMEM((Q, cells, lanes), f32),
        pltpu.VMEM((3, width_rows, depth_rows, lanes), f32),
        pltpu.VMEM((cells, lanes), f32),
    )
    state = pl.pallas_call(
        functools.partial(inner_kernel, depth_cells, width_cells),
        out_shape=stages,
        in_specs=[HBM] * 3,
        out_specs=(VMEM,) * 5,
        scratch_shapes=[
            pltpu.VMEM((Q, width_cells, half[1], lanes), f32),
            pltpu.VMEM((Q, width_cells, half[0], lanes), f32),
            pltpu.VMEM((Q, width_cells, 8, lanes), f32),
            pltpu.SemaphoreType.DMA((4, 3)),
        ],
        compiler_params=GRANT,
        cost_estimate=cost(12),
        name="inner",
    )(in_hbm(edge), in_hbm(middle), in_hbm(halo))

    bumps = transfer.shape[2]
    row = jnp.concatenate([bump_tables(transfer, ray_cells).reshape(-1), direction.astype(f32)])
    row = jnp.pad(row, (0, lanes - row.shape[0]))
    row, _ = lax.optimization_barrier((row, halo))
    tables = lax.all_to_all(
        jnp.broadcast_to(row, (image_count, 8, lanes)), "image", 0, 0, tiled=True
    )
    final, vorticity, *_, plain = pl.pallas_call(
        functools.partial(outer_kernel, depth_cells, width_cells),
        out_shape=(
            jax.ShapeDtypeStruct((Q, cells, lanes), f32),
            jax.ShapeDtypeStruct((cells, lanes), jnp.bfloat16),
            *stages,
        ),
        in_specs=[SMEM, HBM, HBM] + [VMEM] * 7,
        out_specs=(HBM,) + (VMEM,) * 6,
        scratch_shapes=[
            pltpu.VMEM(y_shape.shape, i16),
            pltpu.VMEM(y_shape.shape, i16),
            pltpu.SemaphoreType.DMA,
            pltpu.SemaphoreType.DMA((2, FACE_PARTS)),
        ],
        input_output_aliases={5 + k: 2 + k for k in range(5)},
        compiler_params=GRANT,
        cost_estimate=cost(12),
        name="outer",
    )(parity, in_hbm(ya), in_hbm(yb), ca, cb, *state)

    functions = image_count
    partial = pl.pallas_call(
        functools.partial(render_kernel, depth_cells, width_cells, functions, bumps),
        out_shape=jax.ShapeDtypeStruct((functions, 4, width_cells, lanes), f32),
        in_specs=[SMEM, VMEM],
        out_specs=VMEM,
        scratch_shapes=[
            pltpu.VMEM((2, depth_cells, width_cells, lanes), f32),
            pltpu.VMEM((2, depth_cells, width_cells, lanes), f32),
        ],
        compiler_params=GRANT,
        cost_estimate=cost(16),
        name="render",
    )(tables, in_vmem(plain))
    halves = image_count // depth_count
    groups = [
        [sd * image_count + halves * row + side for sd in range(depth_count) for side in range(halves)]
        for row in range(depth_count)
    ]
    slabs = lax.all_to_all(
        partial, ("depth", "image"), 0, 0, axis_index_groups=groups, tiled=True
    ).reshape(depth_count, halves, 4, width_cells, lanes)
    image = pl.pallas_call(
        functools.partial(composite_kernel, depth_count, halves),
        out_shape=jax.ShapeDtypeStruct((4, halves * width_cells, lanes), f32),
        in_specs=[SMEM, VMEM],
        out_specs=VMEM,
        cost_estimate=cost(1),
        name="composite",
    )(tables[halves * d + i % halves, 0, 5 * bumps][None], in_vmem(slabs))
    route = [
        (sd * image_count + si, (si // halves) * image_count + halves * sd + si % halves)
        for sd in range(depth_count)
        for si in range(image_count)
    ]
    images = lax.ppermute(image, ("depth", "image"), route)
    images = images[None]
    return (
        final.reshape(populations.shape),
        vorticity.reshape(depth_cells, width_cells, lanes),
        images,
    )


def solution(mesh):
    in_specs = (P(None, "depth", "image", None), P("image", None, None), P("image"))
    out_specs = (
        P(None, "depth", "image", None),
        P("depth", "image", None),
        P("image", None, "depth", None),
    )
    return jax.shard_map(
        on_device, mesh=mesh, in_specs=in_specs, out_specs=out_specs, check_vma=False
    )
```
